32 devices in a mesh: gx: 4 (over x, core), gy: 4 (over z), gz: 2 (over y).
Axes of the slice: x: 2, y: 2, z: 4, core: 2. Of those that a mesh axis runs over, the one named last changes fastest.
Arguments:
- iterate: float32 [64, 128, 256], P('gx', 'gy', 'gz'), may hold values from -6 to 6
- residual: float32 [64, 128, 256], P('gx', 'gy', 'gz'), may hold values from -6 to 6
- direction: float32 [64, 128, 256], P('gx', 'gy', 'gz'), may hold values from -1.5 to 1.5
- permeability: float32 [64, 128, 256], P('gx', 'gy', 'gz'), may hold values from 1 to 16
- unfixed_node_mask: int32 [64, 128, 256], P('gx', 'gy', 'gz'), may hold values 0 or 1
- rz_prev: float32 [1], replicated, may hold values from 26214.4 to 104857.6
Outputs:
- updated_potential_values: float32 [64, 128, 256], P('gx', 'gy', 'gz')
- new_residual: float32 [64, 128, 256], P('gx', 'gy', 'gz')
- new_direction: float32 [64, 128, 256], P('gx', 'gy', 'gz')
The draws below stay inside these ranges and needn't reach their ends.
All inputs are finite; a program needn't handle non-finite values. No bound on the sum of `unfixed_node_mask` on one device may be relied on, other than what follows from the above.
Results may differ from the reference program's by a relative error of at most 0.0003.
Values sent between devices are 32-bit elements; how exact they have to be, the bound alone decides.
No kernel may reach another device: no remote copies, remote signals or barrier semaphores. Data moves between devices by JAX's collectives and lax.ppermute only.
A program may use at most 64 MiB of HBM per device.

```python
import math
import jax
import jax.numpy as jnp
from jax import lax

CX = 16
CY = 32
CZ = 128
NX = 64
NY = 128
NZ = 256
N_GX = 4
N_GY = 4
N_GZ = 2


def plant(array, own_key, least, high):
    index_at = [jax.random.randint(jax.random.fold_in(own_key, axis), (), 0, length) for axis, length in enumerate(array.shape)]
    main_axis = array.shape.index(max(array.shape))
    beside = index_at[:main_axis] + [(index_at[main_axis] + 1) % array.shape[main_axis]] + index_at[main_axis + 1:]
    return array.at[tuple(index_at)].set(least).at[tuple(beside)].set(high)


def steps_of(stream_key, shape, split, smallest, largest):
    def one(position, shards_of):
        heights = jax.random.uniform(jax.random.fold_in(jax.random.fold_in(stream_key, 6), position), (shards_of,), jnp.float32, smallest / len(split), largest / len(split))
        return jnp.repeat(jnp.exp(heights), shape[position] // shards_of).reshape((-1,) + (1,) * (len(shape) - position - 1))

    factor_of = one(*split[0])
    for cut in split[1:]:
        factor_of = factor_of * one(*cut)
    return factor_of


def centred(key, dims, scale, bound, cuts=(), dtype=jnp.bfloat16):
    entries = scale * jax.random.normal(key, dims, jnp.float32)
    if cuts:
        entries = entries * steps_of(key, dims, cuts, -0.22, 0.18)
    return jnp.clip(entries, -bound, bound).astype(dtype)


def setup_inputs(seed: int = 0) -> dict:
    seeds = jax.random.split(jax.random.key(seed), 7)
    iterate = centred(seeds[0], (NX, NY, NZ), 1.0, 6.0, ((0, 4), (1, 4), (2, 2)), jnp.float32)
    residual = centred(seeds[1], (NX, NY, NZ), 1.0, 6.0, ((0, 4), (1, 4), (2, 2)), jnp.float32)
    direction = centred(seeds[2], (NX, NY, NZ), 0.1, 1.5, ((0, 4), (1, 4), (2, 2)), jnp.float32)
    permeability = jnp.clip(jnp.exp(math.log(16.0) - 2.7725887 * jax.random.uniform(seeds[3], (NX, NY, NZ), jnp.float32) ** steps_of(seeds[3], (NX, NY, NZ), ((0, 4), (1, 4), (2, 2)), -0.2, 0.2)), 1.0, 16.0)
    unfixed_node_mask = plant((jax.random.randint(seeds[4], (NX, NY, NZ), 0, 8) < 7).astype(jnp.int32), jax.random.fold_in(seeds[4], 1), 0, 1)
    rz_prev = jnp.clip(jax.random.uniform(seeds[5], (1,), jnp.float32, 26214.4, 104857.6), 26214.4, 104857.6)
    return dict(iterate=iterate, residual=residual, direction=direction, permeability=permeability, unfixed_node_mask=unfixed_node_mask, rz_prev=rz_prev)


def tables(n):
    idx = jnp.arange(n).astype(jnp.float32) + 1.0
    basis = jnp.sqrt(2.0 / (n + 1)) * jnp.sin(jnp.pi * idx[:, None] * idx[None, :] / (n + 1))
    values = 2.0 - 2.0 * jnp.cos(jnp.pi * idx / (n + 1))
    return (basis, values)

def rim_masks(ex, ey, ez):

    def along(n):
        ids = jnp.arange(n)
        return ((ids == 0) | (ids == n - 1), (ids >= 2) & (ids <= n - 3))
    onx, inx = along(ex)
    ony, iny = along(ey)
    onz, inz = along(ez)
    onx, inx = (onx[:, None, None], inx[:, None, None])
    ony, iny = (ony[None, :, None], iny[None, :, None])
    onz, inz = (onz[None, None, :], inz[None, None, :])
    count = onx.astype(jnp.int32) + ony.astype(jnp.int32) + onz.astype(jnp.int32)
    outer = (count <= 1).astype(jnp.float32)
    kept = (count == 0) | onx & iny & inz | ony & inx & inz | onz & inx & iny
    return (outer, kept.astype(jnp.float32))

def fdm_solve(box, coef):
    high = lax.Precision.HIGHEST
    sx, lx = tables(box.shape[0])
    sy, ly = tables(box.shape[1])
    sz, lz = tables(box.shape[2])
    work = jnp.einsum('ia,ijk->ajk', sx, box, precision=high)
    work = jnp.einsum('jb,ajk->abk', sy, work, precision=high)
    work = jnp.einsum('kc,abk->abc', sz, work, precision=high)
    work = work / (coef * (lx[:, None, None] + ly[None, :, None] + lz[None, None, :]))
    work = jnp.einsum('ia,abc->ibc', sx, work, precision=high)
    work = jnp.einsum('jb,ibc->ijc', sy, work, precision=high)
    return jnp.einsum('kc,ijc->ijk', sz, work, precision=high)

def stencil(fpad, mpad):
    center = fpad[1:-1, 1:-1, 1:-1]
    mcent = mpad[1:-1, 1:-1, 1:-1]
    pairs = [(fpad[2:, 1:-1, 1:-1], mpad[2:, 1:-1, 1:-1]), (fpad[:-2, 1:-1, 1:-1], mpad[:-2, 1:-1, 1:-1]), (fpad[1:-1, 2:, 1:-1], mpad[1:-1, 2:, 1:-1]), (fpad[1:-1, :-2, 1:-1], mpad[1:-1, :-2, 1:-1]), (fpad[1:-1, 1:-1, 2:], mpad[1:-1, 1:-1, 2:]), (fpad[1:-1, 1:-1, :-2], mpad[1:-1, 1:-1, :-2])]
    total = jnp.zeros_like(center)
    for near_f, near_m in pairs:
        total = total + 0.5 * (mcent + near_m) * (center - near_f)
    return total

def reference(iterate, residual, direction, permeability, unfixed_node_mask, rz_prev):
    maskf = unfixed_node_mask.astype(jnp.float32)
    masked = maskf * residual
    rpad = jnp.pad(masked, 1)
    outer, kept = rim_masks(CX + 2, CY + 2, CZ + 2)

    def brick(flat):
        a = flat // (N_GY * N_GZ)
        b = flat // N_GZ % N_GY
        c = flat % N_GZ
        start = (a * CX, b * CY, c * CZ)
        box = lax.dynamic_slice(rpad, start, (CX + 2, CY + 2, CZ + 2)) * outer
        coef = jnp.mean(lax.dynamic_slice(permeability, start, (CX, CY, CZ)))
        return fdm_solve(box, coef) * kept
    subdomain_parts = lax.map(brick, jnp.arange(N_GX * N_GY * N_GZ).astype(jnp.int32))
    subdomain_parts = subdomain_parts.reshape(N_GX, N_GY, N_GZ, CX + 2, CY + 2, CZ + 2)
    owned = subdomain_parts[:, :, :, 1:-1, 1:-1, 1:-1]
    owned = owned.at[1:, :, :, 0, 1:-1, 1:-1].add(subdomain_parts[:-1, :, :, -1, 2:-2, 2:-2])
    owned = owned.at[:-1, :, :, -1, 1:-1, 1:-1].add(subdomain_parts[1:, :, :, 0, 2:-2, 2:-2])
    owned = owned.at[:, 1:, :, 1:-1, 0, 1:-1].add(subdomain_parts[:, :-1, :, 2:-2, -1, 2:-2])
    owned = owned.at[:, :-1, :, 1:-1, -1, 1:-1].add(subdomain_parts[:, 1:, :, 2:-2, 0, 2:-2])
    owned = owned.at[:, :, 1:, 1:-1, 1:-1, 0].add(subdomain_parts[:, :, :-1, 2:-2, 2:-2, -1])
    owned = owned.at[:, :, :-1, 1:-1, 1:-1, -1].add(subdomain_parts[:, :, 1:, 2:-2, 2:-2, 0])
    precond = owned.transpose(0, 3, 1, 4, 2, 5).reshape(NX, NY, NZ)
    rz = jnp.sum(masked * precond)
    beta = rz / rz_prev[0]
    new_direction = maskf * (precond + beta * direction)
    image = maskf * stencil(jnp.pad(new_direction, 1), jnp.pad(permeability, 1))
    alpha = rz / jnp.sum(new_direction * image)
    return (iterate + alpha * new_direction, residual - alpha * image, new_direction)
```

```python
import functools

import jax
import jax.numpy as jnp
import ml_dtypes
import numpy as np
from jax import lax
from jax.experimental import pallas as pl
from jax.experimental.pallas import tpu as pltpu
from jax.sharding import PartitionSpec as P

AXES = ("gx", "gy", "gz")
F32 = jnp.float32
BF16 = jnp.bfloat16
HIGHEST = lax.Precision.HIGHEST
VMEM = pl.BlockSpec(memory_space=pltpu.VMEM)
SMEM = pl.BlockSpec(memory_space=pltpu.SMEM)
LANES = 256


def swaps(axis, turn):
    count = lax.axis_size(axis)
    return [(i, (i + 1 if (i + turn) % 2 == 0 else i - 1) % count) for i in range(count)]


def swap(block, axis, turn):
    return lax.ppermute(block, axis, swaps(axis, turn))


def place(axis):
    index = lax.axis_index(axis)
    return index % 2 == 0, index > 0, index < lax.axis_size(axis) - 1


def sides(turn0, turn1, where):
    even, below, above = where
    low = jnp.where(below, jnp.where(even, turn1, turn0), 0.0)
    high = jnp.where(above, jnp.where(even, turn0, turn1), 0.0)
    return low, high


def halves(value):
    high = value.astype(BF16)
    return high, (value - high.astype(F32)).astype(BF16)


def dot(a, b):
    return lax.dot_general(a, b, (((1,), (0,)), ((), ())), preferred_element_type=F32)


def iota(shape, dim):
    return lax.broadcasted_iota(jnp.int32, shape, dim)


def basis(n):
    idx = np.arange(n, dtype=np.float64) + 1.0
    values = 2.0 - 2.0 * np.cos(np.pi * idx / (n + 1))
    return np.sqrt(2.0 / (n + 1)) * np.sin(np.pi * idx[:, None] * idx[None, :] / (n + 1)), values


def np_halves(table):
    high = table.astype(np.float32).astype(ml_dtypes.bfloat16)
    return high, (table - high.astype(np.float64)).astype(np.float32).astype(ml_dtypes.bfloat16)


@functools.cache
def solve_tables(size_x, size_y, size_z):
    qx, lx = basis(size_x + 2)
    qy, ly = basis(size_y + 2)
    qz, lz = basis(size_z + 2)
    nx, ny, nz = size_x + 2, size_y + 2, size_z + 2
    own = [(i, j) for i in range(1, nx - 1) for j in range(1, ny - 1)]
    rim = [(i, j) for i in (0, nx - 1) for j in range(1, ny - 1)]
    rim += [(i, j) for j in (0, ny - 1) for i in range(1, nx - 1)]
    place_x, place_y = (np.array(v) for v in zip(*(own + rim)))
    modes = nx * ny
    padded = -(-modes // 16) * 16
    cross = np.zeros((padded, len(place_x)))
    cross[:modes] = (qx[:, None, place_x] * qy[None, :, place_y]).reshape(modes, -1)
    inverse = np.zeros((padded, LANES))
    inverse[:modes, :nz] = 1.0 / ((lx[:, None] + ly[None, :]).reshape(modes, 1) + lz[None, :])
    forward = np.zeros((size_z, LANES))
    forward[:, :nz] = qz[1:-1]
    ends = np.zeros((8, LANES))
    ends[0, :nz] = qz[0]
    ends[1, :nz] = qz[-1]
    fh, fl = np_halves(forward)
    ch, cl = np_halves(cross)
    return dict(
        fwd_hh=np.concatenate([fh, fh]),
        fwd_l=fl,
        ends=ends.astype(np.float32),
        cross_h=ch,
        cross_l=cl,
        inverse=inverse.astype(np.float32),
        back_h=np.ascontiguousarray(ch.T),
        back_l=np.ascontiguousarray(cl.T),
        out_hl=np.concatenate([np.ascontiguousarray(fh.T), np.ascontiguousarray(fl.T)], axis=1),
    )


def lane_rows(fields, lane):
    depth = fields[0].shape[1]
    total = None
    for f, field in enumerate(fields):
        pick = jnp.where((iota((8, depth), 0) == f) & (iota((8, depth), 1) == lane), 1.0, 0.0)
        rows = lax.dot_general(pick, field, (((1,), (1,)), ((), ())), precision=HIGHEST, preferred_element_type=F32)
        total = rows if total is None else total + rows
    return total


def lane_ends(row, even, depth):
    pick = jnp.where((iota((8, depth), 0) == 0) & (iota((8, depth), 1) == jnp.where(even, depth - 1, 0)), 1.0, 0.0)
    rows = jnp.broadcast_to(row, (8, row.shape[1]))
    return lax.dot_general(rows, pick, (((0,), (0,)), ((), ())), precision=HIGHEST, preferred_element_type=F32)


def pack_kernel(res, direction, mu, msk, sx0, sx1, sy0, sy1, sz):
    size_x, size_y, size_z = res.shape
    even_x, even_y, even_z = (place(axis)[0] for axis in AXES)
    mask = msk[...].astype(F32)
    fields = (mask * res[...], mask, mask * direction[...], mu[...])
    for f, field in enumerate(fields):
        low, high = field[0], field[size_x - 1]
        sx0[f] = jnp.where(even_x, high, low)
        sx1[f] = jnp.where(even_x, low, high)
        low, high = field[:, 0], field[:, size_y - 1]
        sy0[f] = jnp.where(even_y, high, low)
        sy1[f] = jnp.where(even_y, low, high)
    flat = [field.reshape(size_x * size_y, size_z) for field in fields]
    sz[...] = lane_rows(flat, jnp.where(even_z, size_z - 1, 0))


def solve_kernel(
    res, mu, msk, rx0, rx1, ry0, ry1, rz,
    fwd_hh, fwd_l, ends, cross_h, cross_l, inverse, back_h, back_l, out_hl,
    own, tx0, tx1, ty0, ty1, tz,
):
    size_x, size_y, size_z = res.shape
    rows = size_x * size_y
    where_x, where_y, where_z = (place(axis) for axis in AXES)
    even_z = where_z[0]
    mask = msk[...].astype(F32).reshape(rows, size_z)
    masked = mask * res[...].reshape(rows, size_z)
    x_low, x_high = sides(rx0[...], rx1[...], where_x)
    y_low, y_high = sides(ry0[...], ry1[...], where_y)
    box = jnp.concatenate([masked, x_low[0], x_high[0], y_low[0], y_high[0]], axis=0)
    box_h, box_l = halves(box)
    work = dot(jnp.concatenate([box_h, box_l], axis=1), fwd_hh[...]) + dot(box_h, fwd_l[...])
    face = jnp.broadcast_to(rz[0:1], (8, rows))
    face = jnp.where(iota((8, rows), 0) == jnp.where(even_z, 1, 0), face, 0.0)
    face = lax.dot_general(face, ends[...], (((0,), (0,)), ((), ())), precision=HIGHEST, preferred_element_type=F32)
    work = jnp.concatenate([work[:rows] + face, work[rows:]], axis=0)
    work_h, work_l = halves(work)
    work = dot(cross_h[...], work_h) + dot(cross_l[...], work_h) + dot(cross_h[...], work_l)
    coef = jnp.sum(mu[...]) * (1.0 / (rows * size_z))
    work = work * (inverse[...] / coef)
    work_h, work_l = halves(work)
    work = dot(back_h[...], work_h) + dot(back_l[...], work_h) + dot(back_h[...], work_l)
    work_h, work_l = halves(work)
    both = dot(work_h, out_hl[...])
    local = both[:, :size_z] + both[:, size_z:] + dot(work_l, out_hl[:, :size_z])
    face = lax.dot_general(ends[...], work[:rows], (((1,), (1,)), ((), ())), precision=HIGHEST, preferred_element_type=F32)

    def inner(shape, dim):
        at = iota(shape, dim)
        return (at >= 1) & (at <= shape[dim] - 2)

    own_flat = mask * local[:rows]
    own_box = own_flat.reshape(size_x, size_y, size_z)
    own[...] = own_box
    at = rows
    shape = (size_y, size_z)
    kept = inner(shape, 0) & inner(shape, 1)
    g_low = jnp.where(kept, local[at : at + size_y] * x_low[1], 0.0)
    g_high = jnp.where(kept, local[at + size_y : at + 2 * size_y] * x_high[1], 0.0)
    at += 2 * size_y
    even = where_x[0]
    low, high = own_box[0], own_box[size_x - 1]
    tx0[0] = jnp.where(even, high, low)
    tx0[1] = jnp.where(even, g_high, g_low)
    tx1[0] = jnp.where(even, low, high)
    tx1[1] = jnp.where(even, g_low, g_high)
    shape = (size_x, size_z)
    kept = inner(shape, 0) & inner(shape, 1)
    g_low = jnp.where(kept, local[at : at + size_x] * y_low[1], 0.0)
    g_high = jnp.where(kept, local[at + size_x : at + 2 * size_x] * y_high[1], 0.0)
    even = where_y[0]
    low, high = own_box[:, 0], own_box[:, size_y - 1]
    ty0[0] = jnp.where(even, high, low)
    ty0[1] = jnp.where(even, g_high, g_low)
    ty1[0] = jnp.where(even, low, high)
    ty1[1] = jnp.where(even, g_low, g_high)
    mine = lane_rows([own_flat], jnp.where(even_z, size_z - 1, 0))
    ids = iota((1, rows), 1)
    x_at, y_at = ids // size_y, ids % size_y
    kept = (x_at >= 1) & (x_at <= size_x - 2) & (y_at >= 1) & (y_at <= size_y - 2)
    ghost = jnp.where(kept, jnp.where(even_z, face[1:2], face[0:1]) * rz[1:2], 0.0)
    tz[...] = jnp.where(iota((8, rows), 0) == 1, jnp.broadcast_to(ghost, (8, rows)), mine)


def flux(value, x_sides, y_sides, face, mu, mu_x, mu_y, mu_face, even_z):
    size_x = y_sides[0].shape[0]
    rows, size_z = value.shape
    size_y = rows // size_x
    box = (size_x, size_y, size_z)
    value_b, mu_b = value.reshape(box), mu.reshape(box)
    ext = jnp.concatenate([x_sides[0][None], value_b, x_sides[1][None]], axis=0)
    mu_ext = jnp.concatenate([mu_x[0][None], mu_b, mu_x[1][None]], axis=0)
    flow = 0.5 * (mu_ext[1:] + mu_ext[:-1]) * (ext[1:] - ext[:-1])
    total = (flow[:-1] - flow[1:]).reshape(rows, size_z)

    def wide(side):
        return jnp.broadcast_to(side[:, None, :], box).reshape(rows, size_z)

    at = iota((rows, size_z), 0) % size_y
    next_v = jnp.where(at == size_y - 1, wide(y_sides[1]), pltpu.roll(value, rows - 1, 0))
    next_m = jnp.where(at == size_y - 1, wide(mu_y[1]), pltpu.roll(mu, rows - 1, 0))
    flow = 0.5 * (mu + next_m) * (next_v - value)
    first = 0.5 * (mu + wide(mu_y[0])) * (value - wide(y_sides[0]))
    total = total + jnp.where(at == 0, first, pltpu.roll(flow, 1, 0)) - flow
    at = iota((rows, size_z), 1)
    next_v = jnp.where(at == size_z - 1, face, pltpu.roll(value, size_z - 1, 1))
    next_m = jnp.where(at == size_z - 1, mu_face, pltpu.roll(mu, size_z - 1, 1))
    flow = 0.5 * (mu + next_m) * (next_v - value)
    first = 0.5 * (mu + mu_face) * (value - face)
    return total + jnp.where(at == 0, first, pltpu.roll(flow, 1, 1)) - flow


def image_kernel(
    res, direction, mu, msk, own, rx0, rx1, ry0, ry1, rz, tx0, tx1, ty0, ty1, tz, qx0, qx1, qy0, qy1, qz,
    z_out, az_out, ad_out, sums,
):
    size_x, size_y, size_z = res.shape
    rows = size_x * size_y
    box = (size_x, size_y, size_z)
    where_x, where_y, where_z = (place(axis) for axis in AXES)
    even_z = where_z[0]
    x_near = sides(rx0[...], rx1[...], where_x)
    y_near = sides(ry0[...], ry1[...], where_y)
    x_sent = sides(tx0[...], tx1[...], where_x)
    y_sent = sides(ty0[...], ty1[...], where_y)
    x_got = sides(qx0[...], qx1[...], where_x)
    y_got = sides(qy0[...], qy1[...], where_y)
    mask = msk[...].astype(F32).reshape(rows, size_z)
    mu_own = mu[...].reshape(rows, size_z)
    mu_x, mu_y = [v[3] for v in x_near], [v[3] for v in y_near]
    mu_face = lane_ends(rz[3:4], even_z, size_z)
    d = mask * direction[...].reshape(rows, size_z)
    d_face = lane_ends(rz[2:3], even_z, size_z)
    ad = mask * flux(d, [v[2] for v in x_near], [v[2] for v in y_near], d_face, mu_own, mu_x, mu_y, mu_face, even_z)
    own_box = own[...]
    z = jnp.concatenate(
        [own_box[:1] + x_got[0][1][None], own_box[1:-1], own_box[-1:] + x_got[1][1][None]], axis=0
    )
    at = iota(box, 1)
    z = z + jnp.where(at == 0, y_got[0][1][:, None, :], 0.0) + jnp.where(at == size_y - 1, y_got[1][1][:, None, :], 0.0)
    z = z.reshape(rows, size_z) + lane_ends(qz[1:2], even_z, size_z)
    z_face = lane_ends(qz[0:1] + tz[1:2], even_z, size_z)
    az = mask * flux(
        z,
        [x_got[s][0] + x_sent[s][1] for s in (0, 1)],
        [y_got[s][0] + y_sent[s][1] for s in (0, 1)],
        z_face, mu_own, mu_x, mu_y, mu_face, even_z,
    )
    z_out[...] = z.reshape(box)
    az_out[...] = az.reshape(box)
    ad_out[...] = ad.reshape(box)
    parts = (
        jnp.sum(res[...].reshape(rows, size_z) * z),
        jnp.sum(z * az),
        jnp.sum(z * ad + d * az),
        jnp.sum(d * ad),
    )
    at = iota(sums.shape, 2)
    line = jnp.zeros(sums.shape, F32)
    for k, part in enumerate(parts):
        line = jnp.where(at == k, part, line)
    sums[...] = line


def update_kernel(rz_prev, sums, iterate, res, direction, msk, z, az, ad, new_iterate, new_res, new_direction):
    line = jnp.sum(sums[...], axis=0)
    rz, zaz, zad, dad = (line[:, k : k + 1] for k in range(4))
    beta = rz / rz_prev[0]
    alpha = rz / (zaz + beta * (zad + beta * dad))
    alpha, beta = (v.reshape(1, 1, 1) for v in (alpha, beta))
    p = z[...] + beta * (msk[...].astype(F32) * direction[...])
    new_direction[...] = p
    new_iterate[...] = iterate[...] + alpha * p
    new_res[...] = res[...] - alpha * (az[...] + beta * ad[...])


def call(kernel, args, outs, specs=None):
    return pl.pallas_call(
        kernel,
        out_shape=[jax.ShapeDtypeStruct(shape, F32) for shape in outs],
        in_specs=specs or [VMEM] * len(args),
        out_specs=[VMEM] * len(outs),
        compiler_params=pltpu.CompilerParams(vmem_limit_bytes=48 * 1024 * 1024),
    )(*args)


def exchange(sx0, sx1, sy0, sy1, sz):
    return (
        swap(sx0, "gx", 0),
        swap(sx1, "gx", 1),
        swap(sy0, "gy", 0),
        swap(sy1, "gy", 1),
        swap(sz, "gz", 0),
    )


def shards(iterate, residual, direction, permeability, unfixed_node_mask, rz_prev):
    size_x, size_y, size_z = residual.shape
    box = residual.shape
    rows = size_x * size_y
    devices = lax.axis_size(AXES)

    def faces(count):
        return [(count, size_y, size_z)] * 2 + [(count, size_x, size_z)] * 2 + [(8, rows)]

    table = solve_tables(size_x, size_y, size_z)
    with jax.named_scope("pack"):
        sent = call(pack_kernel, (residual, direction, permeability, unfixed_node_mask), faces(4))
    with jax.named_scope("faces_in"):
        near = exchange(*sent)
    with jax.named_scope("solve"):
        own, *made = call(
            solve_kernel,
            (residual, permeability, unfixed_node_mask, *near, *map(jnp.asarray, table.values())),
            [box] + faces(2),
        )
    with jax.named_scope("faces_out"):
        got = exchange(*made)
    with jax.named_scope("image"):
        z, az, ad, sums = call(
            image_kernel,
            (residual, direction, permeability, unfixed_node_mask, own, *near, *made, *got),
            [box, box, box, (devices, 1, 128)],
        )
    with jax.named_scope("sums"):
        sums = lax.all_to_all(sums, AXES, 0, 0, tiled=True)
    with jax.named_scope("update"):
        args = (rz_prev, sums, iterate, residual, direction, unfixed_node_mask, z, az, ad)
        return tuple(call(update_kernel, args, [box] * 3, [SMEM] + [VMEM] * 8))


def solution(mesh):
    in_specs = (P(*AXES),) * 5 + (P(),)
    out_specs = (P(*AXES),) * 3
    return jax.shard_map(shards, mesh=mesh, in_specs=in_specs, out_specs=out_specs, check_vma=False)
```

```python
import functools

import jax
import jax.numpy as jnp
import ml_dtypes
import numpy as np
from jax import lax
from jax.experimental import pallas as pl
from jax.experimental.pallas import tpu as pltpu
from jax.sharding import PartitionSpec as P

AXES = ("gx", "gy", "gz")
F32 = jnp.float32
BF16 = jnp.bfloat16
HIGHEST = lax.Precision.HIGHEST
VMEM = pl.BlockSpec(memory_space=pltpu.VMEM)
SMEM = pl.BlockSpec(memory_space=pltpu.SMEM)
HBM = pl.BlockSpec(memory_space=pltpu.HBM)
LANES = 256
GROUP = 6


def swaps(axis, turn):
    counts = [lax.axis_size(name) for name in AXES]
    dim = AXES.index(axis)
    pairs = []
    for source in np.ndindex(*counts):
        target = list(source)
        step = 1 if (source[dim] + turn) % 2 == 0 else -1
        if axis == "gy" and not 0 <= source[dim] + step < counts[dim]:
            target[0] ^= 1
        else:
            target[dim] = (source[dim] + step) % counts[dim]
        pairs.append(tuple(int(np.ravel_multi_index(where, counts)) for where in (source, target)))
    return pairs


def swap(block, axis, turn):
    return lax.ppermute(block, AXES, swaps(axis, turn))


def place(axis):
    index = lax.axis_index(axis)
    return index % 2 == 0, index > 0, index < lax.axis_size(axis) - 1


def sides(turn0, turn1, where):
    even, below, above = where
    low = jnp.where(below, jnp.where(even, turn1, turn0), 0.0)
    high = jnp.where(above, jnp.where(even, turn0, turn1), 0.0)
    return low, high


def halves(value):
    high = value.astype(BF16)
    return high, (value - high.astype(F32)).astype(BF16)


def dot(a, b):
    return lax.dot_general(a, b, (((1,), (0,)), ((), ())), preferred_element_type=F32)


def dot_rows(a, b):
    return lax.dot_general(a, b, (((0,), (0,)), ((), ())), preferred_element_type=F32)


def dot_lanes(a, b):
    return lax.dot_general(a, b, (((1,), (1,)), ((), ())), preferred_element_type=F32)


def iota(shape, dim):
    return lax.broadcasted_iota(jnp.int32, shape, dim)


def basis(n):
    idx = np.arange(n, dtype=np.float64) + 1.0
    values = 2.0 - 2.0 * np.cos(np.pi * idx / (n + 1))
    return np.sqrt(2.0 / (n + 1)) * np.sin(np.pi * idx[:, None] * idx[None, :] / (n + 1)), values


def np_halves(table):
    high = table.astype(np.float32).astype(ml_dtypes.bfloat16)
    return high, (table - high.astype(np.float64)).astype(np.float32).astype(ml_dtypes.bfloat16)


@functools.cache
def solve_tables(size_x, size_y, size_z):
    nx, ny, nz = size_x + 2, size_y + 2, size_z + 2
    qy, ly = basis(ny)
    qz, lz = basis(nz)
    pad = -(-ny // 8) * 8
    forward = np.zeros((size_z, LANES))
    forward[:, :nz] = qz[1:-1]
    ends = np.zeros((2, LANES))
    ends[:, :nz] = qz[[0, -1]]
    fh, fl = np_halves(forward)
    eh, el = np_halves(ends)
    face = np.zeros((16, LANES), ml_dtypes.bfloat16)
    face[0:2], face[2:4], face[4:6] = eh, eh, el
    out_ends = np.zeros((32, LANES), ml_dtypes.bfloat16)
    out_ends[0:2], out_ends[16:18] = eh, el
    into = np.zeros((GROUP * pad, LANES))
    for s in range(GROUP):
        into[s * pad : s * pad + ny, s * size_y : (s + 1) * size_y] = qy[1:-1].T
    rim = np.zeros((pad, 2 * LANES))
    rim[:ny, :LANES], rim[:ny, LANES:] = qy[0][:, None], qy[-1][:, None]
    groups = nx // GROUP
    back = np.zeros((groups, GROUP * size_y + 2 * size_x, LANES))
    for g in range(groups):
        for s in range(GROUP):
            modes = slice(s * pad, s * pad + ny)
            back[g, s * size_y : (s + 1) * size_y, modes] = qy[1:-1]
            i = g * GROUP + s - 1
            if 0 <= i < size_x:
                back[g, GROUP * size_y + i, modes] = qy[0]
                back[g, GROUP * size_y + size_x + i, modes] = qy[-1]
    middle = np.full((pad, LANES), 2.0)
    middle[:ny, :nz] += ly[:, None] + lz[None, :]
    factors = np.zeros((nx, pad, LANES))
    previous = 0.0
    for i in range(nx):
        previous = 1.0 / (middle - previous)
        factors[i] = previous
    ih, il = np_halves(into)
    bh, bl = np_halves(back.reshape(-1, LANES))
    return dict(
        fwd=np.concatenate([fh, fh, fl]),
        face=face,
        into=np.concatenate([ih, il]),
        back=np.concatenate([bh, bl]),
        factors=factors.astype(np.float32).reshape(nx * pad, LANES),
        rim=rim.astype(np.float32),
        out=np.concatenate([np.ascontiguousarray(fh.T), np.ascontiguousarray(fl.T)], axis=1),
        out_ends=out_ends,
    )


def lane_rows(fields, lane):
    depth = fields[0].shape[1]
    total = None
    for f, field in enumerate(fields):
        at = iota((16, 2 * depth), 1)
        pick = jnp.where((iota((16, 2 * depth), 0) == f) & ((at == lane) | (at == lane + depth)), 1.0, 0.0).astype(BF16)
        rows = dot_lanes(pick, jnp.concatenate(halves(field), axis=1))
        total = rows if total is None else total + rows
    return total[:8]


def lane_ends(lines, even, depth):
    count = len(lines)
    pieces = []
    for line in lines:
        pieces += halves(line)
    size = lines[0].shape[1]
    stack = jnp.zeros((16, size), F32)
    for k, piece in enumerate(pieces):
        stack = jnp.where(iota((16, size), 0) == k, piece.astype(F32), stack)
    shape = (16, count * depth)
    lane = jnp.where(even, depth - 1, 0) + iota(shape, 0) // 2 * depth
    pick = jnp.where((iota(shape, 0) < 2 * count) & (iota(shape, 1) == lane), 1.0, 0.0).astype(BF16)
    wide = dot_rows(stack.astype(BF16), pick)
    return [wide[:, k * depth : (k + 1) * depth] for k in range(count)]


def pack_kernel(
    res_hbm, direction_hbm, mu_hbm, msk_hbm,
    sx0, sx1, sy0, sy1, sz, masked_out, mask_out, d_out, mu_out,
    res, direction, msk, arrived,
):
    size_x, size_y, size_z = res.shape
    even_x, even_y, even_z = (place(axis)[0] for axis in AXES)
    copies = [
        pltpu.make_async_copy(source, target, arrived.at[k])
        for k, (source, target) in enumerate(
            ((msk_hbm, msk), (res_hbm, res), (direction_hbm, direction), (mu_hbm, mu_out))
        )
    ]
    for copy in copies:
        copy.start()
    for copy in copies:
        copy.wait()
    mask = msk[...].astype(F32)
    fields = (mask * res[...], mask, mask * direction[...], mu_out[...])
    masked_out[...], mask_out[...], d_out[...] = fields[:3]
    for f, field in enumerate(fields):
        low, high = field[0], field[size_x - 1]
        sx0[f] = jnp.where(even_x, high, low)
        sx1[f] = jnp.where(even_x, low, high)
        low, high = field[:, 0], field[:, size_y - 1]
        sy0[f] = jnp.where(even_y, high, low)
        sy1[f] = jnp.where(even_y, low, high)
    flat = [field.reshape(size_x * size_y, size_z) for field in fields]
    sz[...] = lane_rows(flat, jnp.where(even_z, size_z - 1, 0))


def along_z(rows, fwd, size_z):
    high, low = halves(rows)
    return dot(jnp.concatenate([high, low], axis=1), fwd[: 2 * size_z]) + dot(high, fwd[2 * size_z :])


def own_kernel(masked, *refs):
    count = (len(refs) - 2) // 2
    tables, loaded, (work, arrived) = refs[:count], refs[count : 2 * count], refs[2 * count :]
    copies = [pltpu.make_async_copy(s, t, arrived.at[k]) for k, (s, t) in enumerate(zip(tables, loaded))]
    for copy in copies:
        copy.start()
    for copy in copies:
        copy.wait()
    size_x, size_y, size_z = masked.shape
    work[...] = along_z(masked[...].reshape(size_x * size_y, size_z), loaded[0], size_z)


def solve_kernel(
    work, mask, mu, rx0, rx1, ry0, ry1, rz, fwd, face_table, into, back, factors, rim, out, out_ends,
    own, tx0, tx1, ty0, ty1, tz,
):
    size_x, size_y, size_z = mask.shape
    rows = size_x * size_y
    pad = rim.shape[0]
    nx = size_x + 2
    where_x, where_y, where_z = (place(axis) for axis in AXES)
    even_z = where_z[0]
    x_low, x_high = sides(rx0[0:2], rx1[0:2], where_x)
    y_low, y_high = sides(ry0[0:2], ry1[0:2], where_y)
    edge = along_z(jnp.concatenate([x_low[0], x_high[0], y_low[0], y_high[0]], axis=0), fwd, size_z)
    line = rz[0:1]
    line_h, line_l = halves(line)
    at = iota((16, rows), 0)
    mine = (at < 6) & (at % 2 == jnp.where(even_z, 1, 0))
    line = jnp.where(mine, jnp.where(at // 2 == 1, line_l.astype(F32), line_h.astype(F32)), 0.0)
    face = dot_rows(line.astype(BF16), face_table[...])
    box = jnp.concatenate([edge[:size_y], work[...] + face, edge[size_y : 2 * size_y]], axis=0)
    box_h, box_l = halves(box)
    modes = []
    into_h, into_l = into[: GROUP * pad, : GROUP * size_y], into[GROUP * pad :, : GROUP * size_y]
    for g in range(nx // GROUP):
        part = slice(g * GROUP * size_y, (g + 1) * GROUP * size_y)
        modes.append(dot(into_h, box_h[part]) + dot(into_l, box_h[part]) + dot(into_h, box_l[part]))
    modes = jnp.concatenate(modes, axis=0)
    rim_low, rim_high = rim[:, :LANES], rim[:, LANES:]
    solved = []
    for i in range(nx):
        value = modes[i * pad : (i + 1) * pad]
        if 0 < i < nx - 1:
            at = 2 * size_y + i - 1
            value = value + rim_low * edge[at : at + 1] + rim_high * edge[at + size_x : at + size_x + 1]
        if i:
            value = value + solved[-1]
        solved.append(value * factors[i * pad : (i + 1) * pad])
    for i in reversed(range(nx - 1)):
        solved[i] = solved[i] + factors[i * pad : (i + 1) * pad] * solved[i + 1]
    solved = jnp.concatenate(solved, axis=0)
    high, low = halves(solved)
    group_rows = GROUP * size_y + 2 * size_x
    half = back.shape[0] // 2
    local, y_faces = [], None
    for g in range(nx // GROUP):
        part = slice(g * GROUP * pad, (g + 1) * GROUP * pad)
        table_h = back[g * group_rows : (g + 1) * group_rows, : GROUP * pad]
        table_l = back[half + g * group_rows : half + (g + 1) * group_rows, : GROUP * pad]
        value = dot(table_h, high[part]) + dot(table_l, high[part]) + dot(table_h, low[part])
        local.append(value[: GROUP * size_y])
        rest = value[GROUP * size_y :]
        y_faces = rest if y_faces is None else y_faces + rest
    local = jnp.concatenate(local + [y_faces], axis=0)
    scale = (rows * size_z) / jnp.sum(mu[...])
    local = local * scale
    high, low = halves(local)
    both = dot(high, out[...])
    local = both[:, :size_z] + both[:, size_z:] + dot(low, out[:, :size_z])
    own_h, own_l = high[size_y : size_y + rows], low[size_y : size_y + rows]
    face = dot_lanes(out_ends[0:16], own_h) + dot_lanes(out_ends[0:16], own_l) + dot_lanes(out_ends[16:32], own_h)

    def inner(shape, dim):
        at = iota(shape, dim)
        return (at >= 1) & (at <= shape[dim] - 2)

    own_flat = mask[...].reshape(rows, size_z) * local[size_y : size_y + rows]
    own_box = own_flat.reshape(size_x, size_y, size_z)
    own[...] = own_box
    shape = (size_y, size_z)
    kept = inner(shape, 0) & inner(shape, 1)
    g_low = jnp.where(kept, local[:size_y] * x_low[1], 0.0)
    g_high = jnp.where(kept, local[size_y + rows : 2 * size_y + rows] * x_high[1], 0.0)
    even = where_x[0]
    low, high = own_box[0], own_box[size_x - 1]
    tx0[0] = jnp.where(even, high, low)
    tx0[1] = jnp.where(even, g_high, g_low)
    tx1[0] = jnp.where(even, low, high)
    tx1[1] = jnp.where(even, g_low, g_high)
    shape = (size_x, size_z)
    kept = inner(shape, 0) & inner(shape, 1)
    at = 2 * size_y + rows
    g_low = jnp.where(kept, local[at : at + size_x] * y_low[1], 0.0)
    g_high = jnp.where(kept, local[at + size_x : at + 2 * size_x] * y_high[1], 0.0)
    even = where_y[0]
    low, high = own_box[:, 0], own_box[:, size_y - 1]
    ty0[0] = jnp.where(even, high, low)
    ty0[1] = jnp.where(even, g_high, g_low)
    ty1[0] = jnp.where(even, low, high)
    ty1[1] = jnp.where(even, g_low, g_high)
    mine = lane_rows([own_flat], jnp.where(even_z, size_z - 1, 0))
    ids = iota((1, rows), 1)
    x_at, y_at = ids // size_y, ids % size_y
    kept = (x_at >= 1) & (x_at <= size_x - 2) & (y_at >= 1) & (y_at <= size_y - 2)
    ghost = jnp.where(kept, jnp.where(even_z, face[1:2], face[0:1]) * rz[1:2], 0.0)
    tz[...] = jnp.where(iota((8, rows), 0) == 1, jnp.broadcast_to(ghost, (8, rows)), mine)


def beside(value, y_sides, face, box):
    size_x, size_y, size_z = box
    rows = size_x * size_y

    def wide(side):
        return jnp.broadcast_to(side[:, None, :], box).reshape(rows, size_z)

    at = iota((rows, size_z), 0) % size_y
    next_y = jnp.where(at == size_y - 1, wide(y_sides[1]), pltpu.roll(value, rows - 1, 0))
    at = iota((rows, size_z), 1)
    next_z = jnp.where(at == size_z - 1, face, pltpu.roll(value, size_z - 1, 1))
    return next_y, next_z, wide(y_sides[0])


def flux(value, x_sides, y_sides, face, wx, wy, wy0, wz, wz0, box):
    size_x, size_y, size_z = box
    rows = size_x * size_y
    ext = jnp.concatenate([x_sides[0][None], value.reshape(box), x_sides[1][None]], axis=0)
    flow = wx * (ext[1:] - ext[:-1])
    total = (flow[:-1] - flow[1:]).reshape(rows, size_z)
    next_y, next_z, before_y = beside(value, y_sides, face, box)
    flow = wy * (next_y - value)
    at = iota((rows, size_z), 0) % size_y
    first = wy0 * (value - before_y)
    total = total + jnp.where(at == 0, first, pltpu.roll(flow, 1, 0)) - flow
    flow = wz * (next_z - value)
    first = wz0 * (value - face)
    at = iota((rows, size_z), 1)
    return total + jnp.where(at == 0, first, pltpu.roll(flow, 1, 1)) - flow


def links_kernel(
    mask, d, mu, rx0, rx1, ry0, ry1, rz,
    ad_out, wx_out, wy_out, wy0_out, wz_out, wz0_out,
):
    box = mask.shape
    size_x, size_y, size_z = box
    rows = size_x * size_y
    where_x, where_y, where_z = (place(axis) for axis in AXES)
    x_near = sides(rx0[2:4], rx1[2:4], where_x)
    y_near = sides(ry0[2:4], ry1[2:4], where_y)
    d_face, mu_face = lane_ends([rz[2:3], rz[3:4]], where_z[0], size_z)
    mu_own = mu[...].reshape(rows, size_z)
    ext = jnp.concatenate([x_near[0][1][None], mu[...], x_near[1][1][None]], axis=0)
    wx = 0.5 * (ext[1:] + ext[:-1])
    next_y, next_z, before_y = beside(mu_own, [v[1] for v in y_near], mu_face, box)
    wy, wy0 = 0.5 * (mu_own + next_y), 0.5 * (mu_own + before_y)
    wz, wz0 = 0.5 * (mu_own + next_z), 0.5 * (mu_own + mu_face)
    links = (wx, wy, wy0, wz, wz0)
    wx_out[...], wy_out[...], wy0_out[...], wz_out[...], wz0_out[...] = links
    value = d[...].reshape(rows, size_z)
    ad = flux(value, [v[0] for v in x_near], [v[0] for v in y_near], d_face, *links, box)
    ad_out[...] = mask[...].reshape(rows, size_z) * ad


def image_kernel(
    masked, mask, d, own, tx0, tx1, ty0, ty1, tz, qx0, qx1, qy0, qy1, qz, ad_in, wx, wy, wy0, wz, wz0,
    z_out, az_out, sums,
):
    box = mask.shape
    size_x, size_y, size_z = box
    rows = size_x * size_y
    where_x, where_y, where_z = (place(axis) for axis in AXES)
    x_sent = sides(tx0[1:2], tx1[1:2], where_x)
    y_sent = sides(ty0[1:2], ty1[1:2], where_y)
    x_got = sides(qx0[...], qx1[...], where_x)
    y_got = sides(qy0[...], qy1[...], where_y)
    z_face, z_more = lane_ends([qz[0:1] + tz[1:2], qz[1:2]], where_z[0], size_z)
    own_box = own[...]
    z = jnp.concatenate(
        [own_box[:1] + x_got[0][1][None], own_box[1:-1], own_box[-1:] + x_got[1][1][None]], axis=0
    )
    at = iota(box, 1)
    z = z + jnp.where(at == 0, y_got[0][1][:, None, :], 0.0) + jnp.where(at == size_y - 1, y_got[1][1][:, None, :], 0.0)
    z = z.reshape(rows, size_z) + z_more
    z = z * mask[...].reshape(rows, size_z)
    x_sides = [x_got[s][0] + x_sent[s][0] for s in (0, 1)]
    y_sides = [y_got[s][0] + y_sent[s][0] for s in (0, 1)]
    az = flux(z, x_sides, y_sides, z_face, wx[...], wy[...], wy0[...], wz[...], wz0[...], box)
    az = mask[...].reshape(rows, size_z) * az
    z_out[...] = z
    az_out[...] = az
    ad, value = ad_in[...], d[...].reshape(rows, size_z)
    parts = (
        jnp.sum(masked[...].reshape(rows, size_z) * z),
        jnp.sum(z * az),
        jnp.sum(z * ad + value * az),
        jnp.sum(value * ad),
    )
    at = iota(sums.shape, 2)
    line = jnp.zeros(sums.shape, F32)
    for k, part in enumerate(parts):
        line = jnp.where(at == k, part, line)
    sums[...] = line


def update_kernel(rz_prev, sums, iterate, res, d, z, az, ad, new_iterate, new_res, new_direction):
    line = jnp.sum(sums[...], axis=0)
    rz, zaz, zad, dad = (line[:, k : k + 1] for k in range(4))
    beta = rz / rz_prev[0]
    alpha = rz / (zaz + beta * (zad + beta * dad))
    alpha3, beta3 = (v.reshape(1, 1, 1) for v in (alpha, beta))
    box = d.shape
    p = z[...].reshape(box) + beta3 * d[...]
    new_direction[...] = p
    new_iterate[...] = iterate[...] + alpha3 * p
    new_res[...] = res[...] - alpha3 * (az[...] + beta * ad[...]).reshape(box)


def call(kernel, args, outs, specs=None, scratch=(), flops=0):
    outs = [out if isinstance(out, jax.ShapeDtypeStruct) else jax.ShapeDtypeStruct(out, F32) for out in outs]
    return pl.pallas_call(
        kernel,
        out_shape=outs,
        in_specs=specs or [VMEM] * len(args),
        out_specs=[VMEM] * len(outs),
        scratch_shapes=list(scratch),
        cost_estimate=pl.CostEstimate(flops=flops, bytes_accessed=1 << 20, transcendentals=0),
        compiler_params=pltpu.CompilerParams(vmem_limit_bytes=32 * 1024 * 1024),
    )(*args)


def exchange(sx0, sx1, sy0, sy1, sz):
    return (
        swap(sx0, "gx", 0),
        swap(sx1, "gx", 1),
        swap(sy0, "gy", 0),
        swap(sy1, "gy", 1),
        swap(sz, "gz", 0),
    )


def shards(iterate, residual, direction, permeability, unfixed_node_mask, rz_prev):
    size_x, size_y, size_z = residual.shape
    box = residual.shape
    rows = size_x * size_y
    flat = (rows, size_z)
    devices = lax.axis_size(AXES)

    def faces(count):
        return [(count, size_y, size_z)] * 2 + [(count, size_x, size_z)] * 2 + [(8, rows)]

    tables = list(solve_tables(size_x, size_y, size_z).values())
    with jax.named_scope("pack"):
        *sent, masked, mask, d, mu = call(
            pack_kernel,
            (residual, direction, permeability, unfixed_node_mask),
            faces(4) + [box] * 4,
            [HBM] * 4,
            [pltpu.VMEM(box, F32), pltpu.VMEM(box, F32), pltpu.VMEM(box, jnp.int32), pltpu.SemaphoreType.DMA((4,))],
        )
    with jax.named_scope("faces_in"):
        near = exchange(*sent)
    with jax.named_scope("own_part"):
        *tables, work = call(
            own_kernel,
            (masked, *map(jnp.asarray, tables)),
            [jax.ShapeDtypeStruct(t.shape, t.dtype) for t in tables] + [(rows, LANES)],
            [VMEM] + [HBM] * len(tables),
            [pltpu.SemaphoreType.DMA((len(tables),))],
        )
    with jax.named_scope("solve"):
        own, *made = call(solve_kernel, (work, mask, mu, *near, *tables), [box] + faces(2))
    with jax.named_scope("faces_out"):
        got = exchange(*made)
    with jax.named_scope("links"):
        ad, *links = call(
            links_kernel, (mask, d, mu, *near), [flat, (size_x + 1, size_y, size_z), flat, flat, flat, flat]
        )
    with jax.named_scope("image"):
        z, az, sums = call(
            image_kernel, (masked, mask, d, own, *made, *got, ad, *links), [flat, flat, (devices, 1, 128)]
        )
    with jax.named_scope("sums"):
        sums = lax.all_to_all(sums, AXES, 0, 0, tiled=True)
    with jax.named_scope("update"):
        args = (rz_prev, sums, iterate, residual, d, z, az, ad)
        return tuple(call(update_kernel, args, [box] * 3, [SMEM] + [VMEM] * 7))


def solution(mesh):
    in_specs = (P(*AXES),) * 5 + (P(),)
    out_specs = (P(*AXES),) * 3
    return jax.shard_map(shards, mesh=mesh, in_specs=in_specs, out_specs=out_specs, check_vma=False)
```

```python
import functools

import jax
import jax.numpy as jnp
import ml_dtypes
import numpy as np
from jax import lax
from jax.experimental import pallas as pl
from jax.experimental.pallas import tpu as pltpu
from jax.sharding import PartitionSpec as P

AXES = ("gx", "gy", "gz")
F32 = jnp.float32
BF16 = jnp.bfloat16
HIGHEST = lax.Precision.HIGHEST
VMEM = pl.BlockSpec(memory_space=pltpu.VMEM)
SMEM = pl.BlockSpec(memory_space=pltpu.SMEM)
LANES = 256
GROUP = 6


def swaps(axis, turn):
    counts = [lax.axis_size(name) for name in AXES]
    dim = AXES.index(axis)
    pairs = []
    for source in np.ndindex(*counts):
        target = list(source)
        step = 1 if (source[dim] + turn) % 2 == 0 else -1
        if axis == "gy" and not 0 <= source[dim] + step < counts[dim]:
            target[0] ^= 1
        else:
            target[dim] = (source[dim] + step) % counts[dim]
        pairs.append(tuple(int(np.ravel_multi_index(where, counts)) for where in (source, target)))
    return pairs


def swap(block, axis, turn):
    return lax.ppermute(block, AXES, swaps(axis, turn))


def place(axis):
    index = lax.axis_index(axis)
    return index % 2 == 0, index > 0, index < lax.axis_size(axis) - 1


def sides(turn0, turn1, where):
    even, below, above = where
    low = jnp.where(below, jnp.where(even, turn1, turn0), 0.0)
    high = jnp.where(above, jnp.where(even, turn0, turn1), 0.0)
    return low, high


def halves(value):
    high = value.astype(BF16)
    return high, (value - high.astype(F32)).astype(BF16)


def dot(a, b):
    return lax.dot_general(a, b, (((1,), (0,)), ((), ())), preferred_element_type=F32)


def dot_rows(a, b):
    return lax.dot_general(a, b, (((0,), (0,)), ((), ())), preferred_element_type=F32)


def dot_lanes(a, b):
    return lax.dot_general(a, b, (((1,), (1,)), ((), ())), preferred_element_type=F32)


def iota(shape, dim):
    return lax.broadcasted_iota(jnp.int32, shape, dim)


def basis(n):
    idx = np.arange(n, dtype=np.float64) + 1.0
    values = 2.0 - 2.0 * np.cos(np.pi * idx / (n + 1))
    return np.sqrt(2.0 / (n + 1)) * np.sin(np.pi * idx[:, None] * idx[None, :] / (n + 1)), values


def np_halves(table):
    high = table.astype(np.float32).astype(ml_dtypes.bfloat16)
    return high, (table - high.astype(np.float64)).astype(np.float32).astype(ml_dtypes.bfloat16)


@functools.cache
def solve_tables(size_x, size_y, size_z):
    nx, ny, nz = size_x + 2, size_y + 2, size_z + 2
    qy, ly = basis(ny)
    qz, lz = basis(nz)
    pad = -(-ny // 8) * 8
    forward = np.zeros((size_z, LANES))
    forward[:, :nz] = qz[1:-1]
    ends = np.zeros((2, LANES))
    ends[:, :nz] = qz[[0, -1]]
    fh, fl = np_halves(forward)
    eh, el = np_halves(ends)
    face = np.zeros((16, LANES), ml_dtypes.bfloat16)
    face[0:2], face[2:4], face[4:6] = eh, eh, el
    out_ends = np.zeros((32, LANES), ml_dtypes.bfloat16)
    out_ends[0:2], out_ends[16:18] = eh, el
    into = np.zeros((GROUP * pad, LANES))
    for s in range(GROUP):
        into[s * pad : s * pad + ny, s * size_y : (s + 1) * size_y] = qy[1:-1].T
    rim = np.zeros((pad, LANES // 2))
    rim[:ny, 0], rim[:ny, 1] = qy[0], qy[-1]
    groups = nx // GROUP
    back = np.zeros((GROUP * size_y, LANES))
    faces = np.zeros((groups, 2, size_x, LANES))
    for s in range(GROUP):
        modes = slice(s * pad, s * pad + ny)
        back[s * size_y : (s + 1) * size_y, modes] = qy[1:-1]
        for g in range(groups):
            i = g * GROUP + s - 1
            if 0 <= i < size_x:
                faces[g, 0, i, modes] = qy[0]
                faces[g, 1, i, modes] = qy[-1]
    middle = np.full((pad, LANES), 2.0)
    middle[:ny, :nz] += ly[:, None] + lz[None, :]
    middle[ny:], middle[:, nz:] = 4.0, 4.0
    ih, il = np_halves(into)
    bh, bl = np_halves(back)
    gh, gl = np_halves(faces.reshape(-1, LANES))
    return dict(
        fwd=np.concatenate([fh, fl]),
        middle=middle.astype(np.float32),
        face=face,
        into=np.concatenate([ih, il]),
        back=np.concatenate([bh, bl]),
        back_faces=np.concatenate([gh, gl]),
        rim=rim.astype(np.float32),
        out=np.concatenate([np.ascontiguousarray(fh.T), np.ascontiguousarray(fl.T)], axis=1),
        out_ends=out_ends,
    )


def lane_rows(fields, lane):
    depth = fields[0].shape[1]
    total = None
    for f, field in enumerate(fields):
        at = iota((16, 2 * depth), 1)
        pick = jnp.where((iota((16, 2 * depth), 0) == f) & ((at == lane) | (at == lane + depth)), 1.0, 0.0).astype(BF16)
        rows = dot_lanes(pick, jnp.concatenate(halves(field), axis=1))
        total = rows if total is None else total + rows
    return total[:8]


def lane_ends(lines, even, depth):
    count = len(lines)
    pieces = []
    for line in lines:
        pieces += halves(line)
    size = lines[0].shape[1]
    stack = jnp.zeros((16, size), F32)
    for k, piece in enumerate(pieces):
        stack = jnp.where(iota((16, size), 0) == k, piece.astype(F32), stack)
    shape = (16, count * depth)
    lane = jnp.where(even, depth - 1, 0) + iota(shape, 0) // 2 * depth
    pick = jnp.where((iota(shape, 0) < 2 * count) & (iota(shape, 1) == lane), 1.0, 0.0).astype(BF16)
    wide = dot_rows(stack.astype(BF16), pick)
    return [wide[:, k * depth : (k + 1) * depth] for k in range(count)]


def pack_kernel(masked, msk, direction, mu, sx0, sx1, sy0, sy1, sz, mask_out, d):
    size_x, size_y, size_z = masked.shape
    even_x, even_y, even_z = (place(axis)[0] for axis in AXES)
    mask = msk[...].astype(F32)
    fields = (masked[...], mask, mask * direction[...], mu[...])
    mask_out[...], d[...] = fields[1], fields[2]
    for f, field in enumerate(fields):
        low, high = field[0], field[size_x - 1]
        sx0[f] = jnp.where(even_x, high, low)
        sx1[f] = jnp.where(even_x, low, high)
        low, high = field[:, 0], field[:, size_y - 1]
        sy0[f] = jnp.where(even_y, high, low)
        sy1[f] = jnp.where(even_y, low, high)
    flat = [field.reshape(size_x * size_y, size_z) for field in fields]
    sz[...] = lane_rows(flat, jnp.where(even_z, size_z - 1, 0))


def along_z(rows, fwd, size_z):
    high, low = halves(rows)
    table = fwd[:size_z]
    return dot(jnp.concatenate([high, low], axis=1), jnp.concatenate([table, table], axis=0)) + dot(high, fwd[size_z:])


def own_kernel(masked, mu, fwd, middle, work, factors, scale):
    size_x, size_y, size_z = masked.shape
    work[...] = along_z(masked[...].reshape(size_x * size_y, size_z), fwd, size_z)
    pad = middle.shape[0]
    along = middle[...]
    previous = 1.0 / along
    factors[0:pad] = previous
    for i in range(1, size_x + 2):
        previous = 1.0 / (along - previous)
        factors[i * pad : (i + 1) * pad] = previous
    scale[...] = jnp.full((8, size_z), (size_x * size_y * size_z) / jnp.sum(mu[...]))


def solve_kernel(
    work, factors, scale, mask, rx0, rx1, ry0, ry1, rz, fwd, face_table, into, back, back_faces, rim, out, out_ends,
    own, tx0, tx1, ty0, ty1, tz,
):
    size_x, size_y, size_z = mask.shape
    rows = size_x * size_y
    pad = rim.shape[0]
    nx = size_x + 2
    where_x, where_y, where_z = (place(axis) for axis in AXES)
    even_z = where_z[0]
    x_low, x_high = sides(rx0[0:2], rx1[0:2], where_x)
    y_low, y_high = sides(ry0[0:2], ry1[0:2], where_y)
    edge = along_z(jnp.concatenate([x_low[0], x_high[0], y_low[0], y_high[0]], axis=0), fwd, size_z)
    line = rz[0:1]
    line_h, line_l = halves(line)
    at = iota((16, rows), 0)
    mine = (at < 6) & (at % 2 == jnp.where(even_z, 1, 0))
    line = jnp.where(mine, jnp.where(at // 2 == 1, line_l.astype(F32), line_h.astype(F32)), 0.0)
    face = dot_rows(line.astype(BF16), face_table[...])
    box = jnp.concatenate([edge[:size_y], work[...] + face, edge[size_y : 2 * size_y]], axis=0)
    box_h, box_l = halves(box)
    modes = []
    into_h, into_l = into[: GROUP * pad, : GROUP * size_y], into[GROUP * pad :, : GROUP * size_y]
    for g in range(nx // GROUP):
        part = slice(g * GROUP * size_y, (g + 1) * GROUP * size_y)
        modes.append(dot(into_h, box_h[part]) + dot(into_l, box_h[part]) + dot(into_h, box_l[part]))
    modes = jnp.concatenate(modes, axis=0)
    rim_low, rim_high = (jnp.broadcast_to(rim[:, k : k + 1], (pad, LANES)) for k in (0, 1))
    solved = []
    for i in range(nx):
        value = modes[i * pad : (i + 1) * pad]
        if 0 < i < nx - 1:
            at = 2 * size_y + i - 1
            value = value + rim_low * edge[at : at + 1] + rim_high * edge[at + size_x : at + size_x + 1]
        if i:
            value = value + solved[-1]
        solved.append(value * factors[i * pad : (i + 1) * pad])
    for i in reversed(range(nx - 1)):
        solved[i] = solved[i] + factors[i * pad : (i + 1) * pad] * solved[i + 1]
    solved = jnp.concatenate(solved, axis=0)
    high, low = halves(solved)
    own_rows, face_rows = GROUP * size_y, 2 * size_x
    half = back_faces.shape[0] // 2
    local, y_faces = [], None
    for g in range(nx // GROUP):
        part = slice(g * GROUP * pad, (g + 1) * GROUP * pad)
        line = slice(g * face_rows, (g + 1) * face_rows)
        table_h = jnp.concatenate([back[:own_rows], back_faces[line]], axis=0)[:, : GROUP * pad]
        line = slice(half + g * face_rows, half + (g + 1) * face_rows)
        table_l = jnp.concatenate([back[own_rows:], back_faces[line]], axis=0)[:, : GROUP * pad]
        value = dot(table_h, high[part]) + dot(table_l, high[part]) + dot(table_h, low[part])
        local.append(value[:own_rows])
        rest = value[own_rows:]
        y_faces = rest if y_faces is None else y_faces + rest
    local = jnp.concatenate(local + [y_faces], axis=0)
    local = local * scale[0:1, 0:1]
    high, low = halves(local)
    both = dot(high, out[...])
    local = both[:, :size_z] + both[:, size_z:] + dot(low, out[:, :size_z])
    own_h, own_l = high[size_y : size_y + rows], low[size_y : size_y + rows]
    face = dot_lanes(out_ends[0:16], own_h) + dot_lanes(out_ends[0:16], own_l) + dot_lanes(out_ends[16:32], own_h)

    def inner(shape, dim):
        at = iota(shape, dim)
        return (at >= 1) & (at <= shape[dim] - 2)

    own_flat = mask[...].reshape(rows, size_z) * local[size_y : size_y + rows]
    own_box = own_flat.reshape(size_x, size_y, size_z)
    own[...] = own_box
    shape = (size_y, size_z)
    kept = inner(shape, 0) & inner(shape, 1)
    g_low = jnp.where(kept, local[:size_y] * x_low[1], 0.0)
    g_high = jnp.where(kept, local[size_y + rows : 2 * size_y + rows] * x_high[1], 0.0)
    even = where_x[0]
    low, high = own_box[0], own_box[size_x - 1]
    tx0[0] = jnp.where(even, high, low)
    tx0[1] = jnp.where(even, g_high, g_low)
    tx1[0] = jnp.where(even, low, high)
    tx1[1] = jnp.where(even, g_low, g_high)
    shape = (size_x, size_z)
    kept = inner(shape, 0) & inner(shape, 1)
    at = 2 * size_y + rows
    g_low = jnp.where(kept, local[at : at + size_x] * y_low[1], 0.0)
    g_high = jnp.where(kept, local[at + size_x : at + 2 * size_x] * y_high[1], 0.0)
    even = where_y[0]
    low, high = own_box[:, 0], own_box[:, size_y - 1]
    ty0[0] = jnp.where(even, high, low)
    ty0[1] = jnp.where(even, g_high, g_low)
    ty1[0] = jnp.where(even, low, high)
    ty1[1] = jnp.where(even, g_low, g_high)
    mine = lane_rows([own_flat], jnp.where(even_z, size_z - 1, 0))
    ids = iota((1, rows), 1)
    x_at, y_at = ids // size_y, ids % size_y
    kept = (x_at >= 1) & (x_at <= size_x - 2) & (y_at >= 1) & (y_at <= size_y - 2)
    ghost = jnp.where(kept, jnp.where(even_z, face[1:2], face[0:1]) * rz[1:2], 0.0)
    tz[...] = jnp.where(iota((8, rows), 0) == 1, jnp.broadcast_to(ghost, (8, rows)), mine)


def beside(value, y_sides, face, box):
    size_x, size_y, size_z = box
    rows = size_x * size_y

    def wide(side):
        return jnp.broadcast_to(side[:, None, :], box).reshape(rows, size_z)

    at = iota((rows, size_z), 0) % size_y
    next_y = jnp.where(at == size_y - 1, wide(y_sides[1]), pltpu.roll(value, rows - 1, 0))
    at = iota((rows, size_z), 1)
    next_z = jnp.where(at == size_z - 1, face, pltpu.roll(value, size_z - 1, 1))
    return next_y, next_z, wide(y_sides[0])


def flux(value, x_sides, y_sides, face, wx, wy, wy0, wz, wz0, box):
    size_x, size_y, size_z = box
    rows = size_x * size_y
    ext = jnp.concatenate([x_sides[0][None], value.reshape(box), x_sides[1][None]], axis=0)
    flow = wx * (ext[1:] - ext[:-1])
    total = (flow[:-1] - flow[1:]).reshape(rows, size_z)
    next_y, next_z, before_y = beside(value, y_sides, face, box)
    flow = wy * (next_y - value)
    at = iota((rows, size_z), 0) % size_y
    first = wy0 * (value - before_y)
    total = total + jnp.where(at == 0, first, pltpu.roll(flow, 1, 0)) - flow
    flow = wz * (next_z - value)
    first = wz0 * (value - face)
    at = iota((rows, size_z), 1)
    return total + jnp.where(at == 0, first, pltpu.roll(flow, 1, 1)) - flow


def links_kernel(
    mask, d, mu, rx0, rx1, ry0, ry1, rz,
    ad_out, wx_out, wy_out, wy0_out, wz_out, wz0_out,
):
    box = mask.shape
    size_x, size_y, size_z = box
    rows = size_x * size_y
    where_x, where_y, where_z = (place(axis) for axis in AXES)
    x_near = sides(rx0[2:4], rx1[2:4], where_x)
    y_near = sides(ry0[2:4], ry1[2:4], where_y)
    d_face, mu_face = lane_ends([rz[2:3], rz[3:4]], where_z[0], size_z)
    mu_own = mu[...].reshape(rows, size_z)
    ext = jnp.concatenate([x_near[0][1][None], mu[...], x_near[1][1][None]], axis=0)
    wx = 0.5 * (ext[1:] + ext[:-1])
    next_y, next_z, before_y = beside(mu_own, [v[1] for v in y_near], mu_face, box)
    wy, wy0 = 0.5 * (mu_own + next_y), 0.5 * (mu_own + before_y)
    wz, wz0 = 0.5 * (mu_own + next_z), 0.5 * (mu_own + mu_face)
    links = (wx, wy, wy0, wz, wz0)
    wx_out[...], wy_out[...], wy0_out[...], wz_out[...], wz0_out[...] = links
    value = d[...].reshape(rows, size_z)
    ad = flux(value, [v[0] for v in x_near], [v[0] for v in y_near], d_face, *links, box)
    ad_out[...] = mask[...].reshape(rows, size_z) * ad


def image_kernel(
    masked, mask, d, own, tx0, tx1, ty0, ty1, tz, qx0, qx1, qy0, qy1, qz, ad_in, wx, wy, wy0, wz, wz0,
    z_out, az_out, sums,
):
    box = mask.shape
    size_x, size_y, size_z = box
    rows = size_x * size_y
    where_x, where_y, where_z = (place(axis) for axis in AXES)
    x_sent = sides(tx0[1:2], tx1[1:2], where_x)
    y_sent = sides(ty0[1:2], ty1[1:2], where_y)
    x_got = sides(qx0[...], qx1[...], where_x)
    y_got = sides(qy0[...], qy1[...], where_y)
    z_face, z_more = lane_ends([qz[0:1] + tz[1:2], qz[1:2]], where_z[0], size_z)
    own_box = own[...]
    z = jnp.concatenate(
        [own_box[:1] + x_got[0][1][None], own_box[1:-1], own_box[-1:] + x_got[1][1][None]], axis=0
    )
    at = iota(box, 1)
    z = z + jnp.where(at == 0, y_got[0][1][:, None, :], 0.0) + jnp.where(at == size_y - 1, y_got[1][1][:, None, :], 0.0)
    z = z.reshape(rows, size_z) + z_more
    z = z * mask[...].reshape(rows, size_z)
    x_sides = [x_got[s][0] + x_sent[s][0] for s in (0, 1)]
    y_sides = [y_got[s][0] + y_sent[s][0] for s in (0, 1)]
    az = flux(z, x_sides, y_sides, z_face, wx[...], wy[...], wy0[...], wz[...], wz0[...], box)
    az = mask[...].reshape(rows, size_z) * az
    z_out[...] = z
    az_out[...] = az
    ad, value = ad_in[...], d[...].reshape(rows, size_z)
    parts = (
        jnp.sum(masked[...].reshape(rows, size_z) * z),
        jnp.sum(z * az),
        jnp.sum(z * ad + value * az),
        jnp.sum(value * ad),
    )
    at = iota(sums.shape, 2)
    line = jnp.zeros(sums.shape, F32)
    for k, part in enumerate(parts):
        line = jnp.where(at == k, part, line)
    sums[...] = line


def update_kernel(rz_prev, sums, iterate, res, d, z, az, ad, new_iterate, new_res, new_direction):
    line = jnp.sum(sums[...], axis=0)
    rz, zaz, zad, dad = (line[:, k : k + 1] for k in range(4))
    beta = rz / rz_prev[0]
    alpha = rz / (zaz + beta * (zad + beta * dad))
    alpha3, beta3 = (v.reshape(1, 1, 1) for v in (alpha, beta))
    box = d.shape
    p = z[...].reshape(box) + beta3 * d[...]
    new_direction[...] = p
    new_iterate[...] = iterate[...] + alpha3 * p
    new_res[...] = res[...] - alpha3 * (az[...] + beta * ad[...]).reshape(box)


def call(kernel, args, outs, specs=None):
    outs = [jax.ShapeDtypeStruct(out, F32) for out in outs]
    return pl.pallas_call(
        kernel,
        out_shape=outs,
        in_specs=specs or [VMEM] * len(args),
        out_specs=[VMEM] * len(outs),
        cost_estimate=pl.CostEstimate(flops=0, bytes_accessed=1 << 20, transcendentals=0),
        compiler_params=pltpu.CompilerParams(vmem_limit_bytes=32 * 1024 * 1024),
    )(*args)


def exchange(sx0, sx1, sy0, sy1, sz):
    return (
        swap(sx0, "gx", 0),
        swap(sx1, "gx", 1),
        swap(sy0, "gy", 0),
        swap(sy1, "gy", 1),
        swap(sz, "gz", 0),
    )


def shards(iterate, residual, direction, permeability, unfixed_node_mask, rz_prev):
    size_x, size_y, size_z = residual.shape
    box = residual.shape
    rows = size_x * size_y
    flat = (rows, size_z)
    devices = lax.axis_size(AXES)

    def faces(count):
        return [(count, size_y, size_z)] * 2 + [(count, size_x, size_z)] * 2 + [(8, rows)]

    fwd, middle, *tables = map(jnp.asarray, solve_tables(size_x, size_y, size_z).values())
    with jax.named_scope("masks"):
        masked = unfixed_node_mask.astype(F32) * residual
        mu = permeability
    with jax.named_scope("pack"):
        *sent, mask, d = call(pack_kernel, (masked, unfixed_node_mask, direction, mu), faces(4) + [box] * 2)
    with jax.named_scope("faces_in"):
        near = exchange(*sent)
    with jax.named_scope("own_part"):
        modes = ((size_x + 2) * middle.shape[0], LANES)
        part = call(own_kernel, (masked, mu, fwd, middle), [(rows, LANES), modes, (8, size_z)])
    with jax.named_scope("solve"):
        own, *made = call(solve_kernel, (*part, mask, *near, fwd, *tables), [box] + faces(2))
    with jax.named_scope("faces_out"):
        got = exchange(*made)
    with jax.named_scope("links"):
        ad, *links = call(
            links_kernel, (mask, d, mu, *near), [flat, (size_x + 1, size_y, size_z), flat, flat, flat, flat]
        )
    with jax.named_scope("image"):
        z, az, sums = call(
            image_kernel, (masked, mask, d, own, *made, *got, ad, *links), [flat, flat, (devices, 1, 128)]
        )
    with jax.named_scope("sums"):
        sums = lax.all_to_all(sums, AXES, 0, 0, tiled=True)
    with jax.named_scope("update"):
        args = (rz_prev, sums, iterate, residual, d, z, az, ad)
        return tuple(call(update_kernel, args, [box] * 3, [SMEM] + [VMEM] * 7))


def solution(mesh):
    in_specs = (P(*AXES),) * 5 + (P(),)
    out_specs = (P(*AXES),) * 3
    return jax.shard_map(shards, mesh=mesh, in_specs=in_specs, out_specs=out_specs, check_vma=False)
```

```python
import functools

import jax
import jax.numpy as jnp
import ml_dtypes
import numpy as np
from jax import lax
from jax.experimental import pallas as pl
from jax.experimental.pallas import tpu as pltpu
from jax.sharding import PartitionSpec as P

AXES = ("gx", "gy", "gz")
F32 = jnp.float32
BF16 = jnp.bfloat16
HIGHEST = lax.Precision.HIGHEST
VMEM = pl.BlockSpec(memory_space=pltpu.VMEM)
SMEM = pl.BlockSpec(memory_space=pltpu.SMEM)
LANES = 256
GROUP = 6


def swaps(axis, turn):
    counts = [lax.axis_size(name) for name in AXES]
    dim = AXES.index(axis)
    pairs = []
    for source in np.ndindex(*counts):
        target = list(source)
        step = 1 if (source[dim] + turn) % 2 == 0 else -1
        if axis == "gy" and not 0 <= source[dim] + step < counts[dim]:
            target[0] ^= 1
        else:
            target[dim] = (source[dim] + step) % counts[dim]
        pairs.append(tuple(int(np.ravel_multi_index(where, counts)) for where in (source, target)))
    return pairs


def swap(block, axis, turn):
    return lax.ppermute(block, AXES, swaps(axis, turn))


def place(axis):
    index = lax.axis_index(axis)
    return index % 2 == 0, index > 0, index < lax.axis_size(axis) - 1


def sides(turn0, turn1, where):
    even, below, above = where
    low = jnp.where(below, jnp.where(even, turn1, turn0), 0.0)
    high = jnp.where(above, jnp.where(even, turn0, turn1), 0.0)
    return low, high


def halves(value):
    high = value.astype(BF16)
    return high, (value - high.astype(F32)).astype(BF16)


def dot(a, b):
    return lax.dot_general(a, b, (((1,), (0,)), ((), ())), preferred_element_type=F32)


def dot_rows(a, b):
    return lax.dot_general(a, b, (((0,), (0,)), ((), ())), preferred_element_type=F32)


def dot_lanes(a, b):
    return lax.dot_general(a, b, (((1,), (1,)), ((), ())), preferred_element_type=F32)


def iota(shape, dim):
    return lax.broadcasted_iota(jnp.int32, shape, dim)


def basis(n):
    idx = np.arange(n, dtype=np.float64) + 1.0
    values = 2.0 - 2.0 * np.cos(np.pi * idx / (n + 1))
    return np.sqrt(2.0 / (n + 1)) * np.sin(np.pi * idx[:, None] * idx[None, :] / (n + 1)), values


def np_halves(table):
    high = table.astype(np.float32).astype(ml_dtypes.bfloat16)
    return high, (table - high.astype(np.float64)).astype(np.float32).astype(ml_dtypes.bfloat16)


@functools.cache
def solve_tables(size_x, size_y, size_z):
    nx, ny, nz = size_x + 2, size_y + 2, size_z + 2
    qy, ly = basis(ny)
    qz, lz = basis(nz)
    pad = -(-ny // 8) * 8
    forward = np.zeros((size_z, LANES))
    forward[:, :nz] = qz[1:-1]
    ends = np.zeros((2, LANES))
    ends[:, :nz] = qz[[0, -1]]
    fh, fl = np_halves(forward)
    eh, el = np_halves(ends)
    face = np.zeros((16, LANES), ml_dtypes.bfloat16)
    face[0:2], face[2:4], face[4:6] = eh, eh, el
    out_ends = np.zeros((32, LANES), ml_dtypes.bfloat16)
    out_ends[0:2], out_ends[16:18] = eh, el
    into = np.zeros((GROUP * pad, LANES))
    for s in range(GROUP):
        into[s * pad : s * pad + ny, s * size_y : (s + 1) * size_y] = qy[1:-1].T
    rim = np.zeros((pad, LANES // 2))
    rim[:ny, 0], rim[:ny, 1] = qy[0], qy[-1]
    groups = nx // GROUP
    back = np.zeros((GROUP * size_y, LANES))
    faces = np.zeros((groups, 2, size_x, LANES))
    for s in range(GROUP):
        modes = slice(s * pad, s * pad + ny)
        back[s * size_y : (s + 1) * size_y, modes] = qy[1:-1]
        for g in range(groups):
            i = g * GROUP + s - 1
            if 0 <= i < size_x:
                faces[g, 0, i, modes] = qy[0]
                faces[g, 1, i, modes] = qy[-1]
    middle = np.full((pad, LANES), 2.0)
    middle[:ny, :nz] += ly[:, None] + lz[None, :]
    middle[ny:], middle[:, nz:] = 4.0, 4.0
    ih, il = np_halves(into)
    bh, bl = np_halves(back)
    gh, gl = np_halves(faces.reshape(-1, LANES))
    return dict(
        fwd=np.concatenate([fh, fl]),
        middle=middle.astype(np.float32),
        face=face,
        into=np.concatenate([ih, il]),
        back=np.concatenate([bh, bl]),
        back_faces=np.concatenate([gh, gl]),
        rim=rim.astype(np.float32),
        out=np.concatenate([np.ascontiguousarray(fh.T), np.ascontiguousarray(fl.T)], axis=1),
        out_ends=out_ends,
    )


def lane_rows(fields, lane):
    depth = fields[0].shape[1]
    total = None
    for f, field in enumerate(fields):
        at = iota((16, 2 * depth), 1)
        pick = jnp.where((iota((16, 2 * depth), 0) == f) & ((at == lane) | (at == lane + depth)), 1.0, 0.0).astype(BF16)
        rows = dot_lanes(pick, jnp.concatenate(halves(field), axis=1))
        total = rows if total is None else total + rows
    return total[:8]


def lane_ends(lines, even, depth):
    count = len(lines)
    pieces = []
    for line in lines:
        pieces += halves(line)
    size = lines[0].shape[1]
    stack = jnp.zeros((16, size), F32)
    for k, piece in enumerate(pieces):
        stack = jnp.where(iota((16, size), 0) == k, piece.astype(F32), stack)
    shape = (16, count * depth)
    lane = jnp.where(even, depth - 1, 0) + iota(shape, 0) // 2 * depth
    pick = jnp.where((iota(shape, 0) < 2 * count) & (iota(shape, 1) == lane), 1.0, 0.0).astype(BF16)
    wide = dot_rows(stack.astype(BF16), pick)
    return [wide[:, k * depth : (k + 1) * depth] for k in range(count)]


def pack_kernel(masked, msk, direction, mu, sx0, sx1, sy0, sy1, sz, mask_out, d):
    size_x, size_y, size_z = masked.shape
    even_x, even_y, even_z = (place(axis)[0] for axis in AXES)
    mask = msk[...].astype(F32)
    fields = (masked[...], mask, mask * direction[...], mu[...])
    mask_out[...], d[...] = fields[1], fields[2]
    for f, field in enumerate(fields):
        low, high = field[0], field[size_x - 1]
        sx0[f] = jnp.where(even_x, high, low)
        sx1[f] = jnp.where(even_x, low, high)
        low, high = field[:, 0], field[:, size_y - 1]
        sy0[f] = jnp.where(even_y, high, low)
        sy1[f] = jnp.where(even_y, low, high)
    flat = [field.reshape(size_x * size_y, size_z) for field in fields]
    sz[...] = lane_rows(flat, jnp.where(even_z, size_z - 1, 0))


def along_z(rows, fwd, size_z):
    high, low = halves(rows)
    table = fwd[:size_z]
    return dot(jnp.concatenate([high, low], axis=1), jnp.concatenate([table, table], axis=0)) + dot(high, fwd[size_z:])


def own_kernel(masked, mu, fwd, middle, work, factors, scale):
    size_x, size_y, size_z = masked.shape
    work[...] = along_z(masked[...].reshape(size_x * size_y, size_z), fwd, size_z)
    pad = middle.shape[0]
    along = middle[...]
    previous = 1.0 / along
    factors[0:pad] = previous
    for i in range(1, size_x + 2):
        previous = 1.0 / (along - previous)
        factors[i * pad : (i + 1) * pad] = previous
    scale[...] = jnp.full((8, size_z), (size_x * size_y * size_z) / jnp.sum(mu[...]))


def solve_kernel(
    work, factors, scale, mask, rx0, rx1, ry0, ry1, rz, fwd, face_table, into, back, back_faces, rim, out, out_ends,
    own, tx0, tx1, ty0, ty1, tz,
):
    size_x, size_y, size_z = mask.shape
    rows = size_x * size_y
    pad = rim.shape[0]
    nx = size_x + 2
    where_x, where_y, where_z = (place(axis) for axis in AXES)
    even_z = where_z[0]
    x_low, x_high = sides(rx0[0:2], rx1[0:2], where_x)
    y_low, y_high = sides(ry0[0:2], ry1[0:2], where_y)
    edge = along_z(jnp.concatenate([x_low[0], x_high[0], y_low[0], y_high[0]], axis=0), fwd, size_z)
    line = rz[0:1]
    line_h, line_l = halves(line)
    at = iota((16, rows), 0)
    mine = (at < 6) & (at % 2 == jnp.where(even_z, 1, 0))
    line = jnp.where(mine, jnp.where(at // 2 == 1, line_l.astype(F32), line_h.astype(F32)), 0.0)
    face = dot_rows(line.astype(BF16), face_table[...])
    box = jnp.concatenate([edge[:size_y], work[...] + face, edge[size_y : 2 * size_y]], axis=0)
    box_h, box_l = halves(box)
    modes = []
    into_h, into_l = into[: GROUP * pad, : GROUP * size_y], into[GROUP * pad :, : GROUP * size_y]
    for g in range(nx // GROUP):
        part = slice(g * GROUP * size_y, (g + 1) * GROUP * size_y)
        modes.append(dot(into_h, box_h[part]) + dot(into_l, box_h[part]) + dot(into_h, box_l[part]))
    modes = jnp.concatenate(modes, axis=0)
    rim_low, rim_high = (jnp.broadcast_to(rim[:, k : k + 1], (pad, LANES)) for k in (0, 1))
    solved = []
    for i in range(nx):
        value = modes[i * pad : (i + 1) * pad]
        if 0 < i < nx - 1:
            at = 2 * size_y + i - 1
            value = value + rim_low * edge[at : at + 1] + rim_high * edge[at + size_x : at + size_x + 1]
        if i:
            value = value + solved[-1]
        solved.append(value * factors[i * pad : (i + 1) * pad])
    for i in reversed(range(nx - 1)):
        solved[i] = solved[i] + factors[i * pad : (i + 1) * pad] * solved[i + 1]
    solved = jnp.concatenate(solved, axis=0)
    high, low = halves(solved)
    own_rows, face_rows = GROUP * size_y, 2 * size_x
    half = back_faces.shape[0] // 2
    local, y_faces = [], None
    for g in range(nx // GROUP):
        part = slice(g * GROUP * pad, (g + 1) * GROUP * pad)
        line = slice(g * face_rows, (g + 1) * face_rows)
        table_h = jnp.concatenate([back[:own_rows], back_faces[line]], axis=0)[:, : GROUP * pad]
        line = slice(half + g * face_rows, half + (g + 1) * face_rows)
        table_l = jnp.concatenate([back[own_rows:], back_faces[line]], axis=0)[:, : GROUP * pad]
        value = dot(table_h, high[part]) + dot(table_l, high[part]) + dot(table_h, low[part])
        local.append(value[:own_rows])
        rest = value[own_rows:]
        y_faces = rest if y_faces is None else y_faces + rest
    local = jnp.concatenate(local + [y_faces], axis=0)
    local = local * scale[0:1, 0:1]
    high, low = halves(local)
    both = dot(high, out[...])
    local = both[:, :size_z] + both[:, size_z:] + dot(low, out[:, :size_z])
    own_h, own_l = high[size_y : size_y + rows], low[size_y : size_y + rows]
    face = dot_lanes(out_ends[0:16], own_h) + dot_lanes(out_ends[0:16], own_l) + dot_lanes(out_ends[16:32], own_h)

    def inner(shape, dim):
        at = iota(shape, dim)
        return (at >= 1) & (at <= shape[dim] - 2)

    own_flat = mask[...].reshape(rows, size_z) * local[size_y : size_y + rows]
    own_box = own_flat.reshape(size_x, size_y, size_z)
    own[...] = own_box
    shape = (size_y, size_z)
    kept = inner(shape, 0) & inner(shape, 1)
    g_low = jnp.where(kept, local[:size_y] * x_low[1], 0.0)
    g_high = jnp.where(kept, local[size_y + rows : 2 * size_y + rows] * x_high[1], 0.0)
    even = where_x[0]
    low, high = own_box[0], own_box[size_x - 1]
    tx0[0] = jnp.where(even, high, low)
    tx0[1] = jnp.where(even, g_high, g_low)
    tx1[0] = jnp.where(even, low, high)
    tx1[1] = jnp.where(even, g_low, g_high)
    shape = (size_x, size_z)
    kept = inner(shape, 0) & inner(shape, 1)
    at = 2 * size_y + rows
    g_low = jnp.where(kept, local[at : at + size_x] * y_low[1], 0.0)
    g_high = jnp.where(kept, local[at + size_x : at + 2 * size_x] * y_high[1], 0.0)
    even = where_y[0]
    low, high = own_box[:, 0], own_box[:, size_y - 1]
    ty0[0] = jnp.where(even, high, low)
    ty0[1] = jnp.where(even, g_high, g_low)
    ty1[0] = jnp.where(even, low, high)
    ty1[1] = jnp.where(even, g_low, g_high)
    mine = lane_rows([own_flat], jnp.where(even_z, size_z - 1, 0))
    ids = iota((1, rows), 1)
    x_at, y_at = ids // size_y, ids % size_y
    kept = (x_at >= 1) & (x_at <= size_x - 2) & (y_at >= 1) & (y_at <= size_y - 2)
    ghost = jnp.where(kept, jnp.where(even_z, face[1:2], face[0:1]) * rz[1:2], 0.0)
    tz[...] = jnp.where(iota((8, rows), 0) == 1, jnp.broadcast_to(ghost, (8, rows)), mine)


def stencil(slabs, y_low, y_high, faces, links, box):
    size_x, size_y, size_z = box
    wx, wy, wy0, wz, wz0 = links
    row, lane = iota((size_y, size_z), 0), iota((size_y, size_z), 1)
    below = wx[0] * (slabs[1] - slabs[0])
    for i in range(size_x):
        value, face = slabs[i + 1], faces(i)
        above = wx[i + 1] * (slabs[i + 2] - value)
        total = below - above
        below = above
        flow = wy[i] * (jnp.where(row == size_y - 1, y_high[i : i + 1], pltpu.roll(value, size_y - 1, 0)) - value)
        first = wy0[i : i + 1] * (value - y_low[i : i + 1])
        total = total + (jnp.where(row == 0, first, pltpu.roll(flow, 1, 0)) - flow)
        flow = wz[i] * (jnp.where(lane == size_z - 1, face, pltpu.roll(value, size_z - 1, 1)) - value)
        first = wz0[i] * (value - face)
        yield i, total + (jnp.where(lane == 0, first, pltpu.roll(flow, 1, 1)) - flow)


def links_kernel(
    rz_prev, mask, d, mu, rx0, rx1, ry0, ry1, rz,
    ad_out, wx, wy, wy0, wz, wz0, dad, rz_line,
):
    box = mask.shape
    size_x, size_y, size_z = box
    where_x, where_y, where_z = (place(axis) for axis in AXES)
    x_near = sides(rx0[2:4], rx1[2:4], where_x)
    y_near = sides(ry0[2:4], ry1[2:4], where_y)
    d_face, mu_face = (
        wide.reshape(box) for wide in lane_ends([rz[2:3], rz[3:4]], where_z[0], size_z)
    )
    row, lane = iota((size_y, size_z), 0), iota((size_y, size_z), 1)
    slabs = [x_near[0][1]] + [mu[i] for i in range(size_x)] + [x_near[1][1]]
    wx[0] = 0.5 * (slabs[0] + slabs[1])
    mu_low, mu_high = y_near[0][1], y_near[1][1]
    for i in range(size_x):
        value, face = slabs[i + 1], mu_face[i]
        wx[i + 1] = 0.5 * (value + slabs[i + 2])
        wy[i] = 0.5 * (value + jnp.where(row == size_y - 1, mu_high[i : i + 1], pltpu.roll(value, size_y - 1, 0)))
        wy0[i : i + 1] = 0.5 * (value[0:1] + mu_low[i : i + 1])
        wz[i] = 0.5 * (value + jnp.where(lane == size_z - 1, face, pltpu.roll(value, size_z - 1, 1)))
        wz0[i] = 0.5 * (value + face)
    slabs = [x_near[0][0]] + [d[i] for i in range(size_x)] + [x_near[1][0]]
    total = jnp.zeros((size_y, size_z), F32)
    for i, image in stencil(slabs, y_near[0][0], y_near[1][0], lambda i: d_face[i], (wx, wy, wy0, wz, wz0), box):
        image = mask[i] * image
        ad_out[i] = image
        total = total + slabs[i + 1] * image
    dad[...] = jnp.sum(total, axis=0, keepdims=True)
    rz_line[...] = jnp.full(rz_line.shape, rz_prev[0])


def image_kernel(
    masked, mask, d, own, tx0, tx1, ty0, ty1, tz, qx0, qx1, qy0, qy1, qz, ad, wx, wy, wy0, wz, wz0, dad,
    z_out, az_out, sums,
):
    box = mask.shape
    size_x, size_y, size_z = box
    where_x, where_y, where_z = (place(axis) for axis in AXES)
    x_sent = sides(tx0[1], tx1[1], where_x)
    y_sent = sides(ty0[1], ty1[1], where_y)
    x_got = sides(qx0[...], qx1[...], where_x)
    y_got = sides(qy0[...], qy1[...], where_y)
    face, more = (
        wide.reshape(box) for wide in lane_ends([qz[0:1] + tz[1:2], qz[1:2]], where_z[0], size_z)
    )
    row = iota((size_y, size_z), 0)
    slabs = [x_got[0][0] + x_sent[0]]
    for i in range(size_x):
        value = own[i] + more[i]
        value = value + jnp.where(row == 0, y_got[0][1][i : i + 1], 0.0)
        value = value + jnp.where(row == size_y - 1, y_got[1][1][i : i + 1], 0.0)
        if i == 0:
            value = value + x_got[0][1]
        if i == size_x - 1:
            value = value + x_got[1][1]
        z_out[i] = value
        slabs.append(value)
    slabs.append(x_got[1][0] + x_sent[1])
    y_sides = [y_got[s][0] + y_sent[s] for s in (0, 1)]
    rz = zaz = zad = jnp.zeros((size_y, size_z), F32)
    for i, image in stencil(slabs, *y_sides, lambda i: face[i], (wx, wy, wy0, wz, wz0), box):
        value = slabs[i + 1]
        image = mask[i] * image
        az_out[i] = image
        rz = rz + masked[i] * value
        zaz = zaz + value * image
        zad = zad + (value * ad[i] + d[i] * image)
    at = iota(sums.shape, 2)
    line = jnp.zeros(sums.shape, F32)
    for k, part in enumerate((rz, zaz, zad, dad[...])):
        line = jnp.where(at == k, jnp.sum(part), line)
    sums[...] = line


def update_kernel(
    rz_line, sums, iterate, res, d, z, az, ad, new_iterate, new_res, new_direction, out_iterate, out_res, out_p, gone,
):
    line = jnp.sum(sums[...], axis=0)
    rz, zaz, zad, dad = (line[:, k : k + 1] for k in range(4))
    beta = rz / rz_line[:, 0:1]
    alpha = rz / (zaz + beta * (zad + beta * dad))
    alpha, beta = (v.reshape(1, 1, 1) for v in (alpha, beta))
    p = z[...] + beta * d[...]
    out_p[...] = p
    copies = [pltpu.make_async_copy(out_p, new_direction, gone.at[0])]
    copies[0].start()
    out_iterate[...] = iterate[...] + alpha * p
    copies.append(pltpu.make_async_copy(out_iterate, new_iterate, gone.at[1]))
    copies[1].start()
    out_res[...] = res[...] - alpha * (az[...] + beta * ad[...])
    copies.append(pltpu.make_async_copy(out_res, new_res, gone.at[2]))
    copies[2].start()
    for copy in copies:
        copy.wait()


def call(kernel, args, outs, specs=None, out_spec=VMEM, scratch=()):
    outs = [jax.ShapeDtypeStruct(out, F32) for out in outs]
    return pl.pallas_call(
        kernel,
        out_shape=outs,
        in_specs=specs or [VMEM] * len(args),
        out_specs=[out_spec] * len(outs),
        scratch_shapes=list(scratch),
        cost_estimate=pl.CostEstimate(flops=0, bytes_accessed=1 << 20, transcendentals=0),
        compiler_params=pltpu.CompilerParams(vmem_limit_bytes=32 * 1024 * 1024),
    )(*args)


def exchange(sx0, sx1, sy0, sy1, sz):
    return (
        swap(sx0, "gx", 0),
        swap(sx1, "gx", 1),
        swap(sy0, "gy", 0),
        swap(sy1, "gy", 1),
        swap(sz, "gz", 0),
    )


def shards(iterate, residual, direction, permeability, unfixed_node_mask, rz_prev):
    size_x, size_y, size_z = residual.shape
    box = residual.shape
    rows = size_x * size_y
    flat = (rows, size_z)
    devices = lax.axis_size(AXES)

    def faces(count):
        return [(count, size_y, size_z)] * 2 + [(count, size_x, size_z)] * 2 + [(8, rows)]

    fwd, middle, *tables = map(jnp.asarray, solve_tables(size_x, size_y, size_z).values())
    with jax.named_scope("masks"):
        masked = unfixed_node_mask.astype(F32) * residual
        mu = permeability
    with jax.named_scope("pack"):
        *sent, mask, d = call(pack_kernel, (masked, unfixed_node_mask, direction, mu), faces(4) + [box] * 2)
    with jax.named_scope("faces_in"):
        near = exchange(*sent)
    with jax.named_scope("own_part"):
        modes = ((size_x + 2) * middle.shape[0], LANES)
        part = call(own_kernel, (masked, mu, fwd, middle), [(rows, LANES), modes, (8, size_z)])
    with jax.named_scope("solve"):
        own, *made = call(solve_kernel, (*part, mask, *near, fwd, *tables), [box] + faces(2))
    with jax.named_scope("faces_out"):
        got = exchange(*made)
    with jax.named_scope("links"):
        outs = [box, (size_x + 1, size_y, size_z), box, (size_x, size_z), box, box, (1, size_z), (1, size_z)]
        ad, *links, rz_line = call(links_kernel, (rz_prev, mask, d, mu, *near), outs, [SMEM] + [VMEM] * 8)
    with jax.named_scope("image"):
        z, az, sums = call(image_kernel, (masked, mask, d, own, *made, *got, ad, *links), [box, box, (devices, 1, 128)])
    with jax.named_scope("sums"):
        sums = lax.all_to_all(sums, AXES, 0, 0, tiled=True)
    with jax.named_scope("update"):
        args = (rz_line, sums, iterate, residual, d, z, az, ad)
        scratch = [pltpu.VMEM(box, F32)] * 3 + [pltpu.SemaphoreType.DMA((3,))]
        return tuple(call(update_kernel, args, [box] * 3, None, pl.BlockSpec(memory_space=pl.ANY), scratch))


def solution(mesh):
    in_specs = (P(*AXES),) * 5 + (P(),)
    out_specs = (P(*AXES),) * 3
    return jax.shard_map(shards, mesh=mesh, in_specs=in_specs, out_specs=out_specs, check_vma=False)
```

```python
import functools

import jax
import jax.numpy as jnp
import ml_dtypes
import numpy as np
from jax import lax
from jax.experimental import pallas as pl
from jax.experimental.pallas import tpu as pltpu
from jax.sharding import PartitionSpec as P

AXES = ("gx", "gy", "gz")
F32 = jnp.float32
BF16 = jnp.bfloat16
HIGHEST = lax.Precision.HIGHEST
VMEM = pl.BlockSpec(memory_space=pltpu.VMEM)
SMEM = pl.BlockSpec(memory_space=pltpu.SMEM)
LANES = 256
GROUP = 6


def swaps(axis, turn):
    counts = [lax.axis_size(name) for name in AXES]
    dim = AXES.index(axis)
    pairs = []
    for source in np.ndindex(*counts):
        target = list(source)
        step = 1 if (source[dim] + turn) % 2 == 0 else -1
        if axis == "gy" and not 0 <= source[dim] + step < counts[dim]:
            target[0] ^= 1
        else:
            target[dim] = (source[dim] + step) % counts[dim]
        pairs.append(tuple(int(np.ravel_multi_index(where, counts)) for where in (source, target)))
    return pairs


def swap(block, axis, turn):
    return lax.ppermute(block, AXES, swaps(axis, turn))


def place(axis):
    index = lax.axis_index(axis)
    return index % 2 == 0, index > 0, index < lax.axis_size(axis) - 1


def sides(turn0, turn1, where):
    even, below, above = where
    low = jnp.where(below, jnp.where(even, turn1, turn0), 0.0)
    high = jnp.where(above, jnp.where(even, turn0, turn1), 0.0)
    return low, high


def halves(value):
    high = value.astype(BF16)
    return high, (value - high.astype(F32)).astype(BF16)


def dot(a, b):
    return lax.dot_general(a, b, (((1,), (0,)), ((), ())), preferred_element_type=F32)


def dot_rows(a, b):
    return lax.dot_general(a, b, (((0,), (0,)), ((), ())), preferred_element_type=F32)


def dot_lanes(a, b):
    return lax.dot_general(a, b, (((1,), (1,)), ((), ())), preferred_element_type=F32)


def iota(shape, dim):
    return lax.broadcasted_iota(jnp.int32, shape, dim)


def basis(n):
    idx = np.arange(n, dtype=np.float64) + 1.0
    values = 2.0 - 2.0 * np.cos(np.pi * idx / (n + 1))
    return np.sqrt(2.0 / (n + 1)) * np.sin(np.pi * idx[:, None] * idx[None, :] / (n + 1)), values


def np_halves(table):
    high = table.astype(np.float32).astype(ml_dtypes.bfloat16)
    return high, (table - high.astype(np.float64)).astype(np.float32).astype(ml_dtypes.bfloat16)


@functools.cache
def solve_tables(size_x, size_y, size_z):
    nx, ny, nz = size_x + 2, size_y + 2, size_z + 2
    qy, ly = basis(ny)
    qz, lz = basis(nz)
    pad = -(-ny // 8) * 8
    forward = np.zeros((size_z, LANES))
    forward[:, :nz] = qz[1:-1]
    ends = np.zeros((2, LANES))
    ends[:, :nz] = qz[[0, -1]]
    fh, fl = np_halves(forward)
    eh, el = np_halves(ends)
    face = np.zeros((16, LANES), ml_dtypes.bfloat16)
    face[0:2], face[2:4], face[4:6] = eh, eh, el
    out_ends = np.zeros((32, LANES), ml_dtypes.bfloat16)
    out_ends[0:2], out_ends[16:18] = eh, el
    into = np.zeros((GROUP * pad, LANES))
    for s in range(GROUP):
        into[s * pad : s * pad + ny, s * size_y : (s + 1) * size_y] = qy[1:-1].T
    rim = np.zeros((pad, LANES // 2))
    rim[:ny, 0], rim[:ny, 1] = qy[0], qy[-1]
    back = np.zeros((GROUP * size_y, LANES))
    for s in range(GROUP):
        back[s * size_y : (s + 1) * size_y, s * pad : s * pad + ny] = qy[1:-1]
    middle = np.full((pad, LANES), 2.0)
    middle[:ny, :nz] += ly[:, None] + lz[None, :]
    middle[ny:], middle[:, nz:] = 4.0, 4.0
    ih, il = np_halves(into)
    bh, bl = np_halves(back)
    return dict(
        fwd=np.concatenate([fh, fl]),
        middle=middle.astype(np.float32),
        face=face,
        into=np.concatenate([ih, il]),
        back=np.concatenate([bh, bl]),
        rim=rim.astype(np.float32),
        out=np.concatenate([np.ascontiguousarray(fh.T), np.ascontiguousarray(fl.T)], axis=1),
        out_ends=out_ends,
    )


def lane_rows(fields, lane):
    depth = fields[0].shape[1]
    total = None
    for f, field in enumerate(fields):
        at = iota((16, 2 * depth), 1)
        pick = jnp.where((iota((16, 2 * depth), 0) == f) & ((at == lane) | (at == lane + depth)), 1.0, 0.0).astype(BF16)
        rows = dot_lanes(pick, jnp.concatenate(halves(field), axis=1))
        total = rows if total is None else total + rows
    return total[:8]


def lane_ends(lines, even, depth):
    count = len(lines)
    pieces = []
    for line in lines:
        pieces += halves(line)
    size = lines[0].shape[1]
    stack = jnp.zeros((16, size), F32)
    for k, piece in enumerate(pieces):
        stack = jnp.where(iota((16, size), 0) == k, piece.astype(F32), stack)
    shape = (16, count * depth)
    lane = jnp.where(even, depth - 1, 0) + iota(shape, 0) // 2 * depth
    pick = jnp.where((iota(shape, 0) < 2 * count) & (iota(shape, 1) == lane), 1.0, 0.0).astype(BF16)
    wide = dot_rows(stack.astype(BF16), pick)
    return [wide[:, k * depth : (k + 1) * depth] for k in range(count)]


def pack_kernel(masked, msk, direction, mu, sx0, sx1, sy0, sy1, sz):
    size_x, size_y, size_z = masked.shape
    even_x, even_y, even_z = (place(axis)[0] for axis in AXES)

    def fields(where):
        mask = msk[where].astype(F32)
        return masked[where], mask, mask * direction[where], mu[where]

    for f, (low, high) in enumerate(zip(fields(0), fields(size_x - 1))):
        sx0[f] = jnp.where(even_x, high, low)
        sx1[f] = jnp.where(even_x, low, high)
    every = slice(None)
    for f, (low, high) in enumerate(zip(fields((every, 0)), fields((every, size_y - 1)))):
        sy0[f] = jnp.where(even_y, high, low)
        sy1[f] = jnp.where(even_y, low, high)
    flat = [field.reshape(size_x * size_y, size_z) for field in fields(every)]
    sz[...] = lane_rows(flat, jnp.where(even_z, size_z - 1, 0))


def along_z(rows, fwd, size_z):
    high, low = halves(rows)
    table = fwd[:size_z]
    return dot(jnp.concatenate([high, low], axis=1), jnp.concatenate([table, table], axis=0)) + dot(high, fwd[size_z:])


def own_kernel(masked, msk, direction, mu, fwd, middle, work, mask, d, factors, scale):
    size_x, size_y, size_z = masked.shape
    mask[...] = msk[...].astype(F32)
    d[...] = mask[...] * direction[...]
    work[...] = along_z(masked[...].reshape(size_x * size_y, size_z), fwd, size_z)
    pad = middle.shape[0]
    along = middle[...]
    previous = 1.0 / along
    factors[0:pad] = previous
    for i in range(1, size_x + 2):
        previous = 1.0 / (along - previous)
        factors[i * pad : (i + 1) * pad] = previous
    scale[...] = jnp.full((8, size_z), (size_x * size_y * size_z) / jnp.sum(mu[...]))


def solve_kernel(
    work, factors, scale, mask, rx0, rx1, ry0, ry1, rz, fwd, face_table, into, back, rim, out, out_ends,
    own, tx0, tx1, ty0, ty1, tz,
):
    size_x, size_y, size_z = mask.shape
    rows = size_x * size_y
    pad = rim.shape[0]
    nx = size_x + 2
    where_x, where_y, where_z = (place(axis) for axis in AXES)
    even_z = where_z[0]
    x_low, x_high = sides(rx0[0:2], rx1[0:2], where_x)
    y_low, y_high = sides(ry0[0:2], ry1[0:2], where_y)
    edge = along_z(jnp.concatenate([x_low[0], x_high[0], y_low[0], y_high[0]], axis=0), fwd, size_z)
    line = rz[0:1]
    line_h, line_l = halves(line)
    at = iota((16, rows), 0)
    mine = (at < 6) & (at % 2 == jnp.where(even_z, 1, 0))
    line = jnp.where(mine, jnp.where(at // 2 == 1, line_l.astype(F32), line_h.astype(F32)), 0.0)
    face = dot_rows(line.astype(BF16), face_table[...])
    box = jnp.concatenate([edge[:size_y], work[...] + face, edge[size_y : 2 * size_y]], axis=0)
    box_h, box_l = halves(box)
    modes = []
    into_h, into_l = into[: GROUP * pad, : GROUP * size_y], into[GROUP * pad :, : GROUP * size_y]
    for g in range(nx // GROUP):
        part = slice(g * GROUP * size_y, (g + 1) * GROUP * size_y)
        modes.append(dot(into_h, box_h[part]) + dot(into_l, box_h[part]) + dot(into_h, box_l[part]))
    modes = jnp.concatenate(modes, axis=0)
    rim_low, rim_high = (jnp.broadcast_to(rim[:, k : k + 1], (pad, LANES)) for k in (0, 1))
    solved = []
    for i in range(nx):
        value = modes[i * pad : (i + 1) * pad]
        if 0 < i < nx - 1:
            at = 2 * size_y + i - 1
            value = value + rim_low * edge[at : at + 1] + rim_high * edge[at + size_x : at + size_x + 1]
        if i:
            value = value + solved[-1]
        solved.append(value * factors[i * pad : (i + 1) * pad])
    for i in reversed(range(nx - 1)):
        solved[i] = solved[i] + factors[i * pad : (i + 1) * pad] * solved[i + 1]
    solved = jnp.concatenate(solved, axis=0)
    high, low = halves(solved)
    rest = jnp.zeros((LANES - GROUP * pad, LANES), BF16)
    high, low = (jnp.concatenate([half, rest], axis=0) for half in (high, low))
    own_rows = GROUP * size_y
    back_all = jnp.concatenate([back[:own_rows], back[own_rows:], back[:own_rows]], axis=1)
    local = []
    for g in range(nx // GROUP):
        part = slice(g * GROUP * pad, g * GROUP * pad + LANES)
        local.append(dot(back_all, jnp.concatenate([high[part], high[part], low[part]], axis=0)))
    own_modes = solved[pad : (nx - 1) * pad].reshape(size_x, pad, LANES)
    local += [jnp.sum(own_modes * rim_low[None], axis=1), jnp.sum(own_modes * rim_high[None], axis=1)]
    local = jnp.concatenate(local, axis=0)
    local = local * scale[0:1, 0:1]
    high, low = halves(local)
    both = dot(high, out[...])
    local = both[:, :size_z] + both[:, size_z:] + dot(low, out[:, :size_z])
    own_h, own_l = high[size_y : size_y + rows], low[size_y : size_y + rows]
    face = dot_lanes(out_ends[0:16], own_h) + dot_lanes(out_ends[0:16], own_l) + dot_lanes(out_ends[16:32], own_h)

    def inner(shape, dim):
        at = iota(shape, dim)
        return (at >= 1) & (at <= shape[dim] - 2)

    own_flat = mask[...].reshape(rows, size_z) * local[size_y : size_y + rows]
    own_box = own_flat.reshape(size_x, size_y, size_z)
    own[...] = own_box
    shape = (size_y, size_z)
    kept = inner(shape, 0) & inner(shape, 1)
    g_low = jnp.where(kept, local[:size_y] * x_low[1], 0.0)
    g_high = jnp.where(kept, local[size_y + rows : 2 * size_y + rows] * x_high[1], 0.0)
    even = where_x[0]
    low, high = own_box[0], own_box[size_x - 1]
    tx0[0] = jnp.where(even, high, low)
    tx0[1] = jnp.where(even, g_high, g_low)
    tx1[0] = jnp.where(even, low, high)
    tx1[1] = jnp.where(even, g_low, g_high)
    shape = (size_x, size_z)
    kept = inner(shape, 0) & inner(shape, 1)
    at = 2 * size_y + rows
    g_low = jnp.where(kept, local[at : at + size_x] * y_low[1], 0.0)
    g_high = jnp.where(kept, local[at + size_x : at + 2 * size_x] * y_high[1], 0.0)
    even = where_y[0]
    low, high = own_box[:, 0], own_box[:, size_y - 1]
    ty0[0] = jnp.where(even, high, low)
    ty0[1] = jnp.where(even, g_high, g_low)
    ty1[0] = jnp.where(even, low, high)
    ty1[1] = jnp.where(even, g_low, g_high)
    mine = lane_rows([own_flat], jnp.where(even_z, size_z - 1, 0))
    ids = iota((1, rows), 1)
    x_at, y_at = ids // size_y, ids % size_y
    kept = (x_at >= 1) & (x_at <= size_x - 2) & (y_at >= 1) & (y_at <= size_y - 2)
    ghost = jnp.where(kept, jnp.where(even_z, face[1:2], face[0:1]) * rz[1:2], 0.0)
    tz[...] = jnp.where(iota((8, rows), 0) == 1, jnp.broadcast_to(ghost, (8, rows)), mine)


def stencil(slabs, y_low, y_high, faces, links, box):
    size_x, size_y, size_z = box
    wx, wy, wy0, wz, wz0 = links
    row, lane = iota((size_y, size_z), 0), iota((size_y, size_z), 1)
    below = wx[0] * (slabs[1] - slabs[0])
    for i in range(size_x):
        value, face = slabs[i + 1], faces(i)
        above = wx[i + 1] * (slabs[i + 2] - value)
        total = below - above
        below = above
        flow = wy[i] * (jnp.where(row == size_y - 1, y_high[i : i + 1], pltpu.roll(value, size_y - 1, 0)) - value)
        first = wy0[i : i + 1] * (value - y_low[i : i + 1])
        total = total + (jnp.where(row == 0, first, pltpu.roll(flow, 1, 0)) - flow)
        flow = wz[i] * (jnp.where(lane == size_z - 1, face, pltpu.roll(value, size_z - 1, 1)) - value)
        first = wz0[i] * (value - face)
        yield i, total + (jnp.where(lane == 0, first, pltpu.roll(flow, 1, 1)) - flow)


def links_kernel(
    rz_prev, mask, d, mu, rx0, rx1, ry0, ry1, rz,
    ad_out, wx, wy, wy0, wz, wz0, dad, rz_line,
):
    box = mask.shape
    size_x, size_y, size_z = box
    where_x, where_y, where_z = (place(axis) for axis in AXES)
    x_near = sides(rx0[2:4], rx1[2:4], where_x)
    y_near = sides(ry0[2:4], ry1[2:4], where_y)
    d_face, mu_face = (
        wide.reshape(box) for wide in lane_ends([rz[2:3], rz[3:4]], where_z[0], size_z)
    )
    row, lane = iota((size_y, size_z), 0), iota((size_y, size_z), 1)
    slabs = [x_near[0][1]] + [mu[i] for i in range(size_x)] + [x_near[1][1]]
    wx[0] = 0.5 * (slabs[0] + slabs[1])
    mu_low, mu_high = y_near[0][1], y_near[1][1]
    for i in range(size_x):
        value, face = slabs[i + 1], mu_face[i]
        wx[i + 1] = 0.5 * (value + slabs[i + 2])
        wy[i] = 0.5 * (value + jnp.where(row == size_y - 1, mu_high[i : i + 1], pltpu.roll(value, size_y - 1, 0)))
        wy0[i : i + 1] = 0.5 * (value[0:1] + mu_low[i : i + 1])
        wz[i] = 0.5 * (value + jnp.where(lane == size_z - 1, face, pltpu.roll(value, size_z - 1, 1)))
        wz0[i] = 0.5 * (value + face)
    slabs = [x_near[0][0]] + [d[i] for i in range(size_x)] + [x_near[1][0]]
    total = jnp.zeros((size_y, size_z), F32)
    for i, image in stencil(slabs, y_near[0][0], y_near[1][0], lambda i: d_face[i], (wx, wy, wy0, wz, wz0), box):
        image = mask[i] * image
        ad_out[i] = image
        total = total + slabs[i + 1] * image
    dad[...] = jnp.sum(total, axis=0, keepdims=True)
    rz_line[...] = jnp.full(rz_line.shape, rz_prev[0])


def image_kernel(
    masked, mask, d, own, tx0, tx1, ty0, ty1, tz, qx0, qx1, qy0, qy1, qz, ad, wx, wy, wy0, wz, wz0, dad,
    z_out, az_out, sums,
):
    box = mask.shape
    size_x, size_y, size_z = box
    where_x, where_y, where_z = (place(axis) for axis in AXES)
    x_sent = sides(tx0[1], tx1[1], where_x)
    y_sent = sides(ty0[1], ty1[1], where_y)
    x_got = sides(qx0[...], qx1[...], where_x)
    y_got = sides(qy0[...], qy1[...], where_y)
    face, more = (
        wide.reshape(box) for wide in lane_ends([qz[0:1] + tz[1:2], qz[1:2]], where_z[0], size_z)
    )
    row = iota((size_y, size_z), 0)
    slabs = [x_got[0][0] + x_sent[0]]
    for i in range(size_x):
        value = own[i] + more[i]
        value = value + jnp.where(row == 0, y_got[0][1][i : i + 1], 0.0)
        value = value + jnp.where(row == size_y - 1, y_got[1][1][i : i + 1], 0.0)
        if i == 0:
            value = value + x_got[0][1]
        if i == size_x - 1:
            value = value + x_got[1][1]
        z_out[i] = value
        slabs.append(value)
    slabs.append(x_got[1][0] + x_sent[1])
    y_sides = [y_got[s][0] + y_sent[s] for s in (0, 1)]
    rz = zaz = zad = jnp.zeros((size_y, size_z), F32)
    for i, image in stencil(slabs, *y_sides, lambda i: face[i], (wx, wy, wy0, wz, wz0), box):
        value = slabs[i + 1]
        image = mask[i] * image
        az_out[i] = image
        rz = rz + masked[i] * value
        zaz = zaz + value * image
        zad = zad + (value * ad[i] + d[i] * image)
    at = iota(sums.shape, 2)
    line = jnp.zeros(sums.shape, F32)
    for k, part in enumerate((rz, zaz, zad, dad[...])):
        line = jnp.where(at == k, jnp.sum(part), line)
    sums[...] = line


def update_kernel(
    rz_line, sums, iterate, res, d, z, az, ad, new_iterate, new_res, new_direction, out_iterate, out_res, out_p, gone,
):
    line = jnp.sum(sums[...], axis=0)
    rz, zaz, zad, dad = (line[:, k : k + 1] for k in range(4))
    beta = rz / rz_line[:, 0:1]
    alpha = rz / (zaz + beta * (zad + beta * dad))
    alpha, beta = (v.reshape(1, 1, 1) for v in (alpha, beta))
    p = z[...] + beta * d[...]
    out_p[...] = p
    copies = [pltpu.make_async_copy(out_p, new_direction, gone.at[0])]
    copies[0].start()
    out_iterate[...] = iterate[...] + alpha * p
    copies.append(pltpu.make_async_copy(out_iterate, new_iterate, gone.at[1]))
    copies[1].start()
    out_res[...] = res[...] - alpha * (az[...] + beta * ad[...])
    copies.append(pltpu.make_async_copy(out_res, new_res, gone.at[2]))
    copies[2].start()
    for copy in copies:
        copy.wait()


def call(kernel, args, outs, specs=None, out_spec=VMEM, scratch=()):
    outs = [jax.ShapeDtypeStruct(out, F32) for out in outs]
    return pl.pallas_call(
        kernel,
        out_shape=outs,
        in_specs=specs or [VMEM] * len(args),
        out_specs=[out_spec] * len(outs),
        scratch_shapes=list(scratch),
        cost_estimate=pl.CostEstimate(flops=0, bytes_accessed=1 << 20, transcendentals=0),
        compiler_params=pltpu.CompilerParams(vmem_limit_bytes=32 * 1024 * 1024),
    )(*args)


def exchange(sx0, sx1, sy0, sy1, sz):
    return (
        swap(sx0, "gx", 0),
        swap(sx1, "gx", 1),
        swap(sy0, "gy", 0),
        swap(sy1, "gy", 1),
        swap(sz, "gz", 0),
    )


def shards(iterate, residual, direction, permeability, unfixed_node_mask, rz_prev):
    size_x, size_y, size_z = residual.shape
    box = residual.shape
    rows = size_x * size_y
    flat = (rows, size_z)
    devices = lax.axis_size(AXES)

    def faces(count):
        return [(count, size_y, size_z)] * 2 + [(count, size_x, size_z)] * 2 + [(8, rows)]

    fwd, middle, *tables = map(jnp.asarray, solve_tables(size_x, size_y, size_z).values())
    with jax.named_scope("masks"):
        masked = unfixed_node_mask.astype(F32) * residual
        mu = permeability
    with jax.named_scope("pack"):
        sent = call(pack_kernel, (masked, unfixed_node_mask, direction, mu), faces(4))
    with jax.named_scope("faces_in"):
        near = exchange(*sent)
    with jax.named_scope("own_part"):
        modes = ((size_x + 2) * middle.shape[0], LANES)
        args = (masked, unfixed_node_mask, direction, mu, fwd, middle)
        work, mask, d, *part = call(own_kernel, args, [(rows, LANES), box, box, modes, (8, size_z)])
    with jax.named_scope("solve"):
        own, *made = call(solve_kernel, (work, *part, mask, *near, fwd, *tables), [box] + faces(2))
    with jax.named_scope("faces_out"):
        got = exchange(*made)
    with jax.named_scope("links"):
        outs = [box, (size_x + 1, size_y, size_z), box, (size_x, size_z), box, box, (1, size_z), (1, size_z)]
        ad, *links, rz_line = call(links_kernel, (rz_prev, mask, d, mu, *near), outs, [SMEM] + [VMEM] * 8)
    with jax.named_scope("image"):
        z, az, sums = call(image_kernel, (masked, mask, d, own, *made, *got, ad, *links), [box, box, (devices, 1, 128)])
    with jax.named_scope("sums"):
        sums = lax.all_to_all(sums, AXES, 0, 0, tiled=True)
    with jax.named_scope("update"):
        args = (rz_line, sums, iterate, residual, d, z, az, ad)
        scratch = [pltpu.VMEM(box, F32)] * 3 + [pltpu.SemaphoreType.DMA((3,))]
        return tuple(call(update_kernel, args, [box] * 3, None, pl.BlockSpec(memory_space=pl.ANY), scratch))


def solution(mesh):
    in_specs = (P(*AXES),) * 5 + (P(),)
    out_specs = (P(*AXES),) * 3
    return jax.shard_map(shards, mesh=mesh, in_specs=in_specs, out_specs=out_specs, check_vma=False)
```

```python
import functools

import jax
import jax.numpy as jnp
import ml_dtypes
import numpy as np
from jax import lax
from jax.experimental import pallas as pl
from jax.experimental.pallas import tpu as pltpu
from jax.sharding import PartitionSpec as P

AXES = ("gx", "gy", "gz")
F32 = jnp.float32
BF16 = jnp.bfloat16
HIGHEST = lax.Precision.HIGHEST
VMEM = pl.BlockSpec(memory_space=pltpu.VMEM)
SMEM = pl.BlockSpec(memory_space=pltpu.SMEM)
LANES = 256
GROUP = 6
FOUR = 4


def swaps(axis, turn):
    counts = [lax.axis_size(name) for name in AXES]
    dim = AXES.index(axis)
    pairs = []
    for source in np.ndindex(*counts):
        target = list(source)
        step = 1 if (source[dim] + turn) % 2 == 0 else -1
        if axis == "gy" and not 0 <= source[dim] + step < counts[dim]:
            target[0] ^= 1
        else:
            target[dim] = (source[dim] + step) % counts[dim]
        pairs.append(tuple(int(np.ravel_multi_index(where, counts)) for where in (source, target)))
    return pairs


def swap(block, axis, turn):
    return lax.ppermute(block, AXES, swaps(axis, turn))


def place(axis):
    index = lax.axis_index(axis)
    return index % 2 == 0, index > 0, index < lax.axis_size(axis) - 1


def sides(turn0, turn1, where):
    even, below, above = where
    low = jnp.where(below, jnp.where(even, turn1, turn0), 0.0)
    high = jnp.where(above, jnp.where(even, turn0, turn1), 0.0)
    return low, high


def halves(value):
    high = value.astype(BF16)
    return high, (value - high.astype(F32)).astype(BF16)


def dot(a, b):
    return lax.dot_general(a, b, (((1,), (0,)), ((), ())), preferred_element_type=F32)


def dot_rows(a, b):
    return lax.dot_general(a, b, (((0,), (0,)), ((), ())), preferred_element_type=F32)


def dot_lanes(a, b):
    return lax.dot_general(a, b, (((1,), (1,)), ((), ())), preferred_element_type=F32)


def iota(shape, dim):
    return lax.broadcasted_iota(jnp.int32, shape, dim)


def basis(n):
    idx = np.arange(n, dtype=np.float64) + 1.0
    values = 2.0 - 2.0 * np.cos(np.pi * idx / (n + 1))
    return np.sqrt(2.0 / (n + 1)) * np.sin(np.pi * idx[:, None] * idx[None, :] / (n + 1)), values


def np_halves(table):
    high = table.astype(np.float32).astype(ml_dtypes.bfloat16)
    return high, (table - high.astype(np.float64)).astype(np.float32).astype(ml_dtypes.bfloat16)


@functools.cache
def solve_tables(size_x, size_y, size_z):
    nx, ny, nz = size_x + 2, size_y + 2, size_z + 2
    qy, ly = basis(ny)
    qz, lz = basis(nz)
    pad = -(-ny // 8) * 8
    forward = np.zeros((size_z, LANES))
    forward[:, :nz] = qz[1:-1]
    ends = np.zeros((2, LANES))
    ends[:, :nz] = qz[[0, -1]]
    fh, fl = np_halves(forward)
    eh, el = np_halves(ends)
    out_ends = np.zeros((32, LANES), ml_dtypes.bfloat16)
    out_ends[0:2], out_ends[16:18] = eh, el
    into = np.zeros((FOUR * pad, FOUR * size_y))
    for s in range(FOUR):
        into[s * pad : s * pad + ny, s * size_y : (s + 1) * size_y] = qy[1:-1].T
    ih, il = np_halves(into)
    one = np.zeros((-(-pad // 16) * 16, FOUR * size_y), ml_dtypes.bfloat16)
    for k, half in enumerate((ih, il, ih)):
        one[:pad, k * size_y : (k + 1) * size_y] = half[:pad, :size_y]
    row_ends = np.zeros((8, LANES))
    row_ends[:2] = ends
    rim = np.zeros((pad, LANES // 2))
    rim[:ny, 0], rim[:ny, 1] = qy[0], qy[-1]
    back = np.zeros((GROUP * size_y, LANES))
    for s in range(GROUP):
        back[s * size_y : (s + 1) * size_y, s * pad : s * pad + ny] = qy[1:-1]
    middle = np.full((pad, LANES), 2.0)
    middle[:ny, :nz] += ly[:, None] + lz[None, :]
    middle[ny:], middle[:, nz:] = 4.0, 4.0
    bh, bl = np_halves(back)
    return dict(
        fwd=np.concatenate([fh, fl]),
        middle=middle.astype(np.float32),
        into=np.concatenate([ih, il], axis=1),
        one=one,
        row_ends=row_ends.astype(np.float32),
        back=np.concatenate([bh, bl]),
        rim=rim.astype(np.float32),
        out=np.concatenate([np.ascontiguousarray(fh.T), np.ascontiguousarray(fl.T)], axis=1),
        out_ends=out_ends,
    )


def lane_rows(fields, lane):
    depth = fields[0].shape[1]
    total = None
    for f, field in enumerate(fields):
        at = iota((16, 2 * depth), 1)
        pick = jnp.where((iota((16, 2 * depth), 0) == f) & ((at == lane) | (at == lane + depth)), 1.0, 0.0).astype(BF16)
        rows = dot_lanes(pick, jnp.concatenate(halves(field), axis=1))
        total = rows if total is None else total + rows
    return total[:8]


def lane_ends(lines, even, depth):
    count = len(lines)
    pieces = []
    for line in lines:
        pieces += halves(line)
    size = lines[0].shape[1]
    stack = jnp.zeros((16, size), F32)
    for k, piece in enumerate(pieces):
        stack = jnp.where(iota((16, size), 0) == k, piece.astype(F32), stack)
    shape = (16, count * depth)
    lane = jnp.where(even, depth - 1, 0) + iota(shape, 0) // 2 * depth
    pick = jnp.where((iota(shape, 0) < 2 * count) & (iota(shape, 1) == lane), 1.0, 0.0).astype(BF16)
    wide = dot_rows(stack.astype(BF16), pick)
    return [wide[:, k * depth : (k + 1) * depth] for k in range(count)]


def pack_kernel(masked, msk, direction, mu, sx0, sx1, sy0, sy1, sz):
    size_x, size_y, size_z = masked.shape
    even_x, even_y, even_z = (place(axis)[0] for axis in AXES)

    def fields(where):
        mask = msk[where].astype(F32)
        return masked[where], mask, mask * direction[where], mu[where]

    for f, (low, high) in enumerate(zip(fields(0), fields(size_x - 1))):
        sx0[f] = jnp.where(even_x, high, low)
        sx1[f] = jnp.where(even_x, low, high)
    every = slice(None)
    for f, (low, high) in enumerate(zip(fields((every, 0)), fields((every, size_y - 1)))):
        sy0[f] = jnp.where(even_y, high, low)
        sy1[f] = jnp.where(even_y, low, high)
    flat = [field.reshape(size_x * size_y, size_z) for field in fields(every)]
    sz[...] = lane_rows(flat, jnp.where(even_z, size_z - 1, 0))


def along_z(rows, fwd, size_z):
    high, low = halves(rows)
    both = jnp.concatenate([high, low], axis=1)
    table = jnp.concatenate([fwd[:size_z], fwd[:size_z]], axis=0)
    half = rows.shape[0] // 32 * 16
    parts = [dot(both[part], table) + dot(high[part], fwd[size_z:]) for part in (slice(0, half), slice(half, None))]
    return jnp.concatenate(parts, axis=0)


def own_kernel(masked, msk, direction, mu, middle, into, modes, mask, d, factors, scale):
    size_x, size_y, size_z = masked.shape
    mask[...] = msk[...].astype(F32)
    d[...] = mask[...] * direction[...]
    pad, depth = middle.shape[0], FOUR * size_y
    high, low = halves(masked[...].reshape(size_x * size_y, size_z))
    table = jnp.concatenate([into[...], into[:, :depth]], axis=1)
    for g in range(0, size_x // FOUR, 2):
        pair = []
        for part in (slice(g * depth, (g + 1) * depth), slice((g + 1) * depth, (g + 2) * depth)):
            pair.append(jnp.concatenate([high[part], high[part], low[part]], axis=0))
        value = dot(table, jnp.concatenate(pair, axis=1))
        modes[g * FOUR * pad : (g + 1) * FOUR * pad] = value[:, :size_z]
        modes[(g + 1) * FOUR * pad : (g + 2) * FOUR * pad] = value[:, size_z:]
    along = middle[...]
    previous = 1.0 / along
    factors[0:pad] = previous
    for i in range(1, size_x + 2):
        previous = 1.0 / (along - previous)
        factors[i * pad : (i + 1) * pad] = previous
    scale[...] = jnp.full((8, size_z), (size_x * size_y * size_z) / jnp.sum(mu[...]))


def solve_kernel(
    modes, factors, scale, mask, rx0, rx1, ry0, ry1, rz, fwd, into, one, row_ends, back, rim, out, out_ends,
    own, tx0, tx1, ty0, ty1, tz,
):
    size_x, size_y, size_z = mask.shape
    rows = size_x * size_y
    pad = rim.shape[0]
    nx = size_x + 2
    where_x, where_y, where_z = (place(axis) for axis in AXES)
    even_z = where_z[0]
    x_low, x_high = sides(rx0[0:2], rx1[0:2], where_x)
    y_low, y_high = sides(ry0[0:2], ry1[0:2], where_y)
    depth, count = FOUR * size_y, size_x // FOUR
    line_h, line_l = halves(rz[0:1])
    at = iota((16, depth), 0)
    lines = jnp.zeros((16, depth), F32)
    for g in range(count):
        part = slice(g * depth, (g + 1) * depth)
        lines = jnp.where(at == g, line_h[:, part].astype(F32), lines)
        lines = jnp.where(at == count + g, line_l[:, part].astype(F32), lines)
    lines = lines.astype(BF16)
    face_h, face_l = dot_lanes(into[:, :depth], lines), dot_lanes(into[:, depth:], lines)
    face = face_h[:, :count] + face_h[:, count : 2 * count] + face_l[:, :count]
    end = jnp.where(even_z, row_ends[1:2], row_ends[0:1])
    side_h, side_l = halves(jnp.concatenate([x_low[0], x_high[0]], axis=1))
    rest = jnp.zeros((one.shape[1] - 3 * size_y, 2 * size_z), BF16)
    ghosts = dot(one[...], jnp.concatenate([side_h, side_h, side_l, rest], axis=0))
    rim_low, rim_high = (jnp.broadcast_to(rim[:, k : k + 1], (pad, size_z)) for k in (0, 1))
    slabs = [ghosts[:pad, :size_z]]
    for i in range(size_x):
        value = modes[i * pad : (i + 1) * pad]
        slabs.append(value + rim_low * y_low[0][i : i + 1] + rim_high * y_high[0][i : i + 1])
    slabs.append(ghosts[:pad, size_z:])
    values = along_z(jnp.concatenate(slabs, axis=0), fwd, size_z)
    solved = []
    for i in range(nx):
        value = values[i * pad : (i + 1) * pad]
        if 0 < i < nx - 1:
            g, k = divmod(i - 1, FOUR)
            value = value + face[k * pad : (k + 1) * pad, g : g + 1] * end
        if i:
            value = value + solved[-1]
        solved.append(value * factors[i * pad : (i + 1) * pad])
    for i in reversed(range(nx - 1)):
        solved[i] = solved[i] + factors[i * pad : (i + 1) * pad] * solved[i + 1]
    rim_low, rim_high = (jnp.broadcast_to(rim[:, k : k + 1], (pad, LANES)) for k in (0, 1))
    solved = jnp.concatenate(solved, axis=0)
    high, low = halves(solved)
    rest = jnp.zeros((LANES - GROUP * pad, LANES), BF16)
    high, low = (jnp.concatenate([half, rest], axis=0) for half in (high, low))
    own_rows = GROUP * size_y
    back_all = jnp.concatenate([back[:own_rows], back[own_rows:], back[:own_rows]], axis=1)
    local = []
    for g in range(nx // GROUP):
        part = slice(g * GROUP * pad, g * GROUP * pad + LANES)
        local.append(dot(back_all, jnp.concatenate([high[part], high[part], low[part]], axis=0)))
    own_modes = solved[pad : (nx - 1) * pad].reshape(size_x, pad, LANES)
    local += [jnp.sum(own_modes * rim_low[None], axis=1), jnp.sum(own_modes * rim_high[None], axis=1)]
    local = jnp.concatenate(local, axis=0)
    local = local * scale[0:1, 0:1]
    high, low = halves(local)
    half = high.shape[0] // 32 * 16
    parts = []
    for part in (slice(0, half), slice(half, None)):
        both = dot(high[part], out[...])
        parts.append(both[:, :size_z] + both[:, size_z:] + dot(low[part], out[:, :size_z]))
    local = jnp.concatenate(parts, axis=0)
    own_h, own_l = high[size_y : size_y + rows], low[size_y : size_y + rows]
    face = dot_lanes(out_ends[0:16], own_h) + dot_lanes(out_ends[0:16], own_l) + dot_lanes(out_ends[16:32], own_h)

    def inner(shape, dim):
        at = iota(shape, dim)
        return (at >= 1) & (at <= shape[dim] - 2)

    own_flat = mask[...].reshape(rows, size_z) * local[size_y : size_y + rows]
    own_box = own_flat.reshape(size_x, size_y, size_z)
    own[...] = own_box
    shape = (size_y, size_z)
    kept = inner(shape, 0) & inner(shape, 1)
    g_low = jnp.where(kept, local[:size_y] * x_low[1], 0.0)
    g_high = jnp.where(kept, local[size_y + rows : 2 * size_y + rows] * x_high[1], 0.0)
    even = where_x[0]
    low, high = own_box[0], own_box[size_x - 1]
    tx0[0] = jnp.where(even, high, low)
    tx0[1] = jnp.where(even, g_high, g_low)
    tx1[0] = jnp.where(even, low, high)
    tx1[1] = jnp.where(even, g_low, g_high)
    shape = (size_x, size_z)
    kept = inner(shape, 0) & inner(shape, 1)
    at = 2 * size_y + rows
    g_low = jnp.where(kept, local[at : at + size_x] * y_low[1], 0.0)
    g_high = jnp.where(kept, local[at + size_x : at + 2 * size_x] * y_high[1], 0.0)
    even = where_y[0]
    low, high = own_box[:, 0], own_box[:, size_y - 1]
    ty0[0] = jnp.where(even, high, low)
    ty0[1] = jnp.where(even, g_high, g_low)
    ty1[0] = jnp.where(even, low, high)
    ty1[1] = jnp.where(even, g_low, g_high)
    mine = lane_rows([own_flat], jnp.where(even_z, size_z - 1, 0))
    ids = iota((1, rows), 1)
    x_at, y_at = ids // size_y, ids % size_y
    kept = (x_at >= 1) & (x_at <= size_x - 2) & (y_at >= 1) & (y_at <= size_y - 2)
    ghost = jnp.where(kept, jnp.where(even_z, face[1:2], face[0:1]) * rz[1:2], 0.0)
    for unused in (tx1, ty0, ty1):
        unused[2:] = jnp.zeros((unused.shape[0] - 2, *unused.shape[1:]), F32)
    tz[8:] = jnp.zeros((tz.shape[0] - 8, rows), F32)
    tz[0:8] = jnp.where(iota((8, rows), 0) == 1, jnp.broadcast_to(ghost, (8, rows)), mine)


def stencil(slabs, y_low, y_high, faces, links, box):
    size_x, size_y, size_z = box
    wx, wy, wy0, wz, wz0 = links
    row, lane = iota((size_y, size_z), 0), iota((size_y, size_z), 1)
    below = wx[0] * (slabs[1] - slabs[0])
    for i in range(size_x):
        value, face = slabs[i + 1], faces(i)
        above = wx[i + 1] * (slabs[i + 2] - value)
        total = below - above
        below = above
        flow = wy[i] * (jnp.where(row == size_y - 1, y_high[i : i + 1], pltpu.roll(value, size_y - 1, 0)) - value)
        first = wy0[i : i + 1] * (value - y_low[i : i + 1])
        total = total + (jnp.where(row == 0, first, pltpu.roll(flow, 1, 0)) - flow)
        flow = wz[i] * (jnp.where(lane == size_z - 1, face, pltpu.roll(value, size_z - 1, 1)) - value)
        first = wz0[i] * (value - face)
        yield i, total + (jnp.where(lane == 0, first, pltpu.roll(flow, 1, 1)) - flow)


def links_kernel(
    rz_prev, mask, d, mu, rx0, rx1, ry0, ry1, rz,
    ad_out, wx, wy, wy0, wz, wz0, dad, rz_line,
):
    box = mask.shape
    size_x, size_y, size_z = box
    where_x, where_y, where_z = (place(axis) for axis in AXES)
    x_near = sides(rx0[2:4], rx1[2:4], where_x)
    y_near = sides(ry0[2:4], ry1[2:4], where_y)
    d_face, mu_face = (
        wide.reshape(box) for wide in lane_ends([rz[2:3], rz[3:4]], where_z[0], size_z)
    )
    row, lane = iota((size_y, size_z), 0), iota((size_y, size_z), 1)
    slabs = [x_near[0][1]] + [mu[i] for i in range(size_x)] + [x_near[1][1]]
    wx[0] = 0.5 * (slabs[0] + slabs[1])
    mu_low, mu_high = y_near[0][1], y_near[1][1]
    for i in range(size_x):
        value, face = slabs[i + 1], mu_face[i]
        wx[i + 1] = 0.5 * (value + slabs[i + 2])
        wy[i] = 0.5 * (value + jnp.where(row == size_y - 1, mu_high[i : i + 1], pltpu.roll(value, size_y - 1, 0)))
        wy0[i : i + 1] = 0.5 * (value[0:1] + mu_low[i : i + 1])
        wz[i] = 0.5 * (value + jnp.where(lane == size_z - 1, face, pltpu.roll(value, size_z - 1, 1)))
        wz0[i] = 0.5 * (value + face)
    slabs = [x_near[0][0]] + [d[i] for i in range(size_x)] + [x_near[1][0]]
    total = jnp.zeros((size_y, size_z), F32)
    for i, image in stencil(slabs, y_near[0][0], y_near[1][0], lambda i: d_face[i], (wx, wy, wy0, wz, wz0), box):
        image = mask[i] * image
        ad_out[i] = image
        total = total + slabs[i + 1] * image
    dad[...] = jnp.sum(total, axis=0, keepdims=True)
    rz_line[...] = jnp.full(rz_line.shape, rz_prev[0])


def image_kernel(
    masked, mask, d, own, tx0, tx1, ty0, ty1, tz, qx0, qx1, qy0, qy1, qz, ad, wx, wy, wy0, wz, wz0, dad,
    z_out, az_out, sums,
):
    box = mask.shape
    size_x, size_y, size_z = box
    where_x, where_y, where_z = (place(axis) for axis in AXES)
    x_sent = sides(tx0[1], tx1[1], where_x)
    y_sent = sides(ty0[1], ty1[1], where_y)
    x_got = sides(qx0[0:2], qx1[0:2], where_x)
    y_got = sides(qy0[0:2], qy1[0:2], where_y)
    face, more = (
        wide.reshape(box) for wide in lane_ends([qz[0:1] + tz[1:2], qz[1:2]], where_z[0], size_z)
    )
    row = iota((size_y, size_z), 0)
    slabs = [x_got[0][0] + x_sent[0]]
    for i in range(size_x):
        value = own[i] + more[i]
        value = value + jnp.where(row == 0, y_got[0][1][i : i + 1], 0.0)
        value = value + jnp.where(row == size_y - 1, y_got[1][1][i : i + 1], 0.0)
        if i == 0:
            value = value + x_got[0][1]
        if i == size_x - 1:
            value = value + x_got[1][1]
        z_out[i] = value
        slabs.append(value)
    slabs.append(x_got[1][0] + x_sent[1])
    y_sides = [y_got[s][0] + y_sent[s] for s in (0, 1)]
    rz = zaz = zad = jnp.zeros((size_y, size_z), F32)
    for i, image in stencil(slabs, *y_sides, lambda i: face[i], (wx, wy, wy0, wz, wz0), box):
        value = slabs[i + 1]
        image = mask[i] * image
        az_out[i] = image
        rz = rz + masked[i] * value
        zaz = zaz + value * image
        zad = zad + (value * ad[i] + d[i] * image)
    at = iota(sums.shape, 2)
    line = jnp.zeros(sums.shape, F32)
    for k, part in enumerate((rz, zaz, zad, dad[...])):
        line = jnp.where(at == k, jnp.sum(part), line)
    sums[...] = line


def update_kernel(
    rz_line, sums, iterate, res, d, z, az, ad, new_iterate, new_res, new_direction, out_iterate, out_res, out_p, gone,
):
    line = jnp.sum(sums[...], axis=0)
    rz, zaz, zad, dad = (line[:, k : k + 1] for k in range(4))
    beta = rz / rz_line[:, 0:1]
    alpha = rz / (zaz + beta * (zad + beta * dad))
    alpha, beta = (v.reshape(1, 1, 1) for v in (alpha, beta))
    p = z[...] + beta * d[...]
    out_p[...] = p
    copies = [pltpu.make_async_copy(out_p, new_direction, gone.at[0])]
    copies[0].start()
    out_iterate[...] = iterate[...] + alpha * p
    copies.append(pltpu.make_async_copy(out_iterate, new_iterate, gone.at[1]))
    copies[1].start()
    out_res[...] = res[...] - alpha * (az[...] + beta * ad[...])
    copies.append(pltpu.make_async_copy(out_res, new_res, gone.at[2]))
    copies[2].start()
    for copy in copies:
        copy.wait()


def call(kernel, args, outs, specs=None, out_spec=VMEM, scratch=()):
    outs = [jax.ShapeDtypeStruct(out, F32) for out in outs]
    return pl.pallas_call(
        kernel,
        out_shape=outs,
        in_specs=specs or [VMEM] * len(args),
        out_specs=[out_spec] * len(outs),
        scratch_shapes=list(scratch),
        cost_estimate=pl.CostEstimate(flops=0, bytes_accessed=1 << 20, transcendentals=0),
        compiler_params=pltpu.CompilerParams(vmem_limit_bytes=32 * 1024 * 1024),
    )(*args)


def exchange(sx0, sx1, sy0, sy1, sz):
    return (
        swap(sx0, "gx", 0),
        swap(sx1, "gx", 1),
        swap(sy0, "gy", 0),
        swap(sy1, "gy", 1),
        swap(sz, "gz", 0),
    )


def shards(iterate, residual, direction, permeability, unfixed_node_mask, rz_prev):
    size_x, size_y, size_z = residual.shape
    box = residual.shape
    rows = size_x * size_y
    flat = (rows, size_z)
    devices = lax.axis_size(AXES)

    def faces(count):
        return [(count, size_y, size_z)] * 2 + [(count, size_x, size_z)] * 2 + [(8, rows)]

    layer = size_y * size_z
    made_faces = [(2, size_y, size_z), (3, size_y, size_z)]
    made_faces += [(3 * size_y // size_x, size_x, size_z)] * 2 + [(3 * layer // rows, rows)]

    fwd, middle, into, *tables = map(jnp.asarray, solve_tables(size_x, size_y, size_z).values())
    with jax.named_scope("masks"):
        masked = unfixed_node_mask.astype(F32) * residual
        mu = permeability
    with jax.named_scope("pack"):
        sent = call(pack_kernel, (masked, unfixed_node_mask, direction, mu), faces(4))
    with jax.named_scope("faces_in"):
        near = exchange(*sent)
    with jax.named_scope("own_part"):
        pad = middle.shape[0]
        args = (masked, unfixed_node_mask, direction, mu, middle, into)
        outs = [(size_x * pad, size_z), box, box, ((size_x + 2) * pad, LANES), (8, size_z)]
        modes, mask, d, *part = call(own_kernel, args, outs)
    with jax.named_scope("solve"):
        own, *made = call(solve_kernel, (modes, *part, mask, *near, fwd, into, *tables), [box] + made_faces)
    with jax.named_scope("faces_out"):
        got = exchange(*made)
    with jax.named_scope("links"):
        outs = [box, (size_x + 1, size_y, size_z), box, (size_x, size_z), box, box, (1, size_z), (1, size_z)]
        ad, *links, rz_line = call(links_kernel, (rz_prev, mask, d, mu, *near), outs, [SMEM] + [VMEM] * 8)
    with jax.named_scope("image"):
        z, az, sums = call(image_kernel, (masked, mask, d, own, *made, *got, ad, *links), [box, box, (devices, 1, 128)])
    with jax.named_scope("sums"):
        sums = lax.all_to_all(sums, AXES, 0, 0, tiled=True)
    with jax.named_scope("update"):
        args = (rz_line, sums, iterate, residual, d, z, az, ad)
        scratch = [pltpu.VMEM(box, F32)] * 3 + [pltpu.SemaphoreType.DMA((3,))]
        return tuple(call(update_kernel, args, [box] * 3, None, pl.BlockSpec(memory_space=pl.ANY), scratch))


def solution(mesh):
    in_specs = (P(*AXES),) * 5 + (P(),)
    out_specs = (P(*AXES),) * 3
    return jax.shard_map(shards, mesh=mesh, in_specs=in_specs, out_specs=out_specs, check_vma=False)
```

```python
import functools

import jax
import jax.numpy as jnp
import ml_dtypes
import numpy as np
from jax import lax
from jax.experimental import pallas as pl
from jax.experimental.pallas import tpu as pltpu
from jax.sharding import PartitionSpec as P

AXES = ("gx", "gy", "gz")
F32 = jnp.float32
BF16 = jnp.bfloat16
HIGHEST = lax.Precision.HIGHEST
VMEM = pl.BlockSpec(memory_space=pltpu.VMEM)
SMEM = pl.BlockSpec(memory_space=pltpu.SMEM)
LANES = 256
GROUP = 6
FOUR = 4
FILL = {"gx": 2, "gy": 0}


def swaps(axis, turn):
    counts = [lax.axis_size(name) for name in AXES]
    dim = AXES.index(axis)
    pairs = []
    for source in np.ndindex(*counts):
        target = list(source)
        step = 1 if (source[dim] + turn) % 2 == 0 else -1
        if not 0 <= source[dim] + step < counts[dim] and axis in FILL:
            target[FILL[axis]] ^= 1
        else:
            target[dim] = (source[dim] + step) % counts[dim]
        pairs.append(tuple(int(np.ravel_multi_index(where, counts)) for where in (source, target)))
    return pairs


def swap(block, axis, turn):
    return lax.ppermute(block, AXES, swaps(axis, turn))


def place(axis):
    index = lax.axis_index(axis)
    return index % 2 == 0, index > 0, index < lax.axis_size(axis) - 1


def sides(turn0, turn1, where):
    even, below, above = where
    low = jnp.where(below, jnp.where(even, turn1, turn0), 0.0)
    high = jnp.where(above, jnp.where(even, turn0, turn1), 0.0)
    return low, high


def halves(value):
    high = value.astype(BF16)
    return high, (value - high.astype(F32)).astype(BF16)


def dot(a, b):
    return lax.dot_general(a, b, (((1,), (0,)), ((), ())), preferred_element_type=F32)


def dot_rows(a, b):
    return lax.dot_general(a, b, (((0,), (0,)), ((), ())), preferred_element_type=F32)


def dot_lanes(a, b):
    return lax.dot_general(a, b, (((1,), (1,)), ((), ())), preferred_element_type=F32)


def iota(shape, dim):
    return lax.broadcasted_iota(jnp.int32, shape, dim)


def basis(n):
    idx = np.arange(n, dtype=np.float64) + 1.0
    values = 2.0 - 2.0 * np.cos(np.pi * idx / (n + 1))
    return np.sqrt(2.0 / (n + 1)) * np.sin(np.pi * idx[:, None] * idx[None, :] / (n + 1)), values


def np_halves(table):
    high = table.astype(np.float32).astype(ml_dtypes.bfloat16)
    return high, (table - high.astype(np.float64)).astype(np.float32).astype(ml_dtypes.bfloat16)


@functools.cache
def solve_tables(size_x, size_y, size_z):
    nx, ny, nz = size_x + 2, size_y + 2, size_z + 2
    qy, ly = basis(ny)
    qz, lz = basis(nz)
    pad = -(-ny // 8) * 8
    forward = np.zeros((size_z, LANES))
    forward[:, :nz] = qz[1:-1]
    ends = np.zeros((2, LANES))
    ends[:, :nz] = qz[[0, -1]]
    fh, fl = np_halves(forward)
    eh, el = np_halves(ends)
    out_ends = np.zeros((32, LANES), ml_dtypes.bfloat16)
    out_ends[0:2], out_ends[16:18] = eh, el
    into = np.zeros((FOUR * pad, FOUR * size_y))
    for s in range(FOUR):
        into[s * pad : s * pad + ny, s * size_y : (s + 1) * size_y] = qy[1:-1].T
    ih, il = np_halves(into)
    one = np.zeros((-(-pad // 16) * 16, FOUR * size_y), ml_dtypes.bfloat16)
    for k, half in enumerate((ih, il, ih)):
        one[:pad, k * size_y : (k + 1) * size_y] = half[:pad, :size_y]
    row_ends = np.zeros((8, LANES))
    row_ends[:2] = ends
    rim = np.zeros((pad, LANES // 2))
    rim[:ny, 0], rim[:ny, 1] = qy[0], qy[-1]
    back = np.zeros((GROUP * size_y, LANES))
    for s in range(GROUP):
        back[s * size_y : (s + 1) * size_y, s * pad : s * pad + ny] = qy[1:-1]
    middle = np.full((pad, LANES), 2.0)
    middle[:ny, :nz] += ly[:, None] + lz[None, :]
    middle[ny:], middle[:, nz:] = 4.0, 4.0
    bh, bl = np_halves(back)
    return dict(
        fwd=np.concatenate([fh, fl]),
        middle=middle.astype(np.float32),
        into=np.concatenate([ih, il], axis=1),
        one=one,
        row_ends=row_ends.astype(np.float32),
        back=np.concatenate([bh, bl]),
        rim=rim.astype(np.float32),
        out=np.concatenate([np.ascontiguousarray(fh.T), np.ascontiguousarray(fl.T)], axis=1),
        out_ends=out_ends,
    )


def lane_rows(fields, lane):
    depth = fields[0].shape[1]
    total = None
    for f, field in enumerate(fields):
        at = iota((16, 2 * depth), 1)
        pick = jnp.where((iota((16, 2 * depth), 0) == f) & ((at == lane) | (at == lane + depth)), 1.0, 0.0).astype(BF16)
        rows = dot_lanes(pick, jnp.concatenate(halves(field), axis=1))
        total = rows if total is None else total + rows
    return total[:8]


def lane_ends(lines, even, depth):
    count = len(lines)
    pieces = []
    for line in lines:
        pieces += halves(line)
    size = lines[0].shape[1]
    stack = jnp.zeros((16, size), F32)
    for k, piece in enumerate(pieces):
        stack = jnp.where(iota((16, size), 0) == k, piece.astype(F32), stack)
    shape = (16, count * depth)
    lane = jnp.where(even, depth - 1, 0) + iota(shape, 0) // 2 * depth
    pick = jnp.where((iota(shape, 0) < 2 * count) & (iota(shape, 1) == lane), 1.0, 0.0).astype(BF16)
    wide = dot_rows(stack.astype(BF16), pick)
    return [wide[:, k * depth : (k + 1) * depth] for k in range(count)]


def pack_kernel(masked, msk, direction, mu, sx0, sx1, sy0, sy1, sz):
    size_x, size_y, size_z = masked.shape
    even_x, even_y, even_z = (place(axis)[0] for axis in AXES)

    def fields(where):
        mask = msk[where].astype(F32)
        return masked[where], mask, mask * direction[where], mu[where]

    for f, (low, high) in enumerate(zip(fields(0), fields(size_x - 1))):
        sx0[f] = jnp.where(even_x, high, low)
        sx1[f] = jnp.where(even_x, low, high)
    every = slice(None)
    for f, (low, high) in enumerate(zip(fields((every, 0)), fields((every, size_y - 1)))):
        sy0[f] = jnp.where(even_y, high, low)
        sy1[f] = jnp.where(even_y, low, high)
    flat = [field.reshape(size_x * size_y, size_z) for field in fields(every)]
    sz[...] = lane_rows(flat, jnp.where(even_z, size_z - 1, 0))


def along_z(rows, fwd, size_z):
    high, low = halves(rows)
    both = jnp.concatenate([high, low], axis=1)
    table = jnp.concatenate([fwd[:size_z], fwd[:size_z]], axis=0)
    half = rows.shape[0] // 32 * 16
    parts = [dot(both[part], table) + dot(high[part], fwd[size_z:]) for part in (slice(0, half), slice(half, None))]
    return jnp.concatenate(parts, axis=0)


def own_kernel(masked, msk, direction, mu, middle, into, modes, mask, d, factors, scale):
    size_x, size_y, size_z = masked.shape
    mask[...] = msk[...].astype(F32)
    d[...] = mask[...] * direction[...]
    pad, depth = middle.shape[0], FOUR * size_y
    high, low = halves(masked[...].reshape(size_x * size_y, size_z))
    table = jnp.concatenate([into[...], into[:, :depth]], axis=1)
    for g in range(0, size_x // FOUR, 2):
        pair = []
        for part in (slice(g * depth, (g + 1) * depth), slice((g + 1) * depth, (g + 2) * depth)):
            pair.append(jnp.concatenate([high[part], high[part], low[part]], axis=0))
        value = dot(table, jnp.concatenate(pair, axis=1))
        modes[g * FOUR * pad : (g + 1) * FOUR * pad] = value[:, :size_z]
        modes[(g + 1) * FOUR * pad : (g + 2) * FOUR * pad] = value[:, size_z:]
    along = middle[...]
    previous = 1.0 / along
    factors[0:pad] = previous
    for i in range(1, size_x + 2):
        previous = 1.0 / (along - previous)
        factors[i * pad : (i + 1) * pad] = previous
    scale[...] = jnp.full((8, size_z), (size_x * size_y * size_z) / jnp.sum(mu[...]))


def solve_kernel(
    modes, factors, scale, mask, rx0, rx1, ry0, ry1, rz, fwd, into, one, row_ends, back, rim, out, out_ends,
    own, tx0, tx1, ty0, ty1, tz,
):
    size_x, size_y, size_z = mask.shape
    rows = size_x * size_y
    pad = rim.shape[0]
    nx = size_x + 2
    where_x, where_y, where_z = (place(axis) for axis in AXES)
    even_z = where_z[0]
    x_low, x_high = sides(rx0[0:2], rx1[0:2], where_x)
    y_low, y_high = sides(ry0[0:2], ry1[0:2], where_y)
    depth, count = FOUR * size_y, size_x // FOUR
    line_h, line_l = halves(rz[0:1])
    at = iota((16, depth), 0)
    lines = jnp.zeros((16, depth), F32)
    for g in range(count):
        part = slice(g * depth, (g + 1) * depth)
        lines = jnp.where(at == g, line_h[:, part].astype(F32), lines)
        lines = jnp.where(at == count + g, line_l[:, part].astype(F32), lines)
    lines = lines.astype(BF16)
    face_h, face_l = dot_lanes(into[:, :depth], lines), dot_lanes(into[:, depth:], lines)
    face = face_h[:, :count] + face_h[:, count : 2 * count] + face_l[:, :count]
    end = jnp.where(even_z, row_ends[1:2], row_ends[0:1])
    side_h, side_l = halves(jnp.concatenate([x_low[0], x_high[0]], axis=1))
    rest = jnp.zeros((one.shape[1] - 3 * size_y, 2 * size_z), BF16)
    ghosts = dot(one[...], jnp.concatenate([side_h, side_h, side_l, rest], axis=0))
    rim_low, rim_high = (jnp.broadcast_to(rim[:, k : k + 1], (pad, size_z)) for k in (0, 1))
    slabs = [ghosts[:pad, :size_z]]
    for i in range(size_x):
        value = modes[i * pad : (i + 1) * pad]
        slabs.append(value + rim_low * y_low[0][i : i + 1] + rim_high * y_high[0][i : i + 1])
    slabs.append(ghosts[:pad, size_z:])
    values = along_z(jnp.concatenate(slabs, axis=0), fwd, size_z)
    solved = []
    for i in range(nx):
        value = values[i * pad : (i + 1) * pad]
        if 0 < i < nx - 1:
            g, k = divmod(i - 1, FOUR)
            value = value + face[k * pad : (k + 1) * pad, g : g + 1] * end
        if i:
            value = value + solved[-1]
        solved.append(value * factors[i * pad : (i + 1) * pad])
    for i in reversed(range(nx - 1)):
        solved[i] = solved[i] + factors[i * pad : (i + 1) * pad] * solved[i + 1]
    rim_low, rim_high = (jnp.broadcast_to(rim[:, k : k + 1], (pad, LANES)) for k in (0, 1))
    solved = jnp.concatenate(solved, axis=0)
    high, low = halves(solved)
    rest = jnp.zeros((LANES - GROUP * pad, LANES), BF16)
    high, low = (jnp.concatenate([half, rest], axis=0) for half in (high, low))
    own_rows = GROUP * size_y
    back_all = jnp.concatenate([back[:own_rows], back[own_rows:], back[:own_rows]], axis=1)
    local = []
    for g in range(nx // GROUP):
        part = slice(g * GROUP * pad, g * GROUP * pad + LANES)
        local.append(dot(back_all, jnp.concatenate([high[part], high[part], low[part]], axis=0)))
    own_modes = solved[pad : (nx - 1) * pad].reshape(size_x, pad, LANES)
    local += [jnp.sum(own_modes * rim_low[None], axis=1), jnp.sum(own_modes * rim_high[None], axis=1)]
    local = jnp.concatenate(local, axis=0)
    local = local * scale[0:1, 0:1]
    high, low = halves(local)
    half = high.shape[0] // 32 * 16
    parts = []
    for part in (slice(0, half), slice(half, None)):
        both = dot(high[part], out[...])
        parts.append(both[:, :size_z] + both[:, size_z:] + dot(low[part], out[:, :size_z]))
    local = jnp.concatenate(parts, axis=0)
    own_h, own_l = high[size_y : size_y + rows], low[size_y : size_y + rows]
    face = dot_lanes(out_ends[0:16], own_h) + dot_lanes(out_ends[0:16], own_l) + dot_lanes(out_ends[16:32], own_h)

    def inner(shape, dim):
        at = iota(shape, dim)
        return (at >= 1) & (at <= shape[dim] - 2)

    own_flat = mask[...].reshape(rows, size_z) * local[size_y : size_y + rows]
    own_box = own_flat.reshape(size_x, size_y, size_z)
    own[...] = own_box
    shape = (size_y, size_z)
    kept = inner(shape, 0) & inner(shape, 1)
    g_low = jnp.where(kept, local[:size_y] * x_low[1], 0.0)
    g_high = jnp.where(kept, local[size_y + rows : 2 * size_y + rows] * x_high[1], 0.0)
    even = where_x[0]
    low, high = own_box[0], own_box[size_x - 1]
    tx0[0] = jnp.where(even, high, low)
    tx0[1] = jnp.where(even, g_high, g_low)
    tx1[0] = jnp.where(even, low, high)
    tx1[1] = jnp.where(even, g_low, g_high)
    shape = (size_x, size_z)
    kept = inner(shape, 0) & inner(shape, 1)
    at = 2 * size_y + rows
    g_low = jnp.where(kept, local[at : at + size_x] * y_low[1], 0.0)
    g_high = jnp.where(kept, local[at + size_x : at + 2 * size_x] * y_high[1], 0.0)
    even = where_y[0]
    low, high = own_box[:, 0], own_box[:, size_y - 1]
    ty0[0] = jnp.where(even, high, low)
    ty0[1] = jnp.where(even, g_high, g_low)
    ty1[0] = jnp.where(even, low, high)
    ty1[1] = jnp.where(even, g_low, g_high)
    mine = lane_rows([own_flat], jnp.where(even_z, size_z - 1, 0))
    ids = iota((1, rows), 1)
    x_at, y_at = ids // size_y, ids % size_y
    kept = (x_at >= 1) & (x_at <= size_x - 2) & (y_at >= 1) & (y_at <= size_y - 2)
    ghost = jnp.where(kept, jnp.where(even_z, face[1:2], face[0:1]) * rz[1:2], 0.0)
    for unused in (tx1, ty0, ty1):
        unused[2:] = jnp.zeros((unused.shape[0] - 2, *unused.shape[1:]), F32)
    tz[8:] = jnp.zeros((tz.shape[0] - 8, rows), F32)
    tz[0:8] = jnp.where(iota((8, rows), 0) == 1, jnp.broadcast_to(ghost, (8, rows)), mine)


def stencil(slabs, y_low, y_high, faces, links, box):
    size_x, size_y, size_z = box
    wx, wy, wy0, wz, wz0 = links
    row, lane = iota((size_y, size_z), 0), iota((size_y, size_z), 1)
    below = wx[0] * (slabs[1] - slabs[0])
    for i in range(size_x):
        value, face = slabs[i + 1], faces(i)
        above = wx[i + 1] * (slabs[i + 2] - value)
        total = below - above
        below = above
        flow = wy[i] * (jnp.where(row == size_y - 1, y_high[i : i + 1], pltpu.roll(value, size_y - 1, 0)) - value)
        first = wy0[i : i + 1] * (value - y_low[i : i + 1])
        total = total + (jnp.where(row == 0, first, pltpu.roll(flow, 1, 0)) - flow)
        flow = wz[i] * (jnp.where(lane == size_z - 1, face, pltpu.roll(value, size_z - 1, 1)) - value)
        first = wz0[i] * (value - face)
        yield i, total + (jnp.where(lane == 0, first, pltpu.roll(flow, 1, 1)) - flow)


def links_kernel(
    rz_prev, mask, d, mu, rx0, rx1, ry0, ry1, rz,
    ad_out, wx, wy, wy0, wz, wz0, dad, rz_line,
):
    box = mask.shape
    size_x, size_y, size_z = box
    where_x, where_y, where_z = (place(axis) for axis in AXES)
    x_near = sides(rx0[2:4], rx1[2:4], where_x)
    y_near = sides(ry0[2:4], ry1[2:4], where_y)
    d_face, mu_face = (
        wide.reshape(box) for wide in lane_ends([rz[2:3], rz[3:4]], where_z[0], size_z)
    )
    row, lane = iota((size_y, size_z), 0), iota((size_y, size_z), 1)
    slabs = [x_near[0][1]] + [mu[i] for i in range(size_x)] + [x_near[1][1]]
    wx[0] = 0.5 * (slabs[0] + slabs[1])
    mu_low, mu_high = y_near[0][1], y_near[1][1]
    for i in range(size_x):
        value, face = slabs[i + 1], mu_face[i]
        wx[i + 1] = 0.5 * (value + slabs[i + 2])
        wy[i] = 0.5 * (value + jnp.where(row == size_y - 1, mu_high[i : i + 1], pltpu.roll(value, size_y - 1, 0)))
        wy0[i : i + 1] = 0.5 * (value[0:1] + mu_low[i : i + 1])
        wz[i] = 0.5 * (value + jnp.where(lane == size_z - 1, face, pltpu.roll(value, size_z - 1, 1)))
        wz0[i] = 0.5 * (value + face)
    slabs = [x_near[0][0]] + [d[i] for i in range(size_x)] + [x_near[1][0]]
    total = jnp.zeros((size_y, size_z), F32)
    for i, image in stencil(slabs, y_near[0][0], y_near[1][0], lambda i: d_face[i], (wx, wy, wy0, wz, wz0), box):
        image = mask[i] * image
        ad_out[i] = image
        total = total + slabs[i + 1] * image
    dad[...] = jnp.sum(total, axis=0, keepdims=True)
    rz_line[...] = jnp.full(rz_line.shape, rz_prev[0])


def image_kernel(
    masked, mask, d, own, tx0, tx1, ty0, ty1, tz, qx0, qx1, qy0, qy1, qz, ad, wx, wy, wy0, wz, wz0, dad,
    z_out, az_out, sums,
):
    box = mask.shape
    size_x, size_y, size_z = box
    where_x, where_y, where_z = (place(axis) for axis in AXES)
    x_sent = sides(tx0[1], tx1[1], where_x)
    y_sent = sides(ty0[1], ty1[1], where_y)
    x_got = sides(qx0[0:2], qx1[0:2], where_x)
    y_got = sides(qy0[0:2], qy1[0:2], where_y)
    face, more = (
        wide.reshape(box) for wide in lane_ends([qz[0:1] + tz[1:2], qz[1:2]], where_z[0], size_z)
    )
    row = iota((size_y, size_z), 0)
    slabs = [x_got[0][0] + x_sent[0]]
    for i in range(size_x):
        value = own[i] + more[i]
        value = value + jnp.where(row == 0, y_got[0][1][i : i + 1], 0.0)
        value = value + jnp.where(row == size_y - 1, y_got[1][1][i : i + 1], 0.0)
        if i == 0:
            value = value + x_got[0][1]
        if i == size_x - 1:
            value = value + x_got[1][1]
        z_out[i] = value
        slabs.append(value)
    slabs.append(x_got[1][0] + x_sent[1])
    y_sides = [y_got[s][0] + y_sent[s] for s in (0, 1)]
    rz = zaz = zad = jnp.zeros((size_y, size_z), F32)
    for i, image in stencil(slabs, *y_sides, lambda i: face[i], (wx, wy, wy0, wz, wz0), box):
        value = slabs[i + 1]
        image = mask[i] * image
        az_out[i] = image
        rz = rz + masked[i] * value
        zaz = zaz + value * image
        zad = zad + (value * ad[i] + d[i] * image)
    at = iota(sums.shape, 2)
    line = jnp.zeros(sums.shape, F32)
    for k, part in enumerate((rz, zaz, zad, dad[...])):
        line = jnp.where(at == k, jnp.sum(part), line)
    sums[...] = line


def update_kernel(
    rz_line, sums, iterate, res, d, z, az, ad, new_iterate, new_res, new_direction, out_iterate, out_res, out_p, gone,
):
    line = jnp.sum(sums[...], axis=0)
    rz, zaz, zad, dad = (line[:, k : k + 1] for k in range(4))
    beta = rz / rz_line[:, 0:1]
    alpha = rz / (zaz + beta * (zad + beta * dad))
    alpha, beta = (v.reshape(1, 1, 1) for v in (alpha, beta))
    p = z[...] + beta * d[...]
    out_p[...] = p
    copies = [pltpu.make_async_copy(out_p, new_direction, gone.at[0])]
    copies[0].start()
    out_iterate[...] = iterate[...] + alpha * p
    copies.append(pltpu.make_async_copy(out_iterate, new_iterate, gone.at[1]))
    copies[1].start()
    out_res[...] = res[...] - alpha * (az[...] + beta * ad[...])
    copies.append(pltpu.make_async_copy(out_res, new_res, gone.at[2]))
    copies[2].start()
    for copy in copies:
        copy.wait()


def call(kernel, args, outs, specs=None, out_spec=VMEM, scratch=()):
    outs = [jax.ShapeDtypeStruct(out, F32) for out in outs]
    return pl.pallas_call(
        kernel,
        out_shape=outs,
        in_specs=specs or [VMEM] * len(args),
        out_specs=[out_spec] * len(outs),
        scratch_shapes=list(scratch),
        cost_estimate=pl.CostEstimate(flops=0, bytes_accessed=1 << 20, transcendentals=0),
        compiler_params=pltpu.CompilerParams(vmem_limit_bytes=32 * 1024 * 1024),
    )(*args)


def exchange(sx0, sx1, sy0, sy1, sz):
    return (
        swap(sx0, "gx", 0),
        swap(sx1, "gx", 1),
        swap(sy0, "gy", 0),
        swap(sy1, "gy", 1),
        swap(sz, "gz", 0),
    )


def shards(iterate, residual, direction, permeability, unfixed_node_mask, rz_prev):
    size_x, size_y, size_z = residual.shape
    box = residual.shape
    rows = size_x * size_y
    flat = (rows, size_z)
    devices = lax.axis_size(AXES)

    def faces(count):
        return [(count, size_y, size_z)] * 2 + [(count, size_x, size_z)] * 2 + [(8, rows)]

    layer = size_y * size_z
    made_faces = [(2, size_y, size_z), (3, size_y, size_z)]
    made_faces += [(3 * size_y // size_x, size_x, size_z)] * 2 + [(3 * layer // rows, rows)]

    fwd, middle, into, *tables = map(jnp.asarray, solve_tables(size_x, size_y, size_z).values())
    with jax.named_scope("masks"):
        masked = unfixed_node_mask.astype(F32) * residual
        mu = permeability
    with jax.named_scope("pack"):
        sent = call(pack_kernel, (masked, unfixed_node_mask, direction, mu), faces(4))
    with jax.named_scope("faces_in"):
        near = exchange(*sent)
    with jax.named_scope("own_part"):
        pad = middle.shape[0]
        args = (masked, unfixed_node_mask, direction, mu, middle, into)
        outs = [(size_x * pad, size_z), box, box, ((size_x + 2) * pad, LANES), (8, size_z)]
        modes, mask, d, *part = call(own_kernel, args, outs)
    with jax.named_scope("solve"):
        own, *made = call(solve_kernel, (modes, *part, mask, *near, fwd, into, *tables), [box] + made_faces)
    with jax.named_scope("faces_out"):
        got = exchange(*made)
    with jax.named_scope("links"):
        outs = [box, (size_x + 1, size_y, size_z), box, (size_x, size_z), box, box, (1, size_z), (1, size_z)]
        ad, *links, rz_line = call(links_kernel, (rz_prev, mask, d, mu, *near), outs, [SMEM] + [VMEM] * 8)
    with jax.named_scope("image"):
        z, az, sums = call(image_kernel, (masked, mask, d, own, *made, *got, ad, *links), [box, box, (devices, 1, 128)])
    with jax.named_scope("sums"):
        sums = lax.all_to_all(sums, AXES, 0, 0, tiled=True)
    with jax.named_scope("update"):
        args = (rz_line, sums, iterate, residual, d, z, az, ad)
        scratch = [pltpu.VMEM(box, F32)] * 3 + [pltpu.SemaphoreType.DMA((3,))]
        return tuple(call(update_kernel, args, [box] * 3, None, pl.BlockSpec(memory_space=pl.ANY), scratch))


def solution(mesh):
    in_specs = (P(*AXES),) * 5 + (P(),)
    out_specs = (P(*AXES),) * 3
    return jax.shard_map(shards, mesh=mesh, in_specs=in_specs, out_specs=out_specs, check_vma=False)
```

```python
import functools

import jax
import jax.numpy as jnp
import ml_dtypes
import numpy as np
from jax import lax
from jax.experimental import pallas as pl
from jax.experimental.pallas import tpu as pltpu
from jax.sharding import PartitionSpec as P

AXES = ("gx", "gy", "gz")
F32 = jnp.float32
BF16 = jnp.bfloat16
HIGHEST = lax.Precision.HIGHEST
VMEM = pl.BlockSpec(memory_space=pltpu.VMEM)
SMEM = pl.BlockSpec(memory_space=pltpu.SMEM)
LANES = 256
GROUP = 6
FOUR = 4
FILL = {"gx": 2, "gy": 0}


def swaps(axis, turn):
    counts = [lax.axis_size(name) for name in AXES]
    dim = AXES.index(axis)
    pairs = []
    for source in np.ndindex(*counts):
        target = list(source)
        step = 1 if (source[dim] + turn) % 2 == 0 else -1
        if not 0 <= source[dim] + step < counts[dim] and axis in FILL:
            target[FILL[axis]] ^= 1
        else:
            target[dim] = (source[dim] + step) % counts[dim]
        pairs.append(tuple(int(np.ravel_multi_index(where, counts)) for where in (source, target)))
    return pairs


def swap(block, axis, turn):
    return lax.ppermute(block, AXES, swaps(axis, turn))


def place(axis):
    index = lax.axis_index(axis)
    return index % 2 == 0, index > 0, index < lax.axis_size(axis) - 1


def sides(turn0, turn1, where):
    even, below, above = where
    low = jnp.where(below, jnp.where(even, turn1, turn0), 0.0)
    high = jnp.where(above, jnp.where(even, turn0, turn1), 0.0)
    return low, high


def halves(value):
    high = value.astype(BF16)
    return high, (value - high.astype(F32)).astype(BF16)


def dot(a, b):
    return lax.dot_general(a, b, (((1,), (0,)), ((), ())), preferred_element_type=F32)


def dot_rows(a, b):
    return lax.dot_general(a, b, (((0,), (0,)), ((), ())), preferred_element_type=F32)


def dot_lanes(a, b):
    return lax.dot_general(a, b, (((1,), (1,)), ((), ())), preferred_element_type=F32)


def iota(shape, dim):
    return lax.broadcasted_iota(jnp.int32, shape, dim)


def basis(n):
    idx = np.arange(n, dtype=np.float64) + 1.0
    values = 2.0 - 2.0 * np.cos(np.pi * idx / (n + 1))
    return np.sqrt(2.0 / (n + 1)) * np.sin(np.pi * idx[:, None] * idx[None, :] / (n + 1)), values


def np_halves(table):
    high = table.astype(np.float32).astype(ml_dtypes.bfloat16)
    return high, (table - high.astype(np.float64)).astype(np.float32).astype(ml_dtypes.bfloat16)


@functools.cache
def solve_tables(size_x, size_y, size_z):
    nx, ny, nz = size_x + 2, size_y + 2, size_z + 2
    qy, ly = basis(ny)
    qz, lz = basis(nz)
    pad = -(-ny // 8) * 8
    forward = np.zeros((size_z, LANES))
    forward[:, :nz] = qz[1:-1]
    ends = np.zeros((2, LANES))
    ends[:, :nz] = qz[[0, -1]]
    fh, fl = np_halves(forward)
    last = np.zeros((4, LANES))
    last[:, :nz] = qz[[1, -2, 0, -1]]
    oh, ol = np_halves(last)
    out_ends = np.zeros((32, LANES), ml_dtypes.bfloat16)
    out_ends[0:4], out_ends[16:20] = oh, ol
    into = np.zeros((FOUR * pad, FOUR * size_y))
    for s in range(FOUR):
        into[s * pad : s * pad + ny, s * size_y : (s + 1) * size_y] = qy[1:-1].T
    ih, il = np_halves(into)
    one = np.zeros((-(-pad // 16) * 16, FOUR * size_y), ml_dtypes.bfloat16)
    for k, half in enumerate((ih, il, ih)):
        one[:pad, k * size_y : (k + 1) * size_y] = half[:pad, :size_y]
    row_ends = np.zeros((8, LANES))
    row_ends[:2] = ends
    rim = np.zeros((pad, LANES // 2))
    rim[:ny, 0], rim[:ny, 1] = qy[0], qy[-1]
    back = np.zeros((GROUP * size_y, LANES))
    for s in range(GROUP):
        back[s * size_y : (s + 1) * size_y, s * pad : s * pad + ny] = qy[1:-1]
    middle = np.full((pad, LANES), 2.0)
    middle[:ny, :nz] += ly[:, None] + lz[None, :]
    middle[ny:], middle[:, nz:] = 4.0, 4.0
    bh, bl = np_halves(back)
    return dict(
        fwd=np.concatenate([fh, fl]),
        middle=middle.astype(np.float32),
        into=np.concatenate([ih, il], axis=1),
        one=one,
        row_ends=row_ends.astype(np.float32),
        back=np.concatenate([bh, bl]),
        rim=rim.astype(np.float32),
        out=np.concatenate([np.ascontiguousarray(fh.T), np.ascontiguousarray(fl.T)], axis=1),
        out_ends=out_ends,
    )


def lane_rows(fields, lane):
    depth = fields[0].shape[1]
    total = None
    for f, field in enumerate(fields):
        at = iota((16, 2 * depth), 1)
        pick = jnp.where((iota((16, 2 * depth), 0) == f) & ((at == lane) | (at == lane + depth)), 1.0, 0.0).astype(BF16)
        rows = dot_lanes(pick, jnp.concatenate(halves(field), axis=1))
        total = rows if total is None else total + rows
    return total[:8]


def lane_ends(lines, even, depth):
    count = len(lines)
    pieces = []
    for line in lines:
        pieces += halves(line)
    size = lines[0].shape[1]
    stack = jnp.zeros((16, size), F32)
    for k, piece in enumerate(pieces):
        stack = jnp.where(iota((16, size), 0) == k, piece.astype(F32), stack)
    shape = (16, count * depth)
    lane = jnp.where(even, depth - 1, 0) + iota(shape, 0) // 2 * depth
    pick = jnp.where((iota(shape, 0) < 2 * count) & (iota(shape, 1) == lane), 1.0, 0.0).astype(BF16)
    wide = dot_rows(stack.astype(BF16), pick)
    return [wide[:, k * depth : (k + 1) * depth] for k in range(count)]


def pack_kernel(masked, msk, direction, mu, sx0, sx1, sy0, sy1, sz):
    size_x, size_y, size_z = masked.shape
    even_x, even_y, even_z = (place(axis)[0] for axis in AXES)

    def fields(where):
        mask = msk[where].astype(F32)
        return masked[where], mask, mask * direction[where], mu[where]

    for f, (low, high) in enumerate(zip(fields(0), fields(size_x - 1))):
        sx0[f] = jnp.where(even_x, high, low)
        sx1[f] = jnp.where(even_x, low, high)
    every = slice(None)
    for f, (low, high) in enumerate(zip(fields((every, 0)), fields((every, size_y - 1)))):
        sy0[f] = jnp.where(even_y, high, low)
        sy1[f] = jnp.where(even_y, low, high)
    flat = [field.reshape(size_x * size_y, size_z) for field in fields(every)]
    lane = jnp.where(even_z, size_z - 1, 0)
    pick = jnp.where((iota((16, 2 * size_z), 1) % size_z == lane) & (iota((16, 2 * size_z), 0) < 1), 1.0, 0.0).astype(BF16)
    lines = [dot_lanes(pick, jnp.concatenate(halves(field), axis=1))[0:1] for field in (flat[0], flat[2], flat[3])]
    lines.insert(1, dot_lanes(pick[:, :size_z], flat[1].astype(BF16))[0:1])
    at = iota((8, size_x * size_y), 0)
    total = jnp.zeros(at.shape, F32)
    for f, line in enumerate(lines):
        total = jnp.where(at == f, line, total)
    sz[...] = total


def along_z(rows, fwd, size_z):
    high, low = halves(rows)
    both = jnp.concatenate([high, low], axis=1)
    table = jnp.concatenate([fwd[:size_z], fwd[:size_z]], axis=0)
    half = rows.shape[0] // 32 * 16
    parts = [dot(both[part], table) + dot(high[part], fwd[size_z:]) for part in (slice(0, half), slice(half, None))]
    return jnp.concatenate(parts, axis=0)


def own_kernel(masked, msk, direction, mu, middle, into, modes, mask, d, factors, scale):
    size_x, size_y, size_z = masked.shape
    mask[...] = msk[...].astype(F32)
    d[...] = mask[...] * direction[...]
    pad, depth = middle.shape[0], FOUR * size_y
    high, low = halves(masked[...].reshape(size_x * size_y, size_z))
    table = jnp.concatenate([into[...], into[:, :depth]], axis=1)
    for g in range(0, size_x // FOUR, 2):
        pair = []
        for part in (slice(g * depth, (g + 1) * depth), slice((g + 1) * depth, (g + 2) * depth)):
            pair.append(jnp.concatenate([high[part], high[part], low[part]], axis=0))
        value = dot(table, jnp.concatenate(pair, axis=1))
        modes[g * FOUR * pad : (g + 1) * FOUR * pad] = value[:, :size_z]
        modes[(g + 1) * FOUR * pad : (g + 2) * FOUR * pad] = value[:, size_z:]
    along = middle[...]
    previous = 1.0 / along
    factors[0:pad] = previous
    for i in range(1, size_x + 2):
        previous = 1.0 / (along - previous)
        factors[i * pad : (i + 1) * pad] = previous
    scale[...] = jnp.full((8, size_z), (size_x * size_y * size_z) / jnp.sum(mu[...]))


def solve_kernel(
    modes, factors, scale, mask, sz, rx0, rx1, ry0, ry1, rz, fwd, into, one, row_ends, back, rim, out, out_ends,
    own, tx0, tx1, ty0, ty1, tz,
):
    size_x, size_y, size_z = mask.shape
    rows = size_x * size_y
    pad = rim.shape[0]
    nx = size_x + 2
    where_x, where_y, where_z = (place(axis) for axis in AXES)
    even_z = where_z[0]
    x_low, x_high = sides(rx0[0:2], rx1[0:2], where_x)
    y_low, y_high = sides(ry0[0:2], ry1[0:2], where_y)
    depth, count = FOUR * size_y, size_x // FOUR
    line_h, line_l = halves(rz[0:1])
    at = iota((16, depth), 0)
    lines = jnp.zeros((16, depth), F32)
    for g in range(count):
        part = slice(g * depth, (g + 1) * depth)
        lines = jnp.where(at == g, line_h[:, part].astype(F32), lines)
        lines = jnp.where(at == count + g, line_l[:, part].astype(F32), lines)
    lines = lines.astype(BF16)
    face_h, face_l = dot_lanes(into[:, :depth], lines), dot_lanes(into[:, depth:], lines)
    face = face_h[:, :count] + face_h[:, count : 2 * count] + face_l[:, :count]
    end = jnp.where(even_z, row_ends[1:2], row_ends[0:1])
    side_h, side_l = halves(jnp.concatenate([x_low[0], x_high[0]], axis=1))
    rest = jnp.zeros((one.shape[1] - 3 * size_y, 2 * size_z), BF16)
    ghosts = dot(one[...], jnp.concatenate([side_h, side_h, side_l, rest], axis=0))
    rim_low, rim_high = (jnp.broadcast_to(rim[:, k : k + 1], (pad, size_z)) for k in (0, 1))
    slabs = [ghosts[:pad, :size_z]]
    for i in range(size_x):
        value = modes[i * pad : (i + 1) * pad]
        slabs.append(value + rim_low * y_low[0][i : i + 1] + rim_high * y_high[0][i : i + 1])
    slabs.append(ghosts[:pad, size_z:])
    values = along_z(jnp.concatenate(slabs, axis=0), fwd, size_z)
    solved = []
    for i in range(nx):
        value = values[i * pad : (i + 1) * pad]
        if 0 < i < nx - 1:
            g, k = divmod(i - 1, FOUR)
            value = value + face[k * pad : (k + 1) * pad, g : g + 1] * end
        if i:
            value = value + solved[-1]
        solved.append(value * factors[i * pad : (i + 1) * pad])
    for i in reversed(range(nx - 1)):
        solved[i] = solved[i] + factors[i * pad : (i + 1) * pad] * solved[i + 1]
    rim_low, rim_high = (jnp.broadcast_to(rim[:, k : k + 1], (pad, LANES)) for k in (0, 1))
    solved = jnp.concatenate(solved, axis=0)
    high, low = halves(solved)
    rest = jnp.zeros((LANES - GROUP * pad, LANES), BF16)
    high, low = (jnp.concatenate([half, rest], axis=0) for half in (high, low))
    own_rows = GROUP * size_y
    back_all = jnp.concatenate([back[:own_rows], back[own_rows:], back[:own_rows]], axis=1)
    local = []
    for g in range(nx // GROUP):
        part = slice(g * GROUP * pad, g * GROUP * pad + LANES)
        local.append(dot(back_all, jnp.concatenate([high[part], high[part], low[part]], axis=0)))
    own_modes = solved[pad : (nx - 1) * pad].reshape(size_x, pad, LANES)
    local += [jnp.sum(own_modes * rim_low[None], axis=1), jnp.sum(own_modes * rim_high[None], axis=1)]
    local = jnp.concatenate(local, axis=0)
    local = local * scale[0:1, 0:1]
    high, low = halves(local)
    half = high.shape[0] // 32 * 16
    parts = []
    for part in (slice(0, half), slice(half, None)):
        both = dot(high[part], out[...])
        parts.append(both[:, :size_z] + both[:, size_z:] + dot(low[part], out[:, :size_z]))
    local = jnp.concatenate(parts, axis=0)
    own_h, own_l = high[size_y : size_y + rows], low[size_y : size_y + rows]
    face = dot_lanes(out_ends[0:16], own_h) + dot_lanes(out_ends[0:16], own_l) + dot_lanes(out_ends[16:32], own_h)

    def inner(shape, dim):
        at = iota(shape, dim)
        return (at >= 1) & (at <= shape[dim] - 2)

    own_flat = mask[...].reshape(rows, size_z) * local[size_y : size_y + rows]
    own_box = own_flat.reshape(size_x, size_y, size_z)
    own[...] = own_box
    shape = (size_y, size_z)
    kept = inner(shape, 0) & inner(shape, 1)
    g_low = jnp.where(kept, local[:size_y] * x_low[1], 0.0)
    g_high = jnp.where(kept, local[size_y + rows : 2 * size_y + rows] * x_high[1], 0.0)
    even = where_x[0]
    low, high = own_box[0], own_box[size_x - 1]
    tx0[0] = jnp.where(even, high, low)
    tx0[1] = jnp.where(even, g_high, g_low)
    tx1[0] = jnp.where(even, low, high)
    tx1[1] = jnp.where(even, g_low, g_high)
    shape = (size_x, size_z)
    kept = inner(shape, 0) & inner(shape, 1)
    at = 2 * size_y + rows
    g_low = jnp.where(kept, local[at : at + size_x] * y_low[1], 0.0)
    g_high = jnp.where(kept, local[at + size_x : at + 2 * size_x] * y_high[1], 0.0)
    even = where_y[0]
    low, high = own_box[:, 0], own_box[:, size_y - 1]
    ty0[0] = jnp.where(even, high, low)
    ty0[1] = jnp.where(even, g_high, g_low)
    ty1[0] = jnp.where(even, low, high)
    ty1[1] = jnp.where(even, g_low, g_high)
    mine = jnp.where(even_z, face[1:2], face[0:1]) * sz[1:2]
    ids = iota((1, rows), 1)
    x_at, y_at = ids // size_y, ids % size_y
    kept = (x_at >= 1) & (x_at <= size_x - 2) & (y_at >= 1) & (y_at <= size_y - 2)
    ghost = jnp.where(kept, jnp.where(even_z, face[3:4], face[2:3]) * rz[1:2], 0.0)
    for unused in (tx1, ty0, ty1):
        unused[2:] = jnp.zeros((unused.shape[0] - 2, *unused.shape[1:]), F32)
    tz[8:] = jnp.zeros((tz.shape[0] - 8, rows), F32)
    tz[0:8] = jnp.where(iota((8, rows), 0) == 1, jnp.broadcast_to(ghost, (8, rows)), mine)


def stencil(slabs, y_low, y_high, faces, links, box):
    size_x, size_y, size_z = box
    wx, wy, wy0, wz, wz0 = links
    row, lane = iota((size_y, size_z), 0), iota((size_y, size_z), 1)
    below = wx[0] * (slabs[1] - slabs[0])
    for i in range(size_x):
        value, face = slabs[i + 1], faces(i)
        above = wx[i + 1] * (slabs[i + 2] - value)
        total = below - above
        below = above
        flow = wy[i] * (jnp.where(row == size_y - 1, y_high[i : i + 1], pltpu.roll(value, size_y - 1, 0)) - value)
        first = wy0[i : i + 1] * (value - y_low[i : i + 1])
        total = total + (jnp.where(row == 0, first, pltpu.roll(flow, 1, 0)) - flow)
        flow = wz[i] * (jnp.where(lane == size_z - 1, face, pltpu.roll(value, size_z - 1, 1)) - value)
        first = wz0[i] * (value - face)
        yield i, total + (jnp.where(lane == 0, first, pltpu.roll(flow, 1, 1)) - flow)


def links_kernel(
    rz_prev, mask, d, mu, rx0, rx1, ry0, ry1, rz,
    ad_out, wx, wy, wy0, wz, wz0, dad, rz_line,
):
    box = mask.shape
    size_x, size_y, size_z = box
    where_x, where_y, where_z = (place(axis) for axis in AXES)
    x_near = sides(rx0[2:4], rx1[2:4], where_x)
    y_near = sides(ry0[2:4], ry1[2:4], where_y)
    d_face, mu_face = (
        wide.reshape(box) for wide in lane_ends([rz[2:3], rz[3:4]], where_z[0], size_z)
    )
    row, lane = iota((size_y, size_z), 0), iota((size_y, size_z), 1)
    slabs = [x_near[0][1]] + [mu[i] for i in range(size_x)] + [x_near[1][1]]
    wx[0] = 0.5 * (slabs[0] + slabs[1])
    mu_low, mu_high = y_near[0][1], y_near[1][1]
    for i in range(size_x):
        value, face = slabs[i + 1], mu_face[i]
        wx[i + 1] = 0.5 * (value + slabs[i + 2])
        wy[i] = 0.5 * (value + jnp.where(row == size_y - 1, mu_high[i : i + 1], pltpu.roll(value, size_y - 1, 0)))
        wy0[i : i + 1] = 0.5 * (value[0:1] + mu_low[i : i + 1])
        wz[i] = 0.5 * (value + jnp.where(lane == size_z - 1, face, pltpu.roll(value, size_z - 1, 1)))
        wz0[i] = 0.5 * (value + face)
    slabs = [x_near[0][0]] + [d[i] for i in range(size_x)] + [x_near[1][0]]
    total = jnp.zeros((size_y, size_z), F32)
    for i, image in stencil(slabs, y_near[0][0], y_near[1][0], lambda i: d_face[i], (wx, wy, wy0, wz, wz0), box):
        image = mask[i] * image
        ad_out[i] = image
        total = total + slabs[i + 1] * image
    dad[...] = jnp.sum(total, axis=0, keepdims=True)
    rz_line[...] = jnp.full(rz_line.shape, rz_prev[0])


def image_kernel(
    masked, mask, d, own, tx0, tx1, ty0, ty1, tz, qx0, qx1, qy0, qy1, qz, ad, wx, wy, wy0, wz, wz0, dad,
    z_out, az_out, sums,
):
    box = mask.shape
    size_x, size_y, size_z = box
    where_x, where_y, where_z = (place(axis) for axis in AXES)
    x_sent = sides(tx0[1], tx1[1], where_x)
    y_sent = sides(ty0[1], ty1[1], where_y)
    x_got = sides(qx0[0:2], qx1[0:2], where_x)
    y_got = sides(qy0[0:2], qy1[0:2], where_y)
    face, more = (
        wide.reshape(box) for wide in lane_ends([qz[0:1] + tz[1:2], qz[1:2]], where_z[0], size_z)
    )
    row = iota((size_y, size_z), 0)
    slabs = [x_got[0][0] + x_sent[0]]
    for i in range(size_x):
        value = own[i] + more[i]
        value = value + jnp.where(row == 0, y_got[0][1][i : i + 1], 0.0)
        value = value + jnp.where(row == size_y - 1, y_got[1][1][i : i + 1], 0.0)
        if i == 0:
            value = value + x_got[0][1]
        if i == size_x - 1:
            value = value + x_got[1][1]
        z_out[i] = value
        slabs.append(value)
    slabs.append(x_got[1][0] + x_sent[1])
    y_sides = [y_got[s][0] + y_sent[s] for s in (0, 1)]
    rz = zaz = zad = jnp.zeros((size_y, size_z), F32)
    for i, image in stencil(slabs, *y_sides, lambda i: face[i], (wx, wy, wy0, wz, wz0), box):
        value = slabs[i + 1]
        image = mask[i] * image
        az_out[i] = image
        rz = rz + masked[i] * value
        zaz = zaz + value * image
        zad = zad + (value * ad[i] + d[i] * image)
    at = iota(sums.shape, 2)
    line = jnp.zeros(sums.shape, F32)
    for k, part in enumerate((rz, zaz, zad, dad[...])):
        line = jnp.where(at == k, jnp.sum(part), line)
    sums[...] = line


def update_kernel(
    rz_line, sums, iterate, res, d, z, az, ad, new_iterate, new_res, new_direction, out_iterate, out_res, out_p, gone,
):
    line = jnp.sum(sums[...], axis=0)
    rz, zaz, zad, dad = (line[:, k : k + 1] for k in range(4))
    beta = rz / rz_line[:, 0:1]
    alpha = rz / (zaz + beta * (zad + beta * dad))
    alpha, beta = (v.reshape(1, 1, 1) for v in (alpha, beta))
    p = z[...] + beta * d[...]
    out_p[...] = p
    copies = [pltpu.make_async_copy(out_p, new_direction, gone.at[0])]
    copies[0].start()
    out_iterate[...] = iterate[...] + alpha * p
    copies.append(pltpu.make_async_copy(out_iterate, new_iterate, gone.at[1]))
    copies[1].start()
    out_res[...] = res[...] - alpha * (az[...] + beta * ad[...])
    copies.append(pltpu.make_async_copy(out_res, new_res, gone.at[2]))
    copies[2].start()
    for copy in copies:
        copy.wait()


def call(kernel, args, outs, specs=None, out_spec=VMEM, scratch=()):
    outs = [jax.ShapeDtypeStruct(out, F32) for out in outs]
    return pl.pallas_call(
        kernel,
        out_shape=outs,
        in_specs=specs or [VMEM] * len(args),
        out_specs=[out_spec] * len(outs),
        scratch_shapes=list(scratch),
        cost_estimate=pl.CostEstimate(flops=0, bytes_accessed=1 << 20, transcendentals=0),
        compiler_params=pltpu.CompilerParams(vmem_limit_bytes=32 * 1024 * 1024),
    )(*args)


def exchange(sx0, sx1, sy0, sy1, sz):
    return (
        swap(sx0, "gx", 0),
        swap(sx1, "gx", 1),
        swap(sy0, "gy", 0),
        swap(sy1, "gy", 1),
        swap(sz, "gz", 0),
    )


def shards(iterate, residual, direction, permeability, unfixed_node_mask, rz_prev):
    size_x, size_y, size_z = residual.shape
    box = residual.shape
    rows = size_x * size_y
    flat = (rows, size_z)
    devices = lax.axis_size(AXES)

    def faces(count):
        return [(count, size_y, size_z)] * 2 + [(count, size_x, size_z)] * 2 + [(8, rows)]

    layer = size_y * size_z
    made_faces = [(2, size_y, size_z), (3, size_y, size_z)]
    made_faces += [(3 * size_y // size_x, size_x, size_z)] * 2 + [(3 * layer // rows, rows)]

    fwd, middle, into, *tables = map(jnp.asarray, solve_tables(size_x, size_y, size_z).values())
    with jax.named_scope("masks"):
        masked = unfixed_node_mask.astype(F32) * residual
        mu = permeability
    with jax.named_scope("pack"):
        sent = call(pack_kernel, (masked, unfixed_node_mask, direction, mu), faces(4))
    with jax.named_scope("faces_in"):
        near = exchange(*sent)
    with jax.named_scope("own_part"):
        pad = middle.shape[0]
        args = (masked, unfixed_node_mask, direction, mu, middle, into)
        outs = [(size_x * pad, size_z), box, box, ((size_x + 2) * pad, LANES), (8, size_z)]
        modes, mask, d, *part = call(own_kernel, args, outs)
    with jax.named_scope("solve"):
        own, *made = call(solve_kernel, (modes, *part, mask, sent[-1], *near, fwd, into, *tables), [box] + made_faces)
    with jax.named_scope("faces_out"):
        got = exchange(*made)
    with jax.named_scope("links"):
        outs = [box, (size_x + 1, size_y, size_z), box, (size_x, size_z), box, box, (1, size_z), (1, size_z)]
        ad, *links, rz_line = call(links_kernel, (rz_prev, mask, d, mu, *near), outs, [SMEM] + [VMEM] * 8)
    with jax.named_scope("image"):
        z, az, sums = call(image_kernel, (masked, mask, d, own, *made, *got, ad, *links), [box, box, (devices, 1, 128)])
    with jax.named_scope("sums"):
        sums = lax.all_to_all(sums, AXES, 0, 0, tiled=True)
    with jax.named_scope("update"):
        args = (rz_line, sums, iterate, residual, d, z, az, ad)
        scratch = [pltpu.VMEM(box, F32)] * 3 + [pltpu.SemaphoreType.DMA((3,))]
        return tuple(call(update_kernel, args, [box] * 3, None, pl.BlockSpec(memory_space=pl.ANY), scratch))


def solution(mesh):
    in_specs = (P(*AXES),) * 5 + (P(),)
    out_specs = (P(*AXES),) * 3
    return jax.shard_map(shards, mesh=mesh, in_specs=in_specs, out_specs=out_specs, check_vma=False)
```

```python
import functools

import jax
import jax.numpy as jnp
import ml_dtypes
import numpy as np
from jax import lax
from jax.experimental import pallas as pl
from jax.experimental.pallas import tpu as pltpu
from jax.sharding import PartitionSpec as P

AXES = ("gx", "gy", "gz")
F32 = jnp.float32
BF16 = jnp.bfloat16
HIGHEST = lax.Precision.HIGHEST
VMEM = pl.BlockSpec(memory_space=pltpu.VMEM)
SMEM = pl.BlockSpec(memory_space=pltpu.SMEM)
LANES = 256
GROUP = 6
FOUR = 4
FILL = {"gx": 2, "gy": 0}


def swaps(axis, turn):
    counts = [lax.axis_size(name) for name in AXES]
    dim = AXES.index(axis)
    pairs = []
    for source in np.ndindex(*counts):
        target = list(source)
        step = 1 if (source[dim] + turn) % 2 == 0 else -1
        if not 0 <= source[dim] + step < counts[dim] and axis in FILL:
            target[FILL[axis]] ^= 1
        else:
            target[dim] = (source[dim] + step) % counts[dim]
        pairs.append(tuple(int(np.ravel_multi_index(where, counts)) for where in (source, target)))
    return pairs


def swap(block, axis, turn):
    return lax.ppermute(block, AXES, swaps(axis, turn))


def place(axis):
    index = lax.axis_index(axis)
    return index % 2 == 0, index > 0, index < lax.axis_size(axis) - 1


def sides(turn0, turn1, where):
    even, below, above = where
    low = jnp.where(below, jnp.where(even, turn1, turn0), 0.0)
    high = jnp.where(above, jnp.where(even, turn0, turn1), 0.0)
    return low, high


def halves(value):
    high = value.astype(BF16)
    return high, (value - high.astype(F32)).astype(BF16)


def dot(a, b):
    return lax.dot_general(a, b, (((1,), (0,)), ((), ())), preferred_element_type=F32)


def dot_rows(a, b):
    return lax.dot_general(a, b, (((0,), (0,)), ((), ())), preferred_element_type=F32)


def dot_lanes(a, b):
    return lax.dot_general(a, b, (((1,), (1,)), ((), ())), preferred_element_type=F32)


def iota(shape, dim):
    return lax.broadcasted_iota(jnp.int32, shape, dim)


def basis(n):
    idx = np.arange(n, dtype=np.float64) + 1.0
    values = 2.0 - 2.0 * np.cos(np.pi * idx / (n + 1))
    return np.sqrt(2.0 / (n + 1)) * np.sin(np.pi * idx[:, None] * idx[None, :] / (n + 1)), values


def np_halves(table):
    high = table.astype(np.float32).astype(ml_dtypes.bfloat16)
    return high, (table - high.astype(np.float64)).astype(np.float32).astype(ml_dtypes.bfloat16)


@functools.cache
def solve_tables(size_x, size_y, size_z):
    nx, ny, nz = size_x + 2, size_y + 2, size_z + 2
    qy, ly = basis(ny)
    qz, lz = basis(nz)
    pad = -(-ny // 8) * 8
    forward = np.zeros((size_z, LANES))
    forward[:, :nz] = qz[1:-1]
    ends = np.zeros((2, LANES))
    ends[:, :nz] = qz[[0, -1]]
    fh, fl = np_halves(forward)
    last = np.zeros((4, LANES))
    last[:, :nz] = qz[[1, -2, 0, -1]]
    oh, ol = np_halves(last)
    out_ends = np.zeros((32, LANES), ml_dtypes.bfloat16)
    out_ends[0:4], out_ends[16:20] = oh, ol
    into = np.zeros((FOUR * pad, FOUR * size_y))
    for s in range(FOUR):
        into[s * pad : s * pad + ny, s * size_y : (s + 1) * size_y] = qy[1:-1].T
    ih, il = np_halves(into)
    one = np.zeros((-(-pad // 16) * 16, FOUR * size_y), ml_dtypes.bfloat16)
    for k, half in enumerate((ih, il, ih)):
        one[:pad, k * size_y : (k + 1) * size_y] = half[:pad, :size_y]
    row_ends = np.zeros((8, LANES))
    row_ends[:2] = ends
    rim = np.zeros((pad, LANES // 2))
    rim[:ny, 0], rim[:ny, 1] = qy[0], qy[-1]
    back = np.zeros((GROUP * size_y, LANES))
    for s in range(GROUP):
        back[s * size_y : (s + 1) * size_y, s * pad : s * pad + ny] = qy[1:-1]
    middle = np.full((pad, LANES), 2.0)
    middle[:ny, :nz] += ly[:, None] + lz[None, :]
    middle[ny:], middle[:, nz:] = 4.0, 4.0
    bh, bl = np_halves(back)
    return dict(
        fwd=np.concatenate([fh, fl]),
        middle=middle.astype(np.float32),
        into=np.concatenate([ih, il], axis=1),
        one=one,
        row_ends=row_ends.astype(np.float32),
        back=np.concatenate([bh, bl]),
        rim=rim.astype(np.float32),
        out=np.concatenate([np.ascontiguousarray(fh.T), np.ascontiguousarray(fl.T)], axis=1),
        out_ends=out_ends,
    )


def lane_rows(fields, lane):
    depth = fields[0].shape[1]
    total = None
    for f, field in enumerate(fields):
        at = iota((16, 2 * depth), 1)
        pick = jnp.where((iota((16, 2 * depth), 0) == f) & ((at == lane) | (at == lane + depth)), 1.0, 0.0).astype(BF16)
        rows = dot_lanes(pick, jnp.concatenate(halves(field), axis=1))
        total = rows if total is None else total + rows
    return total[:8]


def lane_ends(lines, even, depth):
    count = len(lines)
    pieces = []
    for line in lines:
        pieces += halves(line)
    size = lines[0].shape[1]
    stack = jnp.zeros((16, size), F32)
    for k, piece in enumerate(pieces):
        stack = jnp.where(iota((16, size), 0) == k, piece.astype(F32), stack)
    shape = (16, count * depth)
    lane = jnp.where(even, depth - 1, 0) + iota(shape, 0) // 2 * depth
    pick = jnp.where((iota(shape, 0) < 2 * count) & (iota(shape, 1) == lane), 1.0, 0.0).astype(BF16)
    wide = dot_rows(stack.astype(BF16), pick)
    return [wide[:, k * depth : (k + 1) * depth] for k in range(count)]


def pack_kernel(masked, msk, direction, mu, sx0, sx1, sy0, sy1, sz):
    size_x, size_y, size_z = masked.shape
    even_x, even_y, even_z = (place(axis)[0] for axis in AXES)

    def fields(where):
        mask = msk[where].astype(F32)
        return masked[where], mask, mask * direction[where], mu[where]

    for f, (low, high) in enumerate(zip(fields(0), fields(size_x - 1))):
        sx0[f] = jnp.where(even_x, high, low)
        sx1[f] = jnp.where(even_x, low, high)
    every = slice(None)
    for f, (low, high) in enumerate(zip(fields((every, 0)), fields((every, size_y - 1)))):
        sy0[f] = jnp.where(even_y, high, low)
        sy1[f] = jnp.where(even_y, low, high)
    flat = [field.reshape(size_x * size_y, size_z) for field in fields(every)]
    lane = jnp.where(even_z, size_z - 1, 0)
    pick = jnp.where((iota((16, 2 * size_z), 1) % size_z == lane) & (iota((16, 2 * size_z), 0) < 1), 1.0, 0.0).astype(BF16)
    lines = [dot_lanes(pick, jnp.concatenate(halves(field), axis=1))[0:1] for field in (flat[0], flat[3])]
    lines.insert(1, dot_lanes(pick[:, :size_z], flat[1].astype(BF16))[0:1])
    lines.insert(2, jnp.transpose(pltpu.roll(flat[2], jnp.where(even_z, 1, 0), 1))[0:1])
    at = iota((8, size_x * size_y), 0)
    total = jnp.zeros(at.shape, F32)
    for f, line in enumerate(lines):
        total = jnp.where(at == f, line, total)
    sz[...] = total


def along_z(rows, fwd, size_z):
    high, low = halves(rows)
    both = jnp.concatenate([high, low], axis=1)
    table = jnp.concatenate([fwd[:size_z], fwd[:size_z]], axis=0)
    half = rows.shape[0] // 32 * 16
    parts = [dot(both[part], table) + dot(high[part], fwd[size_z:]) for part in (slice(0, half), slice(half, None))]
    return jnp.concatenate(parts, axis=0)


def own_kernel(masked, msk, direction, mu, middle, into, modes, mask, d, factors, scale):
    size_x, size_y, size_z = masked.shape
    mask[...] = msk[...].astype(F32)
    d[...] = mask[...] * direction[...]
    pad, depth = middle.shape[0], FOUR * size_y
    high, low = halves(masked[...].reshape(size_x * size_y, size_z))
    table = jnp.concatenate([into[...], into[:, :depth]], axis=1)
    for g in range(0, size_x // FOUR, 2):
        pair = []
        for part in (slice(g * depth, (g + 1) * depth), slice((g + 1) * depth, (g + 2) * depth)):
            pair.append(jnp.concatenate([high[part], high[part], low[part]], axis=0))
        value = dot(table, jnp.concatenate(pair, axis=1))
        modes[g * FOUR * pad : (g + 1) * FOUR * pad] = value[:, :size_z]
        modes[(g + 1) * FOUR * pad : (g + 2) * FOUR * pad] = value[:, size_z:]
    along = middle[...]
    previous = 1.0 / along
    factors[0:pad] = previous
    for i in range(1, size_x + 2):
        previous = 1.0 / (along - previous)
        factors[i * pad : (i + 1) * pad] = previous
    scale[...] = jnp.full((8, size_z), (size_x * size_y * size_z) / jnp.sum(mu[...]))


def solve_kernel(
    modes, factors, scale, mask, sz, rx0, rx1, ry0, ry1, rz, fwd, into, one, row_ends, back, rim, out, out_ends,
    own, tx0, tx1, ty0, ty1, tz,
):
    size_x, size_y, size_z = mask.shape
    rows = size_x * size_y
    pad = rim.shape[0]
    nx = size_x + 2
    where_x, where_y, where_z = (place(axis) for axis in AXES)
    even_z = where_z[0]
    x_low, x_high = sides(rx0[0:2], rx1[0:2], where_x)
    y_low, y_high = sides(ry0[0:2], ry1[0:2], where_y)
    depth, count = FOUR * size_y, size_x // FOUR
    line_h, line_l = halves(rz[0:1])
    at = iota((16, depth), 0)
    lines = jnp.zeros((16, depth), F32)
    for g in range(count):
        part = slice(g * depth, (g + 1) * depth)
        lines = jnp.where(at == g, line_h[:, part].astype(F32), lines)
        lines = jnp.where(at == count + g, line_l[:, part].astype(F32), lines)
    lines = lines.astype(BF16)
    face_h, face_l = dot_lanes(into[:, :depth], lines), dot_lanes(into[:, depth:], lines)
    face = face_h[:, :count] + face_h[:, count : 2 * count] + face_l[:, :count]
    end = jnp.where(even_z, row_ends[1:2], row_ends[0:1])
    side_h, side_l = halves(jnp.concatenate([x_low[0], x_high[0]], axis=1))
    rest = jnp.zeros((one.shape[1] - 3 * size_y, 2 * size_z), BF16)
    ghosts = dot(one[...], jnp.concatenate([side_h, side_h, side_l, rest], axis=0))
    rim_low, rim_high = (jnp.broadcast_to(rim[:, k : k + 1], (pad, size_z)) for k in (0, 1))
    slabs = [ghosts[:pad, :size_z]]
    for i in range(size_x):
        value = modes[i * pad : (i + 1) * pad]
        slabs.append(value + rim_low * y_low[0][i : i + 1] + rim_high * y_high[0][i : i + 1])
    slabs.append(ghosts[:pad, size_z:])
    values = along_z(jnp.concatenate(slabs, axis=0), fwd, size_z)
    solved = []
    for i in range(nx):
        value = values[i * pad : (i + 1) * pad]
        if 0 < i < nx - 1:
            g, k = divmod(i - 1, FOUR)
            value = value + face[k * pad : (k + 1) * pad, g : g + 1] * end
        if i:
            value = value + solved[-1]
        solved.append(value * factors[i * pad : (i + 1) * pad])
    for i in reversed(range(nx - 1)):
        solved[i] = solved[i] + factors[i * pad : (i + 1) * pad] * solved[i + 1]
    rim_low, rim_high = (jnp.broadcast_to(rim[:, k : k + 1], (pad, LANES)) for k in (0, 1))
    solved = jnp.concatenate(solved, axis=0)
    high, low = halves(solved)
    rest = jnp.zeros((LANES - GROUP * pad, LANES), BF16)
    high, low = (jnp.concatenate([half, rest], axis=0) for half in (high, low))
    own_rows = GROUP * size_y
    back_all = jnp.concatenate([back[:own_rows], back[own_rows:], back[:own_rows]], axis=1)
    local = []
    for g in range(nx // GROUP):
        part = slice(g * GROUP * pad, g * GROUP * pad + LANES)
        local.append(dot(back_all, jnp.concatenate([high[part], high[part], low[part]], axis=0)))
    own_modes = solved[pad : (nx - 1) * pad].reshape(size_x, pad, LANES)
    local += [jnp.sum(own_modes * rim_low[None], axis=1), jnp.sum(own_modes * rim_high[None], axis=1)]
    local = jnp.concatenate(local, axis=0)
    local = local * scale[0:1, 0:1]
    high, low = halves(local)
    half = high.shape[0] // 32 * 16
    parts = []
    for part in (slice(0, half), slice(half, None)):
        both = dot(high[part], out[...])
        parts.append(both[:, :size_z] + both[:, size_z:] + dot(low[part], out[:, :size_z]))
    local = jnp.concatenate(parts, axis=0)
    own_h, own_l = high[size_y : size_y + rows], low[size_y : size_y + rows]
    face = dot_lanes(out_ends[0:16], own_h) + dot_lanes(out_ends[0:16], own_l) + dot_lanes(out_ends[16:32], own_h)

    def inner(shape, dim):
        at = iota(shape, dim)
        return (at >= 1) & (at <= shape[dim] - 2)

    own_flat = mask[...].reshape(rows, size_z) * local[size_y : size_y + rows]
    own_box = own_flat.reshape(size_x, size_y, size_z)
    own[...] = own_box
    shape = (size_y, size_z)
    kept = inner(shape, 0) & inner(shape, 1)
    g_low = jnp.where(kept, local[:size_y] * x_low[1], 0.0)
    g_high = jnp.where(kept, local[size_y + rows : 2 * size_y + rows] * x_high[1], 0.0)
    even = where_x[0]
    low, high = own_box[0], own_box[size_x - 1]
    tx0[0] = jnp.where(even, high, low)
    tx0[1] = jnp.where(even, g_high, g_low)
    tx1[0] = jnp.where(even, low, high)
    tx1[1] = jnp.where(even, g_low, g_high)
    shape = (size_x, size_z)
    kept = inner(shape, 0) & inner(shape, 1)
    at = 2 * size_y + rows
    g_low = jnp.where(kept, local[at : at + size_x] * y_low[1], 0.0)
    g_high = jnp.where(kept, local[at + size_x : at + 2 * size_x] * y_high[1], 0.0)
    even = where_y[0]
    low, high = own_box[:, 0], own_box[:, size_y - 1]
    ty0[0] = jnp.where(even, high, low)
    ty0[1] = jnp.where(even, g_high, g_low)
    ty1[0] = jnp.where(even, low, high)
    ty1[1] = jnp.where(even, g_low, g_high)
    mine = jnp.where(even_z, face[1:2], face[0:1]) * sz[1:2]
    ids = iota((1, rows), 1)
    x_at, y_at = ids // size_y, ids % size_y
    kept = (x_at >= 1) & (x_at <= size_x - 2) & (y_at >= 1) & (y_at <= size_y - 2)
    ghost = jnp.where(kept, jnp.where(even_z, face[3:4], face[2:3]) * rz[1:2], 0.0)
    for unused in (tx1, ty0, ty1):
        unused[2:] = jnp.zeros((unused.shape[0] - 2, *unused.shape[1:]), F32)
    tz[8:] = jnp.zeros((tz.shape[0] - 8, rows), F32)
    tz[0:8] = jnp.where(iota((8, rows), 0) == 1, jnp.broadcast_to(ghost, (8, rows)), mine)


def stencil(slabs, y_low, y_high, faces, links, box):
    size_x, size_y, size_z = box
    wx, wy, wy0, wz, wz0 = links
    row, lane = iota((size_y, size_z), 0), iota((size_y, size_z), 1)
    below = wx[0] * (slabs[1] - slabs[0])
    for i in range(size_x):
        value, face = slabs[i + 1], faces(i)
        above = wx[i + 1] * (slabs[i + 2] - value)
        total = below - above
        below = above
        flow = wy[i] * (jnp.where(row == size_y - 1, y_high[i : i + 1], pltpu.roll(value, size_y - 1, 0)) - value)
        first = wy0[i : i + 1] * (value - y_low[i : i + 1])
        total = total + (jnp.where(row == 0, first, pltpu.roll(flow, 1, 0)) - flow)
        flow = wz[i] * (jnp.where(lane == size_z - 1, face, pltpu.roll(value, size_z - 1, 1)) - value)
        first = wz0[i] * (value - face)
        yield i, total + (jnp.where(lane == 0, first, pltpu.roll(flow, 1, 1)) - flow)


def links_kernel(
    rz_prev, mask, d, mu, rx0, rx1, ry0, ry1, rz,
    ad_out, wx, wy, wy0, wz, wz0, dad, rz_line,
):
    box = mask.shape
    size_x, size_y, size_z = box
    where_x, where_y, where_z = (place(axis) for axis in AXES)
    x_near = sides(rx0[2:4], rx1[2:4], where_x)
    y_near = sides(ry0[2:4], ry1[2:4], where_y)
    d_face, mu_face = (
        wide.reshape(box) for wide in lane_ends([rz[2:3], rz[3:4]], where_z[0], size_z)
    )
    row, lane = iota((size_y, size_z), 0), iota((size_y, size_z), 1)
    slabs = [x_near[0][1]] + [mu[i] for i in range(size_x)] + [x_near[1][1]]
    wx[0] = 0.5 * (slabs[0] + slabs[1])
    mu_low, mu_high = y_near[0][1], y_near[1][1]
    for i in range(size_x):
        value, face = slabs[i + 1], mu_face[i]
        wx[i + 1] = 0.5 * (value + slabs[i + 2])
        wy[i] = 0.5 * (value + jnp.where(row == size_y - 1, mu_high[i : i + 1], pltpu.roll(value, size_y - 1, 0)))
        wy0[i : i + 1] = 0.5 * (value[0:1] + mu_low[i : i + 1])
        wz[i] = 0.5 * (value + jnp.where(lane == size_z - 1, face, pltpu.roll(value, size_z - 1, 1)))
        wz0[i] = 0.5 * (value + face)
    slabs = [x_near[0][0]] + [d[i] for i in range(size_x)] + [x_near[1][0]]
    total = jnp.zeros((size_y, size_z), F32)
    for i, image in stencil(slabs, y_near[0][0], y_near[1][0], lambda i: d_face[i], (wx, wy, wy0, wz, wz0), box):
        image = mask[i] * image
        ad_out[i] = image
        total = total + slabs[i + 1] * image
    dad[...] = jnp.sum(total, axis=0, keepdims=True)
    rz_line[...] = jnp.full(rz_line.shape, rz_prev[0])


def image_kernel(
    masked, mask, d, own, tx0, tx1, ty0, ty1, tz, qx0, qx1, qy0, qy1, qz, ad, wx, wy, wy0, wz, wz0, dad,
    z_out, az_out, sums,
):
    box = mask.shape
    size_x, size_y, size_z = box
    where_x, where_y, where_z = (place(axis) for axis in AXES)
    x_sent = sides(tx0[1], tx1[1], where_x)
    y_sent = sides(ty0[1], ty1[1], where_y)
    x_got = sides(qx0[0:2], qx1[0:2], where_x)
    y_got = sides(qy0[0:2], qy1[0:2], where_y)
    face, more = (
        wide.reshape(box) for wide in lane_ends([qz[0:1] + tz[1:2], qz[1:2]], where_z[0], size_z)
    )
    row = iota((size_y, size_z), 0)
    slabs = [x_got[0][0] + x_sent[0]]
    for i in range(size_x):
        value = own[i] + more[i]
        value = value + jnp.where(row == 0, y_got[0][1][i : i + 1], 0.0)
        value = value + jnp.where(row == size_y - 1, y_got[1][1][i : i + 1], 0.0)
        if i == 0:
            value = value + x_got[0][1]
        if i == size_x - 1:
            value = value + x_got[1][1]
        z_out[i] = value
        slabs.append(value)
    slabs.append(x_got[1][0] + x_sent[1])
    y_sides = [y_got[s][0] + y_sent[s] for s in (0, 1)]
    rz = zaz = zad = jnp.zeros((size_y, size_z), F32)
    for i, image in stencil(slabs, *y_sides, lambda i: face[i], (wx, wy, wy0, wz, wz0), box):
        value = slabs[i + 1]
        image = mask[i] * image
        az_out[i] = image
        rz = rz + masked[i] * value
        zaz = zaz + value * image
        zad = zad + (value * ad[i] + d[i] * image)
    at = iota(sums.shape, 2)
    line = jnp.zeros(sums.shape, F32)
    for k, part in enumerate((rz, zaz, zad, dad[...])):
        line = jnp.where(at == k, jnp.sum(part), line)
    sums[...] = line


def update_kernel(
    rz_line, sums, iterate, res, d, z, az, ad, new_iterate, new_res, new_direction, out_iterate, out_res, out_p, gone,
):
    line = jnp.sum(sums[...], axis=0)
    rz, zaz, zad, dad = (line[:, k : k + 1] for k in range(4))
    beta = rz / rz_line[:, 0:1]
    alpha = rz / (zaz + beta * (zad + beta * dad))
    alpha, beta = (v.reshape(1, 1, 1) for v in (alpha, beta))
    p = z[...] + beta * d[...]
    out_p[...] = p
    copies = [pltpu.make_async_copy(out_p, new_direction, gone.at[0])]
    copies[0].start()
    out_iterate[...] = iterate[...] + alpha * p
    copies.append(pltpu.make_async_copy(out_iterate, new_iterate, gone.at[1]))
    copies[1].start()
    out_res[...] = res[...] - alpha * (az[...] + beta * ad[...])
    copies.append(pltpu.make_async_copy(out_res, new_res, gone.at[2]))
    copies[2].start()
    for copy in copies:
        copy.wait()


def call(kernel, args, outs, specs=None, out_spec=VMEM, scratch=()):
    outs = [jax.ShapeDtypeStruct(out, F32) for out in outs]
    return pl.pallas_call(
        kernel,
        out_shape=outs,
        in_specs=specs or [VMEM] * len(args),
        out_specs=[out_spec] * len(outs),
        scratch_shapes=list(scratch),
        cost_estimate=pl.CostEstimate(flops=0, bytes_accessed=1 << 20, transcendentals=0),
        compiler_params=pltpu.CompilerParams(vmem_limit_bytes=32 * 1024 * 1024),
    )(*args)


def exchange(sx0, sx1, sy0, sy1, sz):
    return (
        swap(sx0, "gx", 0),
        swap(sx1, "gx", 1),
        swap(sy0, "gy", 0),
        swap(sy1, "gy", 1),
        swap(sz, "gz", 0),
    )


def shards(iterate, residual, direction, permeability, unfixed_node_mask, rz_prev):
    size_x, size_y, size_z = residual.shape
    box = residual.shape
    rows = size_x * size_y
    flat = (rows, size_z)
    devices = lax.axis_size(AXES)

    def faces(count):
        return [(count, size_y, size_z)] * 2 + [(count, size_x, size_z)] * 2 + [(8, rows)]

    layer = size_y * size_z
    made_faces = [(2, size_y, size_z), (3, size_y, size_z)]
    made_faces += [(3 * size_y // size_x, size_x, size_z)] * 2 + [(3 * layer // rows, rows)]

    fwd, middle, into, *tables = map(jnp.asarray, solve_tables(size_x, size_y, size_z).values())
    with jax.named_scope("masks"):
        masked = unfixed_node_mask.astype(F32) * residual
        mu = permeability
    with jax.named_scope("pack"):
        sent = call(pack_kernel, (masked, unfixed_node_mask, direction, mu), faces(4))
    with jax.named_scope("faces_in"):
        near = exchange(*sent)
    with jax.named_scope("own_part"):
        pad = middle.shape[0]
        args = (masked, unfixed_node_mask, direction, mu, middle, into)
        outs = [(size_x * pad, size_z), box, box, ((size_x + 2) * pad, LANES), (8, size_z)]
        modes, mask, d, *part = call(own_kernel, args, outs)
    with jax.named_scope("solve"):
        own, *made = call(solve_kernel, (modes, *part, mask, sent[-1], *near, fwd, into, *tables), [box] + made_faces)
    with jax.named_scope("faces_out"):
        got = exchange(*made)
    with jax.named_scope("links"):
        outs = [box, (size_x + 1, size_y, size_z), box, (size_x, size_z), box, box, (1, size_z), (1, size_z)]
        ad, *links, rz_line = call(links_kernel, (rz_prev, mask, d, mu, *near), outs, [SMEM] + [VMEM] * 8)
    with jax.named_scope("image"):
        z, az, sums = call(image_kernel, (masked, mask, d, own, *made, *got, ad, *links), [box, box, (devices, 1, 128)])
    with jax.named_scope("sums"):
        sums = lax.all_to_all(sums, AXES, 0, 0, tiled=True)
    with jax.named_scope("update"):
        args = (rz_line, sums, iterate, residual, d, z, az, ad)
        scratch = [pltpu.VMEM(box, F32)] * 3 + [pltpu.SemaphoreType.DMA((3,))]
        return tuple(call(update_kernel, args, [box] * 3, None, pl.BlockSpec(memory_space=pl.ANY), scratch))


def solution(mesh):
    in_specs = (P(*AXES),) * 5 + (P(),)
    out_specs = (P(*AXES),) * 3
    return jax.shard_map(shards, mesh=mesh, in_specs=in_specs, out_specs=out_specs, check_vma=False)
```

```python
import functools

import jax
import jax.numpy as jnp
import ml_dtypes
import numpy as np
from jax import lax
from jax.experimental import pallas as pl
from jax.experimental.pallas import tpu as pltpu
from jax.sharding import PartitionSpec as P

AXES = ("gx", "gy", "gz")
F32 = jnp.float32
BF16 = jnp.bfloat16
HIGHEST = lax.Precision.HIGHEST
VMEM = pl.BlockSpec(memory_space=pltpu.VMEM)
SMEM = pl.BlockSpec(memory_space=pltpu.SMEM)
LANES = 256
GROUP = 6
FOUR = 4
FILL = {"gx": 2, "gy": 0}


def swaps(axis, turn):
    counts = [lax.axis_size(name) for name in AXES]
    dim = AXES.index(axis)
    pairs = []
    for source in np.ndindex(*counts):
        target = list(source)
        step = 1 if (source[dim] + turn) % 2 == 0 else -1
        if not 0 <= source[dim] + step < counts[dim] and axis in FILL:
            target[FILL[axis]] ^= 1
        else:
            target[dim] = (source[dim] + step) % counts[dim]
        pairs.append(tuple(int(np.ravel_multi_index(where, counts)) for where in (source, target)))
    return pairs


def swap(block, axis, turn):
    return lax.ppermute(block, AXES, swaps(axis, turn))


def place(axis):
    index = lax.axis_index(axis)
    return index % 2 == 0, index > 0, index < lax.axis_size(axis) - 1


def sides(turn0, turn1, where):
    even, below, above = where
    low = jnp.where(below, jnp.where(even, turn1, turn0), 0.0)
    high = jnp.where(above, jnp.where(even, turn0, turn1), 0.0)
    return low, high


def halves(value):
    high = value.astype(BF16)
    return high, (value - high.astype(F32)).astype(BF16)


def dot(a, b):
    return lax.dot_general(a, b, (((1,), (0,)), ((), ())), preferred_element_type=F32)


def dot_rows(a, b):
    return lax.dot_general(a, b, (((0,), (0,)), ((), ())), preferred_element_type=F32)


def dot_lanes(a, b):
    return lax.dot_general(a, b, (((1,), (1,)), ((), ())), preferred_element_type=F32)


def iota(shape, dim):
    return lax.broadcasted_iota(jnp.int32, shape, dim)


def basis(n):
    idx = np.arange(n, dtype=np.float64) + 1.0
    values = 2.0 - 2.0 * np.cos(np.pi * idx / (n + 1))
    return np.sqrt(2.0 / (n + 1)) * np.sin(np.pi * idx[:, None] * idx[None, :] / (n + 1)), values


def np_halves(table):
    high = table.astype(np.float32).astype(ml_dtypes.bfloat16)
    return high, (table - high.astype(np.float64)).astype(np.float32).astype(ml_dtypes.bfloat16)


@functools.cache
def solve_tables(size_x, size_y, size_z):
    nx, ny, nz = size_x + 2, size_y + 2, size_z + 2
    qy, ly = basis(ny)
    qz, lz = basis(nz)
    pad = -(-ny // 8) * 8
    forward = np.zeros((size_z, LANES))
    forward[:, :nz] = qz[1:-1]
    ends = np.zeros((2, LANES))
    ends[:, :nz] = qz[[0, -1]]
    fh, fl = np_halves(forward)
    last = np.zeros((4, LANES))
    last[:, :nz] = qz[[1, -2, 0, -1]]
    oh, ol = np_halves(last)
    out_ends = np.zeros((32, LANES), ml_dtypes.bfloat16)
    out_ends[0:4], out_ends[16:20] = oh, ol
    into = np.zeros((FOUR * pad, FOUR * size_y))
    for s in range(FOUR):
        into[s * pad : s * pad + ny, s * size_y : (s + 1) * size_y] = qy[1:-1].T
    ih, il = np_halves(into)
    one = np.zeros((-(-pad // 16) * 16, FOUR * size_y), ml_dtypes.bfloat16)
    for k, half in enumerate((ih, il, ih)):
        one[:pad, k * size_y : (k + 1) * size_y] = half[:pad, :size_y]
    row_ends = np.zeros((8, LANES))
    row_ends[:2] = ends
    rim = np.zeros((pad, LANES // 2))
    rim[:ny, 0], rim[:ny, 1] = qy[0], qy[-1]
    back = np.zeros((GROUP * size_y, LANES))
    for s in range(GROUP):
        back[s * size_y : (s + 1) * size_y, s * pad : s * pad + ny] = qy[1:-1]
    middle = np.full((pad, LANES), 2.0)
    middle[:ny, :nz] += ly[:, None] + lz[None, :]
    middle[ny:], middle[:, nz:] = 4.0, 4.0
    bh, bl = np_halves(back)
    return dict(
        fwd=np.concatenate([fh, fl]),
        middle=middle.astype(np.float32),
        into=np.concatenate([ih, il], axis=1),
        one=one,
        row_ends=row_ends.astype(np.float32),
        back=np.concatenate([bh, bl]),
        rim=rim.astype(np.float32),
        out=np.concatenate([np.ascontiguousarray(fh.T), np.ascontiguousarray(fl.T)], axis=1),
        out_ends=out_ends,
    )


def lane_rows(fields, lane):
    depth = fields[0].shape[1]
    total = None
    for f, field in enumerate(fields):
        at = iota((16, 2 * depth), 1)
        pick = jnp.where((iota((16, 2 * depth), 0) == f) & ((at == lane) | (at == lane + depth)), 1.0, 0.0).astype(BF16)
        rows = dot_lanes(pick, jnp.concatenate(halves(field), axis=1))
        total = rows if total is None else total + rows
    return total[:8]


def lane_ends(lines, even, depth):
    count = len(lines)
    pieces = []
    for line in lines:
        pieces += halves(line)
    size = lines[0].shape[1]
    stack = jnp.zeros((16, size), F32)
    for k, piece in enumerate(pieces):
        stack = jnp.where(iota((16, size), 0) == k, piece.astype(F32), stack)
    shape = (16, count * depth)
    lane = jnp.where(even, depth - 1, 0) + iota(shape, 0) // 2 * depth
    pick = jnp.where((iota(shape, 0) < 2 * count) & (iota(shape, 1) == lane), 1.0, 0.0).astype(BF16)
    wide = dot_rows(stack.astype(BF16), pick)
    return [wide[:, k * depth : (k + 1) * depth] for k in range(count)]


def pack_kernel(masked, msk, direction, mu, sx0, sx1, sy0, sy1, sz):
    size_x, size_y, size_z = masked.shape
    even_x, even_y, even_z = (place(axis)[0] for axis in AXES)

    def fields(where):
        mask = msk[where].astype(F32)
        return masked[where], mask, mask * direction[where], mu[where]

    for f, (low, high) in enumerate(zip(fields(0), fields(size_x - 1))):
        sx0[f] = jnp.where(even_x, high, low)
        sx1[f] = jnp.where(even_x, low, high)
    every = slice(None)
    for f, (low, high) in enumerate(zip(fields((every, 0)), fields((every, size_y - 1)))):
        sy0[f] = jnp.where(even_y, high, low)
        sy1[f] = jnp.where(even_y, low, high)
    flat = [field.reshape(size_x * size_y, size_z) for field in fields(every)]
    lane = jnp.where(even_z, size_z - 1, 0)
    pick = jnp.where((iota((16, 2 * size_z), 1) % size_z == lane) & (iota((16, 2 * size_z), 0) < 1), 1.0, 0.0).astype(BF16)
    lines = [dot_lanes(pick, jnp.concatenate(halves(field), axis=1))[0:1] for field in (flat[0], flat[2], flat[3])]
    lines.insert(1, dot_lanes(pick[:, :size_z], flat[1].astype(BF16))[0:1])
    at = iota((8, size_x * size_y), 0)
    total = jnp.zeros(at.shape, F32)
    for f, line in enumerate(lines):
        total = jnp.where(at == f, line, total)
    sz[...] = total


def along_z(rows, fwd, size_z):
    high, low = halves(rows)
    both = jnp.concatenate([high, low], axis=1)
    table = jnp.concatenate([fwd[:size_z], fwd[:size_z]], axis=0)
    half = rows.shape[0] // 32 * 16
    parts = [dot(both[part], table) + dot(high[part], fwd[size_z:]) for part in (slice(0, half), slice(half, None))]
    return jnp.concatenate(parts, axis=0)


def own_kernel(masked, msk, direction, mu, middle, into, modes, mask, d, factors, scale):
    size_x, size_y, size_z = masked.shape
    mask[...] = msk[...].astype(F32)
    d[...] = mask[...] * direction[...]
    pad, depth = middle.shape[0], FOUR * size_y
    high, low = halves(masked[...].reshape(size_x * size_y, size_z))
    table = jnp.concatenate([into[...], into[:, :depth]], axis=1)
    for g in range(0, size_x // FOUR, 2):
        pair = []
        for part in (slice(g * depth, (g + 1) * depth), slice((g + 1) * depth, (g + 2) * depth)):
            pair.append(jnp.concatenate([high[part], high[part], low[part]], axis=0))
        value = dot(table, jnp.concatenate(pair, axis=1))
        modes[g * FOUR * pad : (g + 1) * FOUR * pad] = value[:, :size_z]
        modes[(g + 1) * FOUR * pad : (g + 2) * FOUR * pad] = value[:, size_z:]
    along = middle[...]
    previous = 1.0 / along
    factors[0:pad] = previous
    for i in range(1, size_x + 2):
        previous = 1.0 / (along - previous)
        factors[i * pad : (i + 1) * pad] = previous
    scale[...] = jnp.full((8, size_z), (size_x * size_y * size_z) / jnp.sum(mu[...]))


def solve_kernel(
    modes, factors, scale, mask, sz, rx0, rx1, ry0, ry1, rz, fwd, into, one, row_ends, back, rim, out, out_ends,
    own, tx0, tx1, ty0, ty1, tz,
):
    size_x, size_y, size_z = mask.shape
    rows = size_x * size_y
    pad = rim.shape[0]
    nx = size_x + 2
    where_x, where_y, where_z = (place(axis) for axis in AXES)
    even_z = where_z[0]
    x_low, x_high = sides(rx0[0:2], rx1[0:2], where_x)
    y_low, y_high = sides(ry0[0:2], ry1[0:2], where_y)
    depth, count = FOUR * size_y, size_x // FOUR
    line_h, line_l = halves(rz[0:1])
    at = iota((16, depth), 0)
    lines = jnp.zeros((16, depth), F32)
    for g in range(count):
        part = slice(g * depth, (g + 1) * depth)
        lines = jnp.where(at == g, line_h[:, part].astype(F32), lines)
        lines = jnp.where(at == count + g, line_l[:, part].astype(F32), lines)
    lines = lines.astype(BF16)
    face_h, face_l = dot_lanes(into[:, :depth], lines), dot_lanes(into[:, depth:], lines)
    face = face_h[:, :count] + face_h[:, count : 2 * count] + face_l[:, :count]
    end = jnp.where(even_z, row_ends[1:2], row_ends[0:1])
    side_h, side_l = halves(jnp.concatenate([x_low[0], x_high[0]], axis=1))
    rest = jnp.zeros((one.shape[1] - 3 * size_y, 2 * size_z), BF16)
    ghosts = dot(one[...], jnp.concatenate([side_h, side_h, side_l, rest], axis=0))
    rim_low, rim_high = (jnp.broadcast_to(rim[:, k : k + 1], (pad, size_z)) for k in (0, 1))
    slabs = [ghosts[:pad, :size_z]]
    for i in range(size_x):
        value = modes[i * pad : (i + 1) * pad]
        slabs.append(value + rim_low * y_low[0][i : i + 1] + rim_high * y_high[0][i : i + 1])
    slabs.append(ghosts[:pad, size_z:])
    values = along_z(jnp.concatenate(slabs, axis=0), fwd, size_z)
    solved = []
    for i in range(nx):
        value = values[i * pad : (i + 1) * pad]
        if 0 < i < nx - 1:
            g, k = divmod(i - 1, FOUR)
            value = value + face[k * pad : (k + 1) * pad, g : g + 1] * end
        if i:
            value = value + solved[-1]
        solved.append(value * factors[i * pad : (i + 1) * pad])
    for i in reversed(range(nx - 1)):
        solved[i] = solved[i] + factors[i * pad : (i + 1) * pad] * solved[i + 1]
    rim_low, rim_high = (jnp.broadcast_to(rim[:, k : k + 1], (pad, LANES)) for k in (0, 1))
    solved = jnp.concatenate(solved, axis=0)
    high, low = halves(solved)
    rest = jnp.zeros((LANES - GROUP * pad, LANES), BF16)
    high, low = (jnp.concatenate([half, rest], axis=0) for half in (high, low))
    own_rows = GROUP * size_y
    back_all = jnp.concatenate([back[:own_rows], back[own_rows:], back[:own_rows]], axis=1)
    local = []
    for g in range(nx // GROUP):
        part = slice(g * GROUP * pad, g * GROUP * pad + LANES)
        local.append(dot(back_all, jnp.concatenate([high[part], high[part], low[part]], axis=0)))
    own_modes = solved[pad : (nx - 1) * pad].reshape(size_x, pad, LANES)
    local += [jnp.sum(own_modes * rim_low[None], axis=1), jnp.sum(own_modes * rim_high[None], axis=1)]
    local = jnp.concatenate(local, axis=0)
    local = local * scale[0:1, 0:1]
    high, low = halves(local)
    half = high.shape[0] // 32 * 16
    parts = []
    for part in (slice(0, half), slice(half, None)):
        both = dot(high[part], out[...])
        parts.append(both[:, :size_z] + both[:, size_z:] + dot(low[part], out[:, :size_z]))
    local = jnp.concatenate(parts, axis=0)
    own_h, own_l = high[size_y : size_y + rows], low[size_y : size_y + rows]
    face = dot_lanes(out_ends[0:16], own_h) + dot_lanes(out_ends[0:16], own_l) + dot_lanes(out_ends[16:32], own_h)

    def inner(shape, dim):
        at = iota(shape, dim)
        return (at >= 1) & (at <= shape[dim] - 2)

    own_flat = mask[...].reshape(rows, size_z) * local[size_y : size_y + rows]
    own_box = own_flat.reshape(size_x, size_y, size_z)
    own[...] = own_box
    shape = (size_y, size_z)
    kept = inner(shape, 0) & inner(shape, 1)
    g_low = jnp.where(kept, local[:size_y] * x_low[1], 0.0)
    g_high = jnp.where(kept, local[size_y + rows : 2 * size_y + rows] * x_high[1], 0.0)
    even = where_x[0]
    low, high = own_box[0], own_box[size_x - 1]
    tx0[0] = jnp.where(even, high, low)
    tx0[1] = jnp.where(even, g_high, g_low)
    tx1[0] = jnp.where(even, low, high)
    tx1[1] = jnp.where(even, g_low, g_high)
    shape = (size_x, size_z)
    kept = inner(shape, 0) & inner(shape, 1)
    at = 2 * size_y + rows
    g_low = jnp.where(kept, local[at : at + size_x] * y_low[1], 0.0)
    g_high = jnp.where(kept, local[at + size_x : at + 2 * size_x] * y_high[1], 0.0)
    even = where_y[0]
    low, high = own_box[:, 0], own_box[:, size_y - 1]
    ty0[0] = jnp.where(even, high, low)
    ty0[1] = jnp.where(even, g_high, g_low)
    ty1[0] = jnp.where(even, low, high)
    ty1[1] = jnp.where(even, g_low, g_high)
    mine = jnp.where(even_z, face[1:2], face[0:1]) * sz[1:2]
    ids = iota((1, rows), 1)
    x_at, y_at = ids // size_y, ids % size_y
    kept = (x_at >= 1) & (x_at <= size_x - 2) & (y_at >= 1) & (y_at <= size_y - 2)
    ghost = jnp.where(kept, jnp.where(even_z, face[3:4], face[2:3]) * rz[1:2], 0.0)
    for unused in (tx1, ty0, ty1):
        unused[2:] = jnp.zeros((unused.shape[0] - 2, *unused.shape[1:]), F32)
    tz[8:] = jnp.zeros((tz.shape[0] - 8, rows), F32)
    tz[0:8] = jnp.where(iota((8, rows), 0) == 1, jnp.broadcast_to(ghost, (8, rows)), mine)


def stencil(slabs, y_low, y_high, faces, links, box):
    size_x, size_y, size_z = box
    wx, wy, wy0, wz, wz0 = links
    row, lane = iota((size_y, size_z), 0), iota((size_y, size_z), 1)
    below = wx[0] * (slabs[1] - slabs[0])
    for i in range(size_x):
        value, face = slabs[i + 1], faces(i)
        above = wx[i + 1] * (slabs[i + 2] - value)
        total = below - above
        below = above
        flow = wy[i] * (jnp.where(row == size_y - 1, y_high[i : i + 1], pltpu.roll(value, size_y - 1, 0)) - value)
        first = wy0[i : i + 1] * (value - y_low[i : i + 1])
        total = total + (jnp.where(row == 0, first, pltpu.roll(flow, 1, 0)) - flow)
        flow = wz[i] * (jnp.where(lane == size_z - 1, face, pltpu.roll(value, size_z - 1, 1)) - value)
        first = wz0[i] * (value - face)
        yield i, total + (jnp.where(lane == 0, first, pltpu.roll(flow, 1, 1)) - flow)


def links_kernel(
    rz_prev, mask, d, mu, rx0, rx1, ry0, ry1, rz,
    ad_out, wx, wy, wy0, wz, wz0, dad, rz_line,
):
    box = mask.shape
    size_x, size_y, size_z = box
    where_x, where_y, where_z = (place(axis) for axis in AXES)
    x_near = sides(rx0[2:4], rx1[2:4], where_x)
    y_near = sides(ry0[2:4], ry1[2:4], where_y)
    d_face, mu_face = (
        wide.reshape(box) for wide in lane_ends([rz[2:3], rz[3:4]], where_z[0], size_z)
    )
    row, lane = iota((size_y, size_z), 0), iota((size_y, size_z), 1)
    slabs = [x_near[0][1]] + [mu[i] for i in range(size_x)] + [x_near[1][1]]
    wx[0] = 0.5 * (slabs[0] + slabs[1])
    mu_low, mu_high = y_near[0][1], y_near[1][1]
    for i in range(size_x):
        value, face = slabs[i + 1], mu_face[i]
        wx[i + 1] = 0.5 * (value + slabs[i + 2])
        wy[i] = 0.5 * (value + jnp.where(row == size_y - 1, mu_high[i : i + 1], pltpu.roll(value, size_y - 1, 0)))
        wy0[i : i + 1] = 0.5 * (value[0:1] + mu_low[i : i + 1])
        wz[i] = 0.5 * (value + jnp.where(lane == size_z - 1, face, pltpu.roll(value, size_z - 1, 1)))
        wz0[i] = 0.5 * (value + face)
    slabs = [x_near[0][0]] + [d[i] for i in range(size_x)] + [x_near[1][0]]
    total = jnp.zeros((size_y, size_z), F32)
    for i, image in stencil(slabs, y_near[0][0], y_near[1][0], lambda i: d_face[i], (wx, wy, wy0, wz, wz0), box):
        image = mask[i] * image
        ad_out[i] = image
        total = total + slabs[i + 1] * image
    dad[...] = jnp.sum(total, axis=0, keepdims=True)
    rz_line[...] = jnp.full(rz_line.shape, rz_prev[0])


def image_kernel(
    masked, mask, d, own, tx0, tx1, ty0, ty1, tz, qx0, qx1, qy0, qy1, qz, ad, wx, wy, wy0, wz, wz0, dad,
    z_out, az_out, sums,
):
    box = mask.shape
    size_x, size_y, size_z = box
    where_x, where_y, where_z = (place(axis) for axis in AXES)
    x_sent = sides(tx0[1], tx1[1], where_x)
    y_sent = sides(ty0[1], ty1[1], where_y)
    x_got = sides(qx0[0:2], qx1[0:2], where_x)
    y_got = sides(qy0[0:2], qy1[0:2], where_y)
    face, more = (
        wide.reshape(box) for wide in lane_ends([qz[0:1] + tz[1:2], qz[1:2]], where_z[0], size_z)
    )
    row = iota((size_y, size_z), 0)
    slabs = [x_got[0][0] + x_sent[0]]
    for i in range(size_x):
        value = own[i] + more[i]
        value = value + jnp.where(row == 0, y_got[0][1][i : i + 1], 0.0)
        value = value + jnp.where(row == size_y - 1, y_got[1][1][i : i + 1], 0.0)
        if i == 0:
            value = value + x_got[0][1]
        if i == size_x - 1:
            value = value + x_got[1][1]
        z_out[i] = value
        slabs.append(value)
    slabs.append(x_got[1][0] + x_sent[1])
    y_sides = [y_got[s][0] + y_sent[s] for s in (0, 1)]
    rz = zaz = zad = jnp.zeros((size_y, size_z), F32)
    for i, image in stencil(slabs, *y_sides, lambda i: face[i], (wx, wy, wy0, wz, wz0), box):
        value = slabs[i + 1]
        image = mask[i] * image
        az_out[i] = image
        rz = rz + masked[i] * value
        zaz = zaz + value * image
        zad = zad + 2.0 * (value * ad[i])
    at = iota(sums.shape, 2)
    line = jnp.zeros(sums.shape, F32)
    for k, part in enumerate((rz, zaz, zad, dad[...])):
        line = jnp.where(at == k, jnp.sum(part), line)
    sums[...] = line


def update_kernel(
    rz_line, sums, iterate, res, d, z, az, ad, new_iterate, new_res, new_direction, out_iterate, out_res, out_p, gone,
):
    line = jnp.sum(sums[...], axis=0)
    rz, zaz, zad, dad = (line[:, k : k + 1] for k in range(4))
    beta = rz / rz_line[:, 0:1]
    alpha = rz / (zaz + beta * (zad + beta * dad))
    alpha, beta = (v.reshape(1, 1, 1) for v in (alpha, beta))
    p = z[...] + beta * d[...]
    out_p[...] = p
    copies = [pltpu.make_async_copy(out_p, new_direction, gone.at[0])]
    copies[0].start()
    out_iterate[...] = iterate[...] + alpha * p
    copies.append(pltpu.make_async_copy(out_iterate, new_iterate, gone.at[1]))
    copies[1].start()
    out_res[...] = res[...] - alpha * (az[...] + beta * ad[...])
    copies.append(pltpu.make_async_copy(out_res, new_res, gone.at[2]))
    copies[2].start()
    for copy in copies:
        copy.wait()


def call(kernel, args, outs, specs=None, out_spec=VMEM, scratch=()):
    outs = [jax.ShapeDtypeStruct(out, F32) for out in outs]
    return pl.pallas_call(
        kernel,
        out_shape=outs,
        in_specs=specs or [VMEM] * len(args),
        out_specs=[out_spec] * len(outs),
        scratch_shapes=list(scratch),
        cost_estimate=pl.CostEstimate(flops=0, bytes_accessed=1 << 20, transcendentals=0),
        compiler_params=pltpu.CompilerParams(vmem_limit_bytes=32 * 1024 * 1024),
    )(*args)


def exchange(sx0, sx1, sy0, sy1, sz):
    return (
        swap(sx0, "gx", 0),
        swap(sx1, "gx", 1),
        swap(sy0, "gy", 0),
        swap(sy1, "gy", 1),
        swap(sz, "gz", 0),
    )


def shards(iterate, residual, direction, permeability, unfixed_node_mask, rz_prev):
    size_x, size_y, size_z = residual.shape
    box = residual.shape
    rows = size_x * size_y
    flat = (rows, size_z)
    devices = lax.axis_size(AXES)

    def faces(count):
        return [(count, size_y, size_z)] * 2 + [(count, size_x, size_z)] * 2 + [(8, rows)]

    layer = size_y * size_z
    made_faces = [(2, size_y, size_z), (3, size_y, size_z)]
    made_faces += [(3 * size_y // size_x, size_x, size_z)] * 2 + [(3 * layer // rows, rows)]

    fwd, middle, into, *tables = map(jnp.asarray, solve_tables(size_x, size_y, size_z).values())
    with jax.named_scope("masks"):
        masked = unfixed_node_mask.astype(F32) * residual
        mu = permeability
    with jax.named_scope("pack"):
        sent = call(pack_kernel, (masked, unfixed_node_mask, direction, mu), faces(4))
    with jax.named_scope("faces_in"):
        near = exchange(*sent)
    with jax.named_scope("own_part"):
        pad = middle.shape[0]
        args = (masked, unfixed_node_mask, direction, mu, middle, into)
        outs = [(size_x * pad, size_z), box, box, ((size_x + 2) * pad, LANES), (8, size_z)]
        modes, mask, d, *part = call(own_kernel, args, outs)
    with jax.named_scope("solve"):
        own, *made = call(solve_kernel, (modes, *part, mask, sent[-1], *near, fwd, into, *tables), [box] + made_faces)
    with jax.named_scope("faces_out"):
        got = exchange(*made)
    with jax.named_scope("links"):
        outs = [box, (size_x + 1, size_y, size_z), box, (size_x, size_z), box, box, (1, size_z), (1, size_z)]
        ad, *links, rz_line = call(links_kernel, (rz_prev, mask, d, mu, *near), outs, [SMEM] + [VMEM] * 8)
    with jax.named_scope("image"):
        z, az, sums = call(image_kernel, (masked, mask, d, own, *made, *got, ad, *links), [box, box, (devices, 1, 128)])
    with jax.named_scope("sums"):
        sums = lax.all_to_all(sums, AXES, 0, 0, tiled=True)
    with jax.named_scope("update"):
        args = (rz_line, sums, iterate, residual, d, z, az, ad)
        scratch = [pltpu.VMEM(box, F32)] * 3 + [pltpu.SemaphoreType.DMA((3,))]
        return tuple(call(update_kernel, args, [box] * 3, None, pl.BlockSpec(memory_space=pl.ANY), scratch))


def solution(mesh):
    in_specs = (P(*AXES),) * 5 + (P(),)
    out_specs = (P(*AXES),) * 3
    return jax.shard_map(shards, mesh=mesh, in_specs=in_specs, out_specs=out_specs, check_vma=False)
```
